32 devices in a mesh: groups: 2 (over y), dp: 4 (over z), cuts: 2 (over x), grad: 2 (over core).
Axes of the slice: x: 2, y: 2, z: 4, core: 2. Of those that a mesh axis runs over, the one named last changes fastest.
Arguments:
- acts: bfloat16 [1, 6144, 1024], P(None, ('groups', 'dp', 'grad'), 'cuts'), parts along dimension 1, may hold values from -20 to 20
- outgrads: bfloat16 [1, 6144, 1024], P(None, ('groups', 'dp', 'grad'), 'cuts'), parts along dimension 1, may hold values from -20 to 20
- grads: float32 [2, 1024, 1024], P('groups', ('dp', 'grad'), 'cuts'), parts along dimension 0, may hold values from -6 to 6
Outputs:
- precond: float32 [2, 1024, 1024], P('groups', ('dp', 'grad'), 'cuts'), parts along dimension 0
The draws below stay inside these ranges and needn't reach their ends.
There are 2 independent parts, one for each index of `groups`. The reference program is written for one: setup_inputs(seed, part) draws one part's arguments, and reference() takes and returns one part's arrays. A program takes and returns all parts, laid end to end along the dimension named above; each array names one. Nothing has to cross between parts.
All inputs are finite; a program needn't handle non-finite values. Where the reference program divides by a largest or mean magnitude, that divisor is 1e-20 or more.
Results may differ from the reference program's by a relative error of at most 0.0003.
Values sent between devices are 32-bit elements; how exact they have to be, the bound alone decides.
No kernel may reach another device: no remote copies, remote signals or barrier semaphores. Data moves between devices by JAX's collectives and lax.ppermute only.
A program may use at most 64 MiB of HBM per device.

```python
import math
import jax
import jax.numpy as jnp
from jax import lax

BLK = 512
L = 1
ITERS = 4
TOKENS = 3072
IN = 1024
OUT = 1024


def mould(key, noise, width, feat_lo, feat_hi):
    key_feat, key_tok = jax.random.split(key, 2)
    feat = jnp.exp(jax.random.uniform(key_feat, (L, 1, width), jnp.float32, math.log(feat_lo), math.log(feat_hi)))
    tok = jnp.exp(jax.random.uniform(key_tok, (L, TOKENS, 1), jnp.float32, math.log(0.5), math.log(2.0)))
    return jnp.clip(noise * feat * tok, -20.0, 20.0)


def draw_acts(key, part):
    key = jax.random.fold_in(key, 11)
    key_noise, key_rest = jax.random.split(key)
    noise = jnp.clip(jax.random.normal(key_noise, (L, TOKENS, IN), jnp.float32), -5.0, 5.0)
    return mould(key_rest, noise, IN, 0.5, 2.0).astype(jnp.bfloat16)


def draw_outgrads(key, part):
    key = jax.random.fold_in(key, 23)
    key_noise, key_rest = jax.random.split(key)
    noise = jnp.clip(jax.random.normal(key_noise, (L, TOKENS, OUT), jnp.float32), -5.0, 5.0)
    return mould(key_rest, noise, OUT, 0.5, 2.0).astype(jnp.bfloat16)


def levels(rng, extent, shards, least, largest):
    level, own = 1.0, jax.random.fold_in(rng, 6)
    for position, shards_of in shards:
        heights = jnp.exp(jax.random.uniform(jax.random.fold_in(own, position), (shards_of,), jnp.float32, least / len(shards), largest / len(shards)))
        level = level * jnp.repeat(heights, extent[position] // shards_of).reshape([-1 if axis == position else 1 for axis in range(len(extent))])
    return level


def centred(key, dims, scale, most, cuts=(), kind=jnp.bfloat16):
    loudness = levels(key, dims, cuts, -0.22, 0.18) if cuts else 1.0
    entries = jax.random.normal(key, dims, jnp.float32) * scale * loudness
    return jnp.minimum(jnp.maximum(entries, -most), most).astype(kind)


def setup_inputs(seed: int = 0, part: int = 0) -> dict:
    key_of = jax.random.split(jax.random.key(seed), 4)
    part_splits = jax.random.split(jax.random.fold_in(key_of[3], part), 4)
    acts = draw_acts(jax.random.fold_in(jax.random.fold_in(key_of[3], part), 71), part)
    outgrads = draw_outgrads(jax.random.fold_in(jax.random.fold_in(key_of[3], part), 71), part)
    grads = centred(part_splits[2], (L, IN, OUT), 1.0, 6.0, ((1, 8), (2, 2)), jnp.float32)
    return {"acts": acts, "outgrads": outgrads, "grads": grads}


DAMPING = 0.5
START = 1.9
HIGH = lax.Precision.HIGHEST


def block_factor(data, start):
    piece = lax.dynamic_slice_in_dim(data, start, BLK, 1)
    total = jnp.dot(piece.T, piece, preferred_element_type=jnp.float32)
    eye = jnp.eye(BLK, dtype=jnp.float32)
    return total * (1.0 / TOKENS) + DAMPING * eye


def newton_inverse(factor):
    eye = jnp.eye(BLK, dtype=jnp.float32)
    bound = jnp.max(jnp.sum(jnp.abs(factor), axis=1)) + 1e-6
    iterate = eye * (START / bound)
    for step in range(ITERS):
        product = jnp.dot(factor, iterate, precision=HIGH)
        iterate = 2.0 * iterate - jnp.dot(iterate, product, precision=HIGH)
    return iterate


def reference(acts, outgrads, grads):
    count = IN // BLK
    result = []
    for layer in range(L):
        left = jnp.stack([newton_inverse(block_factor(acts[layer], block * BLK)) for block in range(count)])
        right = jnp.stack([newton_inverse(block_factor(outgrads[layer], block * BLK)) for block in range(count)])
        tiles = grads[layer].reshape(count, BLK, count, BLK)
        middle = jnp.einsum("ipq,iqjr->ipjr", left, tiles, precision=HIGH)
        final = jnp.einsum("ipjr,jrs->ipjs", middle, right, precision=HIGH)
        result.append(final.reshape(IN, OUT))
    return jnp.stack(result)
```

```python
import functools
import jax
import jax.numpy as jnp
from jax import lax
from jax.experimental import pallas as pl
from jax.experimental.pallas import tpu as pltpu
from jax.sharding import PartitionSpec as P

ITERS = 4
DAMPING = 0.5
START = 1.9
LANE = 128
QUAD = 4
AXES = ("dp", "cuts", "grad")
PARAMS = pltpu.CompilerParams(vmem_limit_bytes=48 * 1024 * 1024)


def slots(order):
    count = order // LANE
    above = [(i, j) for i in range(count) for j in range(i + 1, count)]
    return above, count // 2


def packed_rows(order):
    above, pairs = slots(order)
    return (len(above) + pairs) * LANE + -(-pairs // 8) * 8


def places():
    rows = lax.broadcasted_iota(jnp.int32, (LANE, LANE), 0)
    cols = lax.broadcasted_iota(jnp.int32, (LANE, LANE), 1)
    return rows, cols


def pack(block, order, out_ref):
    above, pairs = slots(order)
    rows, cols = places()
    for slot, (i, j) in enumerate(above):
        out_ref[slot * LANE : (slot + 1) * LANE, :] = block(i, j)
    diagonals = []
    for pair in range(pairs):
        slot = len(above) + pair
        first, second = block(2 * pair, 2 * pair), block(2 * pair + 1, 2 * pair + 1)
        out_ref[slot * LANE : (slot + 1) * LANE, :] = jnp.where(rows <= cols, first, second)
        diagonals.append(jnp.sum(jnp.where(rows == cols, second, 0.0), axis=0, keepdims=True))
    top = (len(above) + pairs) * LANE
    spare = out_ref.shape[0] - top - pairs
    out_ref[top:, :] = jnp.concatenate(diagonals + [jnp.zeros((spare, LANE), jnp.float32)], 0)


def unpack(piece, order, out_ref, scale=1.0, shift=0.0):
    above, pairs = slots(order)
    rows, cols = places()

    def put(i, j, value):
        out_ref[i * LANE : (i + 1) * LANE, j * LANE : (j + 1) * LANE] = value

    for slot, (i, j) in enumerate(above):
        value = piece(slot * LANE, (slot + 1) * LANE) * scale
        put(i, j, value)
        put(j, i, value.T)
    top = (len(above) + pairs) * LANE
    diagonals = piece(top, top + -(-pairs // 8) * 8)
    damping = jnp.where(rows == cols, shift, 0.0)
    for pair in range(pairs):
        slot = len(above) + pair
        both = piece(slot * LANE, (slot + 1) * LANE)
        turned = both.T
        put(2 * pair, 2 * pair, jnp.where(rows <= cols, both, turned) * scale + damping)
        second = jnp.where(rows > cols, both, jnp.where(rows < cols, turned, diagonals[pair : pair + 1, :]))
        put(2 * pair + 1, 2 * pair + 1, second * scale + damping)


def halves(value):
    high = value.astype(jnp.bfloat16)
    return high, (value - high.astype(jnp.float32)).astype(jnp.bfloat16)


def times(left, right):
    dot = functools.partial(jnp.dot, preferred_element_type=jnp.float32)
    return dot(left[0], right[0]) + (dot(left[0], right[1]) + dot(left[1], right[0]))


def square(x_ref):
    x = x_ref[...]
    return lax.dot_general(x, x, (((0,), (0,)), ((), ())), preferred_element_type=jnp.float32)


def block_of(value):
    return lambda i, j: value[i * LANE : (i + 1) * LANE, j * LANE : (j + 1) * LANE]


def cov_send_kernel(acts_ref, outgrads_ref, out_ref):
    core = lax.axis_index("grad")

    @pl.when(core == 0)
    def _():
        pack(block_of(square(outgrads_ref)), outgrads_ref.shape[1], out_ref)

    @pl.when(core != 0)
    def _():
        pack(block_of(square(acts_ref)), acts_ref.shape[1], out_ref)


def cov_keep_kernel(acts_ref, outgrads_ref, other_ref, out_ref):
    core = lax.axis_index("grad")

    @pl.when(core == 0)
    def _():
        pack(block_of(square(acts_ref)), acts_ref.shape[1], out_ref)

    @pl.when(core != 0)
    def _():
        pack(block_of(square(outgrads_ref)), outgrads_ref.shape[1], out_ref)

    out_ref[...] += other_ref[...]


def inverse_kernel(scale, order, *refs):
    *sums, out_ref, factor_ref = refs

    def piece(start, stop):
        total = sums[0][start:stop, :]
        for ref in sums[1:]:
            total = total + ref[start:stop, :]
        return total

    unpack(piece, order, factor_ref, scale, DAMPING)
    factor = factor_ref[...]
    bound = jnp.max(jnp.sum(jnp.abs(factor), axis=0, keepdims=True), axis=1, keepdims=True) + 1e-06
    start = START / bound
    rows = lax.broadcasted_iota(jnp.int32, (order, order), 0)
    cols = lax.broadcasted_iota(jnp.int32, (order, order), 1)
    eye = jnp.where(rows == cols, 1.0, 0.0)
    power = eye - start * factor
    total = power
    power_halves = halves(power)
    power = times(power_halves, power_halves)
    for step in range(1, ITERS):
        power_halves = halves(power)
        total = total + power + times(halves(total), power_halves)
        if step < ITERS - 1:
            power = times(power_halves, power_halves)
    pack(block_of(start * (eye + total)), order, out_ref)


def final_kernel(order, spread, *refs):
    own_ref, other_ref, *rest = refs
    pieces = rest[:spread]
    out_ref, left_ref, right_ref, tile_ref = rest[spread:]
    core = lax.axis_index("grad")
    position = lax.axis_index("dp") * lax.axis_size("grad") + core
    mine = lax.rem(position, spread)
    rows_dev = out_ref.shape[0]

    @pl.when(core == 0)
    def _():
        unpack(lambda a, b: own_ref[a:b, :], order, left_ref)
        unpack(lambda a, b: other_ref[a:b, :], order, right_ref)

    @pl.when(core != 0)
    def _():
        unpack(lambda a, b: other_ref[a:b, :], order, left_ref)
        unpack(lambda a, b: own_ref[a:b, :], order, right_ref)

    for turn, ref in enumerate(pieces):
        tile_ref[pl.ds(pl.multiple_of((mine ^ turn) * rows_dev, rows_dev), rows_dev), :] = ref[...]
    left = left_ref[pl.ds(pl.multiple_of(mine * rows_dev, rows_dev), rows_dev), :]
    middle = times(halves(left), halves(tile_ref[...]))
    out_ref[...] = times(halves(middle), halves(right_ref[...]))


def call(kernel, shape, scratch, *args):
    return pl.pallas_call(
        kernel,
        out_shape=jax.ShapeDtypeStruct(shape, jnp.float32),
        scratch_shapes=scratch,
        compiler_params=PARAMS,
    )(*args)


class Plan:
    def __init__(self, dp, cuts):
        self.dp, self.cuts = dp, cuts
        self.rounds = max(QUAD - 1, 2 * cuts - 1)

    def index(self, z, x, core):
        return (z * self.cuts + x) * 2 + core

    def root(self, z, x, core):
        return z // QUAD * QUAD + 1 + (x + core) % 2

    def across(self, bit):
        return [
            (self.index(z, x, core), self.index(z ^ bit, x, core))
            for z in range(self.dp)
            for x in range(self.cuts)
            for core in range(2)
        ]

    def gather(self, turn):
        pairs = []
        for x in range(self.cuts):
            for core in range(2):
                for base in range(0, self.dp, QUAD):
                    root = self.root(base, x, core)
                    others = sorted((z for z in range(base, base + QUAD) if z != root), key=lambda z: -abs(z - root))
                    pairs.append((self.index(others[turn], x, core), self.index(root, x, core)))
        return pairs

    def spread(self, turn):
        pairs = []
        for x in range(self.cuts):
            for base in range(0, self.dp, QUAD):
                root = self.root(base, x, 1)
                others = sorted((z for z in range(base, base + QUAD) if z != root), key=lambda z: -abs(z - root))
                if turn < len(others):
                    pairs.append((self.index(root, x, 1), self.index(others[turn], x, 1)))
                if x // 2 != base // QUAD:
                    continue
                root = self.root(base, x, 0)
                targets = [(z, x + d) for d in range(self.cuts) for z in (root ^ 1, root)]
                targets = [(z, other % self.cuts) for z, other in targets if (z, other) != (root, x)]
                if turn < len(targets):
                    z, other = targets[turn]
                    pairs.append((self.index(root, x, 0), self.index(z, other, 0)))
        return pairs


def swap_cores(array):
    return lax.ppermute(array, "grad", [(0, 1), (1, 0)])


def per_device(acts, outgrads, grads):
    dp, cuts, cores = (lax.axis_size(name) for name in AXES)
    tok_rows, order = acts.shape[1:]
    dev_count = dp * cores
    spread = dev_count // cuts
    plan = Plan(dp, cuts)
    shape = (packed_rows(order), LANE)
    acts, outgrads, grads = acts[0], outgrads[0], grads[0]

    pieces = [grads, swap_cores(grads)]
    while len(pieces) < spread:
        moved = [lax.ppermute(piece, AXES, plan.across(len(pieces) // 2)) for piece in pieces]
        pieces += moved

    sent = call(cov_send_kernel, shape, [], acts, outgrads)
    chip = call(cov_keep_kernel, shape, [], acts, outgrads, swap_cores(sent))
    bit = QUAD
    while bit < dp:
        chip = chip + lax.ppermute(chip, AXES, plan.across(bit))
        bit *= 2
    sums = [chip] + [lax.ppermute(chip, AXES, plan.gather(turn)) for turn in range(QUAD - 1)]
    scale = 1.0 / (tok_rows * dev_count)
    inverse = call(
        functools.partial(inverse_kernel, scale, order), shape, [pltpu.VMEM((order, order), jnp.float32)], *sums
    )
    z, x, core = (lax.axis_index(name) for name in AXES)
    is_root = z % QUAD == 1 + (x + core) % 2
    needed = jnp.logical_or(core == 1, x // 2 == z // QUAD)
    mine = jnp.where(jnp.logical_and(is_root, needed), inverse, 0.0)
    for turn in range(plan.rounds):
        mine = mine + lax.ppermute(inverse, AXES, plan.spread(turn))
    other = swap_cores(mine)
    square_scratch = pltpu.VMEM((order, order), jnp.float32)
    out = call(
        functools.partial(final_kernel, order, spread), grads.shape, [square_scratch] * 3, mine, other, *pieces
    )
    return out[None]


def solution(mesh):
    in_specs = (
        P(None, ("groups", "dp", "grad"), "cuts"),
        P(None, ("groups", "dp", "grad"), "cuts"),
        P("groups", ("dp", "grad"), "cuts"),
    )
    out_specs = P("groups", ("dp", "grad"), "cuts")
    return jax.shard_map(
        per_device, mesh=mesh, in_specs=in_specs, out_specs=out_specs, check_vma=False
    )
```

```python
import functools
import jax
import jax.numpy as jnp
from jax import lax
from jax.experimental import pallas as pl
from jax.experimental.pallas import tpu as pltpu
from jax.sharding import PartitionSpec as P

ITERS = 4
DAMPING = 0.5
START = 1.9
LANE = 128
QUAD = 4
AXES = ("dp", "cuts", "grad")
PARAMS = pltpu.CompilerParams(vmem_limit_bytes=48 * 1024 * 1024)


def slots(order):
    count = order // LANE
    above = [(i, j) for i in range(count) for j in range(i + 1, count)]
    return above, count // 2


def packed_rows(order):
    above, pairs = slots(order)
    return (len(above) + pairs) * LANE + -(-pairs // 8) * 8


def places():
    rows = lax.broadcasted_iota(jnp.int32, (LANE, LANE), 0)
    cols = lax.broadcasted_iota(jnp.int32, (LANE, LANE), 1)
    return rows, cols


def pack(block, order, out_ref):
    above, pairs = slots(order)
    rows, cols = places()
    for slot, (i, j) in enumerate(above):
        out_ref[slot * LANE : (slot + 1) * LANE, :] = block(i, j)
    diagonals = []
    for pair in range(pairs):
        slot = len(above) + pair
        first, second = block(2 * pair, 2 * pair), block(2 * pair + 1, 2 * pair + 1)
        out_ref[slot * LANE : (slot + 1) * LANE, :] = jnp.where(rows <= cols, first, second)
        diagonals.append(jnp.sum(jnp.where(rows == cols, second, 0.0), axis=0, keepdims=True))
    top = (len(above) + pairs) * LANE
    spare = out_ref.shape[0] - top - pairs
    out_ref[top:, :] = jnp.concatenate(diagonals + [jnp.zeros((spare, LANE), jnp.float32)], 0)


def unpack(piece, order, out_ref, scale=1.0, shift=0.0):
    above, pairs = slots(order)
    rows, cols = places()

    def put(i, j, value):
        out_ref[i * LANE : (i + 1) * LANE, j * LANE : (j + 1) * LANE] = value

    for slot, (i, j) in enumerate(above):
        value = piece(slot * LANE, (slot + 1) * LANE) * scale
        put(i, j, value)
        put(j, i, value.T)
    top = (len(above) + pairs) * LANE
    diagonals = piece(top, top + -(-pairs // 8) * 8)
    damping = jnp.where(rows == cols, shift, 0.0)
    for pair in range(pairs):
        slot = len(above) + pair
        both = piece(slot * LANE, (slot + 1) * LANE)
        turned = both.T
        put(2 * pair, 2 * pair, jnp.where(rows <= cols, both, turned) * scale + damping)
        second = jnp.where(rows > cols, both, jnp.where(rows < cols, turned, diagonals[pair : pair + 1, :]))
        put(2 * pair + 1, 2 * pair + 1, second * scale + damping)


def halves(value):
    high = value.astype(jnp.bfloat16)
    return high, (value - high.astype(jnp.float32)).astype(jnp.bfloat16)


def times(left, right):
    dot = functools.partial(jnp.dot, preferred_element_type=jnp.float32)
    return dot(left[0], right[0]) + (dot(left[0], right[1]) + dot(left[1], right[0]))


def cov_kernel(keep, acts_ref, outgrads_ref, out_ref):
    core = lax.axis_index("grad")

    def write(x_ref):
        x = x_ref[...]
        total = lax.dot_general(x, x, (((0,), (0,)), ((), ())), preferred_element_type=jnp.float32)
        pack(block_of(total), x.shape[1], out_ref)

    @pl.when((core == 0) == keep)
    def _():
        write(acts_ref)

    @pl.when((core == 0) != keep)
    def _():
        write(outgrads_ref)


def block_of(value):
    return lambda i, j: value[i * LANE : (i + 1) * LANE, j * LANE : (j + 1) * LANE]


def inverse_kernel(scale, order, *refs):
    *sums, out_ref, factor_ref = refs

    def piece(start, stop):
        total = sums[0][start:stop, :]
        for ref in sums[1:]:
            total = total + ref[start:stop, :]
        return total

    unpack(piece, order, factor_ref, scale, DAMPING)
    factor = factor_ref[...]
    bound = jnp.max(jnp.sum(jnp.abs(factor), axis=0, keepdims=True), axis=1, keepdims=True) + 1e-06
    start = START / bound
    rows = lax.broadcasted_iota(jnp.int32, (order, order), 0)
    cols = lax.broadcasted_iota(jnp.int32, (order, order), 1)
    eye = jnp.where(rows == cols, 1.0, 0.0)
    power = eye - start * factor
    total = power
    power_halves = halves(power)
    power = times(power_halves, power_halves)
    for step in range(1, ITERS):
        power_halves = halves(power)
        total = total + power + times(halves(total), power_halves)
        if step < ITERS - 1:
            power = times(power_halves, power_halves)
    pack(block_of(start * (eye + total)), order, out_ref)


def final_kernel(order, spread, *refs):
    own_ref, other_ref, *rest = refs
    pieces = rest[:spread]
    out_ref, left_ref, right_ref, tile_ref = rest[spread:]
    core = lax.axis_index("grad")
    position = lax.axis_index("dp") * lax.axis_size("grad") + core
    mine = lax.rem(position, spread)
    rows_dev = out_ref.shape[0]

    @pl.when(core == 0)
    def _():
        unpack(lambda a, b: own_ref[a:b, :], order, left_ref)
        unpack(lambda a, b: other_ref[a:b, :], order, right_ref)

    @pl.when(core != 0)
    def _():
        unpack(lambda a, b: other_ref[a:b, :], order, left_ref)
        unpack(lambda a, b: own_ref[a:b, :], order, right_ref)

    for turn, ref in enumerate(pieces):
        tile_ref[pl.ds(pl.multiple_of((mine ^ turn) * rows_dev, rows_dev), rows_dev), :] = ref[...]
    left = left_ref[pl.ds(pl.multiple_of(mine * rows_dev, rows_dev), rows_dev), :]
    middle = times(halves(left), halves(tile_ref[...]))
    out_ref[...] = times(halves(middle), halves(right_ref[...]))


def call(kernel, shape, scratch, *args):
    return pl.pallas_call(
        kernel,
        out_shape=jax.ShapeDtypeStruct(shape, jnp.float32),
        scratch_shapes=scratch,
        compiler_params=PARAMS,
    )(*args)


class Plan:
    def __init__(self, dp, cuts):
        self.dp, self.cuts = dp, cuts
        self.bases = range(0, dp, QUAD)

    def index(self, z, x, core):
        return (z * self.cuts + x % self.cuts) * 2 + core

    def root(self, base, x, core):
        return base + 1 + (x + core) % 2

    def needed(self, base, x):
        return x // 2 == base // QUAD

    def across(self, bit):
        return [
            (self.index(z, x, core), self.index(z ^ bit, x, core))
            for z in range(self.dp)
            for x in range(self.cuts)
            for core in range(2)
        ]

    def neighbours(self, outward):
        middle = (1, 2) if outward else (0, 3)
        return [pair for pair in self.across(1) if pair[0] // (2 * self.cuts) % QUAD in middle]

    def collect(self, turn):
        pairs = []
        for x in range(self.cuts):
            for core in range(2):
                for base in self.bases:
                    root = self.root(base, x, core)
                    middle = 2 * base + QUAD - 1 - root
                    source = (middle ^ 1, middle, root ^ 1)[turn]
                    pairs.append((self.index(source, x, core), self.index(root, x, core)))
        return pairs

    def first(self, turn):
        pairs = []
        for x in range(self.cuts):
            for base in self.bases:
                if self.needed(base, x):
                    root = self.root(base, x, 0)
                    pairs.append((self.index(root, x, 0), self.index(root, x + turn, 0)))
                if turn == 1:
                    root = self.root(base, x, 1)
                    pairs.append((self.index(root, x, 1), self.index(2 * base + QUAD - 1 - root, x, 1)))
        return pairs

    def outward(self, turn):
        pairs = []
        for x in range(self.cuts):
            for base in self.bases:
                if self.needed(base, x):
                    root = self.root(base, x, 0)
                    pairs.append((self.index(root, x + turn, 0), self.index(root ^ 1, x + turn, 0)))
                if turn < 2:
                    root = self.root(base, x, 1)
                    chip = root if turn == 0 else 2 * base + QUAD - 1 - root
                    pairs.append((self.index(chip, x, 1), self.index(chip ^ 1, x, 1)))
        return pairs


def swap_cores(array):
    return lax.ppermute(array, "grad", [(0, 1), (1, 0)])


def per_device(acts, outgrads, grads):
    dp, cuts, cores = (lax.axis_size(name) for name in AXES)
    tok_rows, order = acts.shape[1:]
    dev_count = dp * cores
    spread = dev_count // cuts
    plan = Plan(dp, cuts)
    shape = (packed_rows(order), LANE)
    acts, outgrads, grads = acts[0], outgrads[0], grads[0]

    sent, kept = (
        call(functools.partial(cov_kernel, keep), shape, [], acts, outgrads) for keep in (False, True)
    )
    chip = kept + swap_cores(sent)
    bit = QUAD
    while bit < dp:
        chip = chip + lax.ppermute(chip, AXES, plan.across(bit))
        bit *= 2
    grads, chip = lax.optimization_barrier((grads, chip))
    sums = [chip] + [lax.ppermute(chip, AXES, plan.collect(turn)) for turn in range(QUAD - 1)]
    outward = lax.ppermute(grads, AXES, plan.neighbours(True))
    pieces = [grads, swap_cores(grads)]
    sums, outward, pieces = lax.optimization_barrier((sums, outward, pieces))
    scale = 1.0 / (tok_rows * dev_count)
    inverse = call(
        functools.partial(inverse_kernel, scale, order), shape, [pltpu.VMEM((order, order), jnp.float32)], *sums
    )
    inverse, grads = lax.optimization_barrier((inverse, grads))
    z, x, core = (lax.axis_index(name) for name in AXES)
    is_root = z % QUAD == 1 + (x + core) % 2
    needed = jnp.logical_or(core == 1, x // 2 == z // QUAD)
    arrived = [lax.ppermute(inverse, AXES, plan.first(turn)) for turn in range(1, cuts)]
    outer = [lax.ppermute(inverse, AXES, plan.outward(0))]
    inward = lax.ppermute(grads, AXES, plan.neighbours(False))
    outer += [lax.ppermute(array, AXES, plan.outward(turn + 1)) for turn, array in enumerate(arrived)]
    neighbour = outward + inward
    pieces += [neighbour, swap_cores(neighbour)]
    while len(pieces) < spread:
        pieces += [lax.ppermute(piece, AXES, plan.across(len(pieces) // 2)) for piece in pieces]
    pieces = pieces[:spread]
    arrived, outer, pieces = lax.optimization_barrier((arrived, outer, pieces))
    mine = jnp.where(jnp.logical_and(is_root, needed), inverse, 0.0)
    for array in arrived + outer:
        mine = mine + array
    other = swap_cores(mine)
    square_scratch = pltpu.VMEM((order, order), jnp.float32)
    out = call(
        functools.partial(final_kernel, order, spread), grads.shape, [square_scratch] * 3, mine, other, *pieces
    )
    return out[None]


def solution(mesh):
    in_specs = (
        P(None, ("groups", "dp", "grad"), "cuts"),
        P(None, ("groups", "dp", "grad"), "cuts"),
        P("groups", ("dp", "grad"), "cuts"),
    )
    out_specs = P("groups", ("dp", "grad"), "cuts")
    return jax.shard_map(
        per_device, mesh=mesh, in_specs=in_specs, out_specs=out_specs, check_vma=False
    )
```

```python
import functools
import jax
import jax.numpy as jnp
from jax import lax
from jax.experimental import pallas as pl
from jax.experimental.pallas import tpu as pltpu
from jax.sharding import PartitionSpec as P

ITERS = 4
DAMPING = 0.5
START = 1.9
LANE = 128
QUAD = 4
AXES = ("groups", "dp", "cuts", "grad")
PARAMS = pltpu.CompilerParams(vmem_limit_bytes=48 * 1024 * 1024)


def half_blocks(order, half):
    count = order // LANE // 2
    own = range(half * count, (half + 1) * count)
    return [(i, j) for i in own for j in own if i < j], [(i, i + 1) for i in own[::2]]


def joining_blocks(order):
    count = order // LANE
    return [(i, j) for i in range(count // 2) for j in range(count // 2, count)]


def part_rows(order):
    above, pairs = half_blocks(order, 0)
    own = (len(above) + len(pairs)) * LANE + -(-len(pairs) // 8) * 8
    return len(joining_blocks(order)) * LANE + own, own


def places():
    rows = lax.broadcasted_iota(jnp.int32, (LANE, LANE), 0)
    cols = lax.broadcasted_iota(jnp.int32, (LANE, LANE), 1)
    return rows, cols


def pack(block, order, a_ref, b_ref, second=None):
    rows, cols = places()

    def own(half):
        above, pairs = half_blocks(order, half)
        values = [block(i, j) for i, j in above]
        values += [jnp.where(rows <= cols, block(i, i), block(j, j)) for i, j in pairs]
        last = [jnp.sum(jnp.where(rows == cols, block(j, j), 0.0), axis=0, keepdims=True) for _, j in pairs]
        return values + [jnp.concatenate(last + [jnp.zeros((-len(pairs) % 8, LANE), jnp.float32)], 0)]

    def put(ref, values):
        top = 0
        for value in values:
            ref[top : top + value.shape[0], :] = value
            top += value.shape[0]

    joining = [block(i, j) for i, j in joining_blocks(order)]
    here, there = own(0), own(1)
    if second is not None:
        here, there = (
            [jnp.where(second, q, p) for p, q in zip(here, there)],
            [jnp.where(second, p, q) for p, q in zip(here, there)],
        )
    put(a_ref, joining + here)
    put(b_ref, there)


def unpack(a_piece, b_piece, order, out_ref, second=None, scale=1.0, shift=0.0):
    rows, cols = places()
    damping = jnp.where(rows == cols, shift, 0.0)

    def put(i, j, value):
        out_ref[i * LANE : (i + 1) * LANE, j * LANE : (j + 1) * LANE] = value

    joining = joining_blocks(order)
    for slot, (i, j) in enumerate(joining):
        value = a_piece(slot * LANE, (slot + 1) * LANE) * scale
        put(i, j, value)
        put(j, i, value.T)

    def own(piece, top):
        above, pairs = half_blocks(order, 0)
        count = len(above) + len(pairs)
        values = [piece(top + k * LANE, top + (k + 1) * LANE) for k in range(count)]
        top += count * LANE
        return values + [piece(top, top + -(-len(pairs) // 8) * 8)]

    here, there = own(a_piece, len(joining) * LANE), own(b_piece, 0)
    if second is not None:
        here, there = (
            [jnp.where(second, q, p) for p, q in zip(here, there)],
            [jnp.where(second, p, q) for p, q in zip(here, there)],
        )
    for half, values in ((0, here), (1, there)):
        above, pairs = half_blocks(order, half)
        for k, (i, j) in enumerate(above):
            value = values[k] * scale
            put(i, j, value)
            put(j, i, value.T)
        for k, (i, j) in enumerate(pairs):
            both = values[len(above) + k]
            turned = both.T
            put(i, i, jnp.where(rows <= cols, both, turned) * scale + damping)
            last = jnp.where(rows > cols, both, jnp.where(rows < cols, turned, values[-1][k : k + 1, :]))
            put(j, j, last * scale + damping)


def halves(value):
    high = value.astype(jnp.bfloat16)
    return high, (value - high.astype(jnp.float32)).astype(jnp.bfloat16)


def times(left, right):
    dot = functools.partial(jnp.dot, preferred_element_type=jnp.float32)
    return dot(left[0], right[0]) + (dot(left[0], right[1]) + dot(left[1], right[0]))


def rows_of(pair, start, stop):
    return pair[0][start:stop, :], pair[1][start:stop, :]


def upper_times(left, right):
    middle = left[0].shape[0] // 2
    top = times(rows_of(left, 0, middle), right)
    corner = times(rows_of(left, middle, 2 * middle), (right[0][:, middle:], right[1][:, middle:]))
    return top, corner


def whole(top, corner):
    middle = corner.shape[0]
    return jnp.concatenate([top, jnp.concatenate([top[:, middle:].T, corner], 1)], 0)


def cov_kernel(keep, acts_ref, outgrads_ref, out_ref):
    core = lax.axis_index("grad")

    def write(x_ref):
        x = x_ref[...]
        order = x.shape[1]
        split = part_rows(order)[0]
        total = lax.dot_general(x, x, (((0,), (0,)), ((), ())), preferred_element_type=jnp.float32)
        pack(block_of(total), order, out_ref.at[:split], out_ref.at[split:])

    @pl.when((core == 0) == keep)
    def _():
        write(acts_ref)

    @pl.when((core == 0) != keep)
    def _():
        write(outgrads_ref)


def block_of(value):
    return lambda i, j: value[i * LANE : (i + 1) * LANE, j * LANE : (j + 1) * LANE]


def chip_kernel(kept_ref, other_ref, own_rows_ref, other_rows_ref, chip_ref, rows_ref, outer_ref):
    chip_ref[...] = kept_ref[...] + other_ref[...]
    core = lax.axis_index("grad")
    rows, columns = own_rows_ref.shape

    def put(start, ref):
        for column in range(columns // LANE):
            rows_ref[start : start + rows, :] = ref[:, column * LANE : (column + 1) * LANE]
            start += rows

    for own in range(2):

        @pl.when(core == own)
        def _():
            put(own * rows * columns // LANE, own_rows_ref)
            put((1 - own) * rows * columns // LANE, other_rows_ref)

    used = 2 * rows * columns // LANE
    rows_ref[used:, :] = jnp.zeros((rows_ref.shape[0] - used, LANE), jnp.float32)

    @pl.when(is_middle())
    def _():
        outer_ref[...] = rows_ref[...]

    @pl.when(jnp.logical_not(is_middle()))
    def _():
        outer_ref[...] = chip_ref[...]


def inverse_kernel(scale, order, *refs):
    *sums, rows_ref, out_ref, direct_ref, factor_ref = refs
    split = part_rows(order)[0]

    def piece(start, stop):
        total = sums[0][start:stop, :]
        for ref in sums[1:]:
            total = total + ref[start:stop, :]
        return total

    unpack(piece, lambda a, b: piece(split + a, split + b), order, factor_ref, None, scale, DAMPING)
    factor = factor_ref[...]
    bound = jnp.max(jnp.sum(jnp.abs(factor), axis=0, keepdims=True), axis=1, keepdims=True) + 1e-06
    start = START / bound
    rows = lax.broadcasted_iota(jnp.int32, (order, order), 0)
    cols = lax.broadcasted_iota(jnp.int32, (order, order), 1)
    eye = jnp.where(rows == cols, 1.0, 0.0)
    total = eye - start * factor
    power_halves = halves(total)
    middle = order // 2
    for step in range(1, ITERS):
        power = whole(*upper_times(power_halves, power_halves))
        power_halves = halves(power)
        top, corner = upper_times(halves(total), power_halves)
        known = total + power
        top, corner = top + known[:middle], corner + known[middle:, middle:]
        if step < ITERS - 1:
            total = whole(top, corner)

    def block(i, j):
        if i < middle // LANE:
            value = block_of(top)(i, j)
        else:
            value = block_of(corner)(i - middle // LANE, j - middle // LANE)
        return start * (value + block_of(eye)(i, j))

    pack(block, order, out_ref.at[:split], out_ref.at[split:], lax.axis_index("cuts") % 2 == 1)

    @pl.when(is_middle())
    def _():
        direct_ref[...] = out_ref[...]

    @pl.when(jnp.logical_not(is_middle()))
    def _():
        direct_ref[...] = rows_ref[...]


def choose_kernel(which, *refs):
    *arrays, out_ref = refs
    index = which()
    for place, ref in enumerate(arrays):

        @pl.when(index == place)
        def _():
            out_ref[...] = ref[...]


def final_kernel(
    order,
    spread,
    own_ref,
    other_ref,
    own_rows_ref,
    other_rows_ref,
    outer_ref,
    outer_other_ref,
    direct_ref,
    direct_other_ref,
    out_ref,
    left_ref,
    right_ref,
    tile_ref,
):
    core = lax.axis_index("grad")
    position = lax.axis_index("dp") * lax.axis_size("grad") + core
    mine = lax.rem(position, spread)
    rows_dev = out_ref.shape[0]
    split = part_rows(order)[0]

    def reader(ref, top):
        return lambda start, stop: ref[top + start : top + stop, :]

    def fill(packed_ref, out_ref, second):
        unpack(reader(packed_ref, 0), reader(packed_ref, split), order, out_ref, second)

    left_second = lax.rem(lax.div(position, spread), 2) == 1
    right_second = lax.rem(lax.axis_index("cuts"), 2) == 1

    @pl.when(core != 0)
    def _():
        fill(own_ref, left_ref, left_second)
        fill(other_ref, right_ref, right_second)

    @pl.when(core == 0)
    def _():
        fill(other_ref, left_ref, left_second)
        fill(own_ref, right_ref, right_second)

    def place(position):
        return pl.ds(pl.multiple_of(position * rows_dev, rows_dev), rows_dev)

    tile_ref[place(mine), :] = own_rows_ref[...]
    tile_ref[place(mine ^ 1), :] = other_rows_ref[...]
    here = core == rows_core()
    for middle, refs in ((False, (outer_ref, outer_other_ref)), (True, (direct_ref, direct_other_ref))):
        for own, ref in zip((True, False), refs):

            @pl.when(jnp.logical_and(is_middle() == middle, here == own))
            def _():
                start = 0
                for turn in range(2):
                    for column in range(order // LANE):
                        tile_ref[place((mine // 2 ^ 1) * 2 + turn), column * LANE : (column + 1) * LANE] = ref[
                            start : start + rows_dev, :
                        ]
                        start += rows_dev

    left = left_ref[pl.ds(pl.multiple_of(mine * rows_dev, rows_dev), rows_dev), :]
    middle = times(halves(left), halves(tile_ref[...]))
    out_ref[...] = times(halves(middle), halves(right_ref[...]))


def call(kernel, shapes, scratch, *args):
    return pl.pallas_call(
        kernel,
        out_shape=[jax.ShapeDtypeStruct(shape, jnp.float32) for shape in shapes],
        scratch_shapes=scratch,
        compiler_params=PARAMS,
    )(*args)


class Plan:
    def __init__(self, groups, dp, cuts):
        self.groups, self.dp, self.cuts = groups, dp, cuts
        self.bases = range(0, dp, QUAD)

    def index(self, z, x, core):
        return (z * self.cuts + x % self.cuts) * 2 + core

    def roots(self, base, x):
        return base + 1 + x % 2, base + 2 - x % 2

    def one_way(self, pairs):
        pairs = list(pairs)
        size = self.dp * self.cuts * 2
        return [(group * size + a, group * size + b) for group in range(self.groups) for a, b in pairs]

    def swaps(self, pairs):
        size = self.dp * self.cuts * 2
        partner = {}
        for a, b in self.one_way(pairs):
            partner[a], partner[b] = b, a
        for device in range(size * self.groups):
            other = device ^ 1
            if other in partner:
                other = (device + size) % (2 * size) + device // (2 * size) * 2 * size
            if device not in partner and other not in partner and other < size * self.groups:
                partner[device], partner[other] = other, device
        return sorted(partner.items())

    def across(self, bit):
        return self.one_way(
            (self.index(z, x, core), self.index(z ^ bit, x, core))
            for z in range(self.dp)
            for x in range(self.cuts)
            for core in range(2)
        )

    def collect(self):
        far, near, outer = [], [], []
        for x in range(self.cuts):
            for base in self.bases:
                left, right = self.roots(base, x)
                left_root, right_root = self.index(left, x, 1), self.index(right, x, 0)
                far.append((self.index(right ^ 1, x, 0), left_root))
                far.append((self.index(left ^ 1, x, 1), right_root))
                near.append((self.index(right, x, 0), left_root))
                outer.append((self.index(left ^ 1, x, 0), left_root))
                outer.append((self.index(right ^ 1, x, 1), right_root))
        return self.one_way(far), self.swaps(near), self.swaps(outer)

    def spread(self):
        hops = [[] for turn in range(1, self.cuts)]
        direct = []
        relays = [[] for turn in range(1, self.cuts)]
        for x in range(self.cuts):
            for base in self.bases:
                left, right = self.roots(base, x)
                right_root, middle = self.index(right, x, 0), self.index(left, x, 0)
                hops[0].append((right_root, middle))
                left_root = self.index(left, x, 1)
                direct.append((right_root, self.index(right ^ 1, x, 0)))
                direct.append((left_root, self.index(left ^ 1, x, 1)))
                relays[0].append((middle, self.index(left ^ 1, x, 0)))
                if x // 2 != base // QUAD:
                    continue
                for turn in range(1, self.cuts):
                    abreast = self.index(left, x + turn, 1)
                    hops[turn - 1].append((left_root, abreast))
                    relays[turn - 1].append((abreast, self.index(left ^ 1, x + turn, 1)))
        return [self.swaps(pairs) for pairs in hops], self.swaps(direct), [self.swaps(pairs) for pairs in relays]

    def which(self):
        z, x, core = (lax.axis_index(name) for name in AXES[1:])
        zq, middle = lax.rem(z, QUAD), is_middle()
        block = lax.div(z, 2)
        turn = lax.rem(x + self.cuts - block, self.cuts)
        left = jnp.where(middle, turn, jnp.where(turn == 0, self.cuts, self.cuts + turn))
        right_root = 2 - lax.rem(x, 2)
        right = jnp.where(
            zq == right_root, 0, jnp.where(middle, 1, jnp.where((zq ^ 1) == right_root, self.cuts, self.cuts + 1))
        )
        return jnp.where(core == 1, left, right)


def is_middle():
    zq = lax.rem(lax.axis_index("dp"), QUAD)
    return jnp.logical_or(zq == 1, zq == 2)


def rows_core():
    zq = lax.rem(lax.axis_index("dp"), QUAD)
    left = 1 + lax.rem(lax.axis_index("cuts"), 2)
    return jnp.where(is_middle(), zq == left, (zq ^ 1) != left).astype(jnp.int32)


def swap_cores(array):
    return lax.ppermute(array, "grad", [(0, 1), (1, 0)])


def per_device(acts, outgrads, grads):
    groups, dp, cuts, cores = (lax.axis_size(name) for name in AXES)
    tok_rows, order = acts.shape[1:]
    dev_count = dp * cores
    spread = dev_count // cuts
    plan = Plan(groups, dp, cuts)
    split, rest = part_rows(order)
    shape = (split + rest, LANE)
    acts, outgrads, grads = acts[0], outgrads[0], grads[0]

    (sent,), (kept,) = (
        call(functools.partial(cov_kernel, keep), [shape], [], acts, outgrads) for keep in (False, True)
    )
    other_rows = swap_cores(grads)
    chip, rows, outer = call(chip_kernel, [shape] * 3, [], kept, swap_cores(sent), grads, other_rows)
    bit = QUAD
    while bit < dp:
        chip = chip + lax.ppermute(chip, AXES, plan.across(bit))
        outer = jnp.where(is_middle(), outer, chip)
        bit *= 2
    far, near, outward = plan.collect()
    sums = [lax.ppermute(array, AXES, pairs) for array, pairs in ((chip, far), (chip, near), (outer, outward))]
    outer_rows = sums[2]
    sums.append(swap_cores(chip))
    scale = 1.0 / (tok_rows * dev_count)
    square_scratch = pltpu.VMEM((order, order), jnp.float32)
    inverse, direct = call(
        functools.partial(inverse_kernel, scale, order), [shape] * 2, [square_scratch], *sums, rows
    )

    hops, outward, relays = plan.spread()
    hopped = [lax.ppermute(inverse, AXES, pairs) for pairs in hops]
    direct = lax.ppermute(direct, AXES, outward)
    relayed = [lax.ppermute(array, AXES, pairs) for array, pairs in zip(hopped, relays)]
    (own,) = call(functools.partial(choose_kernel, plan.which), [shape], [], inverse, *hopped, direct, *relayed)
    (out,) = call(
        functools.partial(final_kernel, order, spread),
        [grads.shape],
        [square_scratch] * 3,
        own,
        swap_cores(own),
        grads,
        other_rows,
        outer_rows,
        swap_cores(outer_rows),
        direct,
        swap_cores(direct),
    )
    return out[None]


def solution(mesh):
    in_specs = (
        P(None, ("groups", "dp", "grad"), "cuts"),
        P(None, ("groups", "dp", "grad"), "cuts"),
        P("groups", ("dp", "grad"), "cuts"),
    )
    out_specs = P("groups", ("dp", "grad"), "cuts")
    return jax.shard_map(
        per_device, mesh=mesh, in_specs=in_specs, out_specs=out_specs, check_vma=False
    )
```

```python
import functools
import jax
import jax.numpy as jnp
from jax import lax
from jax.experimental import pallas as pl
from jax.experimental.pallas import tpu as pltpu
from jax.sharding import PartitionSpec as P

ITERS = 4
DAMPING = 0.5
START = 1.9
LANE = 128
QUAD = 4
AXES = ("groups", "dp", "cuts", "grad")
PARAMS = pltpu.CompilerParams(vmem_limit_bytes=48 * 1024 * 1024)


def half_blocks(order, half):
    count = order // LANE // 2
    own = range(half * count, (half + 1) * count)
    return [(i, j) for i in own for j in own if i < j], [(i, i + 1) for i in own[::2]]


def joining_blocks(order):
    count = order // LANE
    return [(i, j) for i in range(count // 2) for j in range(count // 2, count)]


def part_rows(order):
    above, pairs = half_blocks(order, 0)
    own = (len(above) + len(pairs)) * LANE + -(-len(pairs) // 8) * 8
    return len(joining_blocks(order)) * LANE, 2 * own


def places():
    rows = lax.broadcasted_iota(jnp.int32, (LANE, LANE), 0)
    cols = lax.broadcasted_iota(jnp.int32, (LANE, LANE), 1)
    return rows, cols


def pack(block, order, a_ref, b_ref):
    rows, cols = places()
    for slot, (i, j) in enumerate(joining_blocks(order)):
        a_ref[slot * LANE : (slot + 1) * LANE, :] = block(i, j)
    top = 0
    for half in range(2):
        above, pairs = half_blocks(order, half)
        values = [block(i, j) for i, j in above]
        values += [jnp.where(rows <= cols, block(i, i), block(j, j)) for i, j in pairs]
        last = [jnp.sum(jnp.where(rows == cols, block(j, j), 0.0), axis=0, keepdims=True) for _, j in pairs]
        values.append(jnp.concatenate(last + [jnp.zeros((-len(pairs) % 8, LANE), jnp.float32)], 0))
        for value in values:
            b_ref[top : top + value.shape[0], :] = value
            top += value.shape[0]


def unpack(a_piece, b_piece, order, out_ref, scale=1.0, shift=0.0):
    rows, cols = places()
    damping = jnp.where(rows == cols, shift, 0.0)

    def put(i, j, value):
        out_ref[i * LANE : (i + 1) * LANE, j * LANE : (j + 1) * LANE] = value

    def put_both(i, j, value):
        put(i, j, value)
        put(j, i, value.T)

    for slot, (i, j) in enumerate(joining_blocks(order)):
        put_both(i, j, a_piece(slot * LANE, (slot + 1) * LANE) * scale)
    top = 0
    for half in range(2):
        above, pairs = half_blocks(order, half)
        for i, j in above:
            put_both(i, j, b_piece(top, top + LANE) * scale)
            top += LANE
        after = top + len(pairs) * LANE
        last = b_piece(after, after + -(-len(pairs) // 8) * 8)
        for k, (i, j) in enumerate(pairs):
            both = b_piece(top, top + LANE)
            turned = both.T
            put(i, i, jnp.where(rows <= cols, both, turned) * scale + damping)
            second = jnp.where(rows > cols, both, jnp.where(rows < cols, turned, last[k : k + 1, :]))
            put(j, j, second * scale + damping)
            top += LANE
        top += last.shape[0]


def halves(value):
    high = value.astype(jnp.bfloat16)
    return high, (value - high.astype(jnp.float32)).astype(jnp.bfloat16)


def times(left, right):
    dot = functools.partial(jnp.dot, preferred_element_type=jnp.float32)
    return dot(left[0], right[0]) + (dot(left[0], right[1]) + dot(left[1], right[0]))


def rows_of(pair, start, stop):
    return pair[0][start:stop, :], pair[1][start:stop, :]


def upper_times(left, right):
    middle = left[0].shape[0] // 2
    top = times(rows_of(left, 0, middle), right)
    corner = times(rows_of(left, middle, 2 * middle), (right[0][:, middle:], right[1][:, middle:]))
    return top, corner


def upper_square(value):
    dot = functools.partial(jnp.dot, preferred_element_type=jnp.float32)
    high, low = value
    middle = high.shape[0] // 2
    mixed = dot(high, low)
    top = dot(high[:middle], high) + (mixed[:middle] + mixed[:, :middle].T)
    corner = mixed[middle:, middle:]
    return top, dot(high[middle:], high[:, middle:]) + (corner + corner.T)


def whole(top, corner):
    middle = corner.shape[0]
    return jnp.concatenate([top, jnp.concatenate([top[:, middle:].T, corner], 1)], 0)


def cov_kernel(x_ref, out_ref):
    x = x_ref[...]
    order = x.shape[1]
    split = part_rows(order)[0]
    total = lax.dot_general(x, x, (((0,), (0,)), ((), ())), preferred_element_type=jnp.float32)
    pack(block_of(total), order, out_ref.at[:split], out_ref.at[split:])


def block_of(value):
    return lambda i, j: value[i * LANE : (i + 1) * LANE, j * LANE : (j + 1) * LANE]


def chip_kernel(kept_ref, other_ref, own_rows_ref, other_rows_ref, chip_ref, rows_ref, outer_ref):
    chip_ref[...] = kept_ref[...] + other_ref[...]
    core = lax.axis_index("grad")
    rows, columns = own_rows_ref.shape

    def put(start, ref):
        for column in range(columns // LANE):
            rows_ref[start : start + rows, :] = ref[:, column * LANE : (column + 1) * LANE]
            start += rows

    for own in range(2):

        @pl.when(core == own)
        def _():
            put(own * rows * columns // LANE, own_rows_ref)
            put((1 - own) * rows * columns // LANE, other_rows_ref)

    used = 2 * rows * columns // LANE
    rows_ref[used:, :] = jnp.zeros((rows_ref.shape[0] - used, LANE), jnp.float32)

    @pl.when(is_middle())
    def _():
        outer_ref[...] = rows_ref[...]

    @pl.when(jnp.logical_not(is_middle()))
    def _():
        outer_ref[...] = chip_ref[...]


def inverse_kernel(scale, order, *refs):
    *sums, rows_ref, a_ref, b_ref, direct_ref, factor_ref = refs
    split = part_rows(order)[0]

    def piece(start, stop):
        total = sums[0][start:stop, :]
        for ref in sums[1:]:
            total = total + ref[start:stop, :]
        return total

    unpack(piece, lambda a, b: piece(split + a, split + b), order, factor_ref, scale, DAMPING)
    factor = factor_ref[...]
    bound = jnp.max(jnp.sum(jnp.abs(factor), axis=0, keepdims=True), axis=1, keepdims=True) + 1e-06
    start = START / bound
    rows = lax.broadcasted_iota(jnp.int32, (order, order), 0)
    cols = lax.broadcasted_iota(jnp.int32, (order, order), 1)
    eye = jnp.where(rows == cols, 1.0, 0.0)
    total = eye - start * factor
    power_halves = halves(total)
    middle = order // 2
    for step in range(1, ITERS):
        power = whole(*upper_square(power_halves))
        power_halves = halves(power)
        top, corner = upper_times(halves(total), power_halves)
        known = total + power
        top, corner = top + known[:middle], corner + known[middle:, middle:]
        if step < ITERS - 1:
            total = whole(top, corner)

    def block(i, j):
        if i < middle // LANE:
            value = block_of(top)(i, j)
        else:
            value = block_of(corner)(i - middle // LANE, j - middle // LANE)
        return start * (value + block_of(eye)(i, j))

    @pl.when(is_middle())
    def _():
        pack(block, order, a_ref, b_ref)
        direct_ref[:split, :] = a_ref[...]
        direct_ref[split:, :] = b_ref[...]

    @pl.when(jnp.logical_not(is_middle()))
    def _():
        a_ref[...] = rows_ref[:split, :]
        b_ref[...] = rows_ref[split:, :]
        direct_ref[...] = rows_ref[...]


def choose_kernel(which, start, *refs):
    *arrays, out_ref = refs
    index = which()
    rows = out_ref.shape[0]
    for place, ref in enumerate(arrays):
        first = 0 if ref.shape[0] == rows else start

        @pl.when(index == place)
        def _():
            out_ref[...] = ref[first : first + rows, :]


def final_kernel(order, spread, *refs):
    own, other, refs = refs[:2], refs[2:4], refs[4:]
    own_rows_ref, other_rows_ref, outer_ref, outer_other_ref, direct_ref, relayed_a, relayed_b, *refs = refs
    out_ref, left_ref, right_ref, tile_ref = refs
    core = lax.axis_index("grad")
    position = lax.axis_index("dp") * lax.axis_size("grad") + core
    mine = lax.rem(position, spread)
    rows_dev = out_ref.shape[0]
    def fill(parts, out_ref):
        a_ref, b_ref = parts
        unpack(lambda start, stop: a_ref[start:stop, :], lambda start, stop: b_ref[start:stop, :], order, out_ref)

    @pl.when(core != 0)
    def _():
        fill(own, left_ref)
        fill(other, right_ref)

    @pl.when(core == 0)
    def _():
        fill(other, left_ref)
        fill(own, right_ref)

    def place(position):
        return pl.ds(pl.multiple_of(position * rows_dev, rows_dev), rows_dev)

    tile_ref[place(mine), :] = own_rows_ref[...]
    tile_ref[place(mine ^ 1), :] = other_rows_ref[...]
    here = core == rows_core()
    cases = (
        (False, True, (outer_ref,)),
        (False, False, (outer_other_ref,)),
        (True, True, (direct_ref,)),
        (True, False, (relayed_a, relayed_b)),
    )
    for middle, arrived, parts in cases:

        @pl.when(jnp.logical_and(is_middle() == middle, here == arrived))
        def _():
            start, part = 0, 0
            for turn in range(2):
                for column in range(order // LANE):
                    if start == parts[part].shape[0]:
                        start, part = 0, part + 1
                    tile_ref[place((mine // 2 ^ 1) * 2 + turn), column * LANE : (column + 1) * LANE] = parts[part][
                        start : start + rows_dev, :
                    ]
                    start += rows_dev

    left = left_ref[pl.ds(pl.multiple_of(mine * rows_dev, rows_dev), rows_dev), :]
    middle = times(halves(left), halves(tile_ref[...]))
    out_ref[...] = times(halves(middle), halves(right_ref[...]))


def call(kernel, shapes, scratch, *args):
    return pl.pallas_call(
        kernel,
        out_shape=[jax.ShapeDtypeStruct(shape, jnp.float32) for shape in shapes],
        scratch_shapes=scratch,
        compiler_params=PARAMS,
    )(*args)


class Plan:
    def __init__(self, groups, dp, cuts):
        self.groups, self.dp, self.cuts = groups, dp, cuts
        self.bases = range(0, dp, QUAD)

    def index(self, z, x, core):
        return (z * self.cuts + x % self.cuts) * 2 + core

    def roots(self, base, x):
        return base + 1 + x % 2, base + 2 - x % 2

    def one_way(self, pairs):
        pairs = list(pairs)
        size = self.dp * self.cuts * 2
        return [(group * size + a, group * size + b) for group in range(self.groups) for a, b in pairs]

    def swaps(self, pairs):
        size = self.dp * self.cuts * 2
        partner = {}
        for a, b in self.one_way(pairs):
            partner[a], partner[b] = b, a
        for device in range(size * self.groups):
            other = device ^ 1
            if other in partner:
                other = (device + size) % (2 * size) + device // (2 * size) * 2 * size
            if device not in partner and other not in partner and other < size * self.groups:
                partner[device], partner[other] = other, device
        return sorted(partner.items())

    def across(self, bit):
        return self.one_way(
            (self.index(z, x, core), self.index(z ^ bit, x, core))
            for z in range(self.dp)
            for x in range(self.cuts)
            for core in range(2)
        )

    def collect(self):
        far, near, outer = [], [], []
        for x in range(self.cuts):
            for base in self.bases:
                left, right = self.roots(base, x)
                left_root, right_root = self.index(left, x, 1), self.index(right, x, 0)
                far.append((self.index(right ^ 1, x, 0), left_root))
                far.append((self.index(left ^ 1, x, 1), right_root))
                near.append((self.index(right, x, 0), left_root))
                outer.append((self.index(left ^ 1, x, 0), left_root))
                outer.append((self.index(right ^ 1, x, 1), right_root))
        return self.one_way(far), self.swaps(near), self.swaps(outer)

    def spread(self):
        hops = [[] for turn in range(1, self.cuts)]
        direct = []
        relays = [[] for turn in range(1, self.cuts)]
        for x in range(self.cuts):
            for base in self.bases:
                left, right = self.roots(base, x)
                right_root, middle = self.index(right, x, 0), self.index(left, x, 0)
                hops[0].append((right_root, middle))
                left_root = self.index(left, x, 1)
                direct.append((right_root, self.index(right ^ 1, x, 0)))
                direct.append((left_root, self.index(left ^ 1, x, 1)))
                relays[0].append((middle, self.index(left ^ 1, x, 0)))
                if x // 2 != base // QUAD:
                    continue
                for turn in range(1, self.cuts):
                    abreast = self.index(left, x + turn, 1)
                    hops[turn - 1].append((left_root, abreast))
                    relays[turn - 1].append((abreast, self.index(left ^ 1, x + turn, 1)))
        return [self.swaps(pairs) for pairs in hops], self.swaps(direct), [self.swaps(pairs) for pairs in relays]

    def which(self):
        z, x, core = (lax.axis_index(name) for name in AXES[1:])
        zq, middle = lax.rem(z, QUAD), is_middle()
        block = lax.div(z, 2)
        turn = lax.rem(x + self.cuts - block, self.cuts)
        left = jnp.where(middle, turn, jnp.where(turn == 0, self.cuts, self.cuts + turn))
        right_root = 2 - lax.rem(x, 2)
        right = jnp.where(
            zq == right_root, 0, jnp.where(middle, 1, jnp.where((zq ^ 1) == right_root, self.cuts, self.cuts + 1))
        )
        return jnp.where(core == 1, left, right)


def is_middle():
    zq = lax.rem(lax.axis_index("dp"), QUAD)
    return jnp.logical_or(zq == 1, zq == 2)


def rows_core():
    zq = lax.rem(lax.axis_index("dp"), QUAD)
    left = 1 + lax.rem(lax.axis_index("cuts"), 2)
    return jnp.where(is_middle(), zq == left, (zq ^ 1) != left).astype(jnp.int32)


def swap_cores(array):
    return lax.ppermute(array, "grad", [(0, 1), (1, 0)])


def per_device(acts, outgrads, grads):
    groups, dp, cuts, cores = (lax.axis_size(name) for name in AXES)
    tok_rows, order = acts.shape[1:]
    dev_count = dp * cores
    spread = dev_count // cuts
    plan = Plan(groups, dp, cuts)
    split, rest = part_rows(order)
    shape = (split + rest, LANE)
    acts, outgrads, grads = acts[0], outgrads[0], grads[0]

    core = lax.axis_index("grad")
    (sent,) = call(cov_kernel, [shape], [], jnp.where(core == 0, outgrads, acts))
    (kept,) = call(cov_kernel, [shape], [], jnp.where(core == 0, acts, outgrads))
    other_rows = swap_cores(grads)
    chip, rows, outer = call(chip_kernel, [shape] * 3, [], kept, swap_cores(sent), grads, other_rows)
    bit = QUAD
    while bit < dp:
        chip = chip + lax.ppermute(chip, AXES, plan.across(bit))
        outer = jnp.where(is_middle(), outer, chip)
        bit *= 2
    far, near, outward = plan.collect()
    sums = [lax.ppermute(array, AXES, pairs) for array, pairs in ((chip, far), (chip, near), (outer, outward))]
    outer_rows = sums[2]
    sums.append(swap_cores(chip))
    scale = 1.0 / (tok_rows * dev_count)
    square_scratch = pltpu.VMEM((order, order), jnp.float32)
    *inverse, direct = call(
        functools.partial(inverse_kernel, scale, order),
        [(split, LANE), (rest, LANE), shape],
        [square_scratch],
        *sums,
        rows,
    )

    hops, outward, relays = plan.spread()
    hopped = [[lax.ppermute(inverse[0], AXES, pairs) for pairs in hops]]
    direct = lax.ppermute(direct, AXES, outward)
    hopped.append([lax.ppermute(inverse[1], AXES, pairs) for pairs in hops])
    own, relayed = [], []
    for part, start in ((0, 0), (1, split)):
        arrived = [lax.ppermute(array, AXES, pairs) for array, pairs in zip(hopped[part], relays)]
        (chosen,) = call(
            functools.partial(choose_kernel, plan.which, start),
            [inverse[part].shape],
            [],
            inverse[part],
            *hopped[part],
            direct,
            *arrived,
        )
        own.append(chosen)
        relayed.append(arrived[0])
    (out,) = call(
        functools.partial(final_kernel, order, spread),
        [grads.shape],
        [square_scratch] * 3,
        *own,
        *map(swap_cores, own),
        grads,
        other_rows,
        outer_rows,
        swap_cores(outer_rows),
        direct,
        *relayed,
    )
    return out[None]


def solution(mesh):
    in_specs = (
        P(None, ("groups", "dp", "grad"), "cuts"),
        P(None, ("groups", "dp", "grad"), "cuts"),
        P("groups", ("dp", "grad"), "cuts"),
    )
    out_specs = P("groups", ("dp", "grad"), "cuts")
    return jax.shard_map(
        per_device, mesh=mesh, in_specs=in_specs, out_specs=out_specs, check_vma=False
    )
```

```python
import functools
import jax
import jax.numpy as jnp
from jax import lax
from jax.experimental import pallas as pl
from jax.experimental.pallas import tpu as pltpu
from jax.sharding import PartitionSpec as P

ITERS = 4
DAMPING = 0.5
START = 1.9
LANE = 128
QUAD = 4
AXES = ("groups", "dp", "cuts", "grad")
PARAMS = pltpu.CompilerParams(vmem_limit_bytes=48 * 1024 * 1024)


def half_blocks(order, half):
    count = order // LANE // 2
    own = range(half * count, (half + 1) * count)
    return [(i, j) for i in own for j in own if i < j], [(i, i + 1) for i in own[::2]]


def joining_blocks(order):
    count = order // LANE
    return [(i, j) for i in range(count // 2) for j in range(count // 2, count)]


def part_rows(order):
    above, pairs = half_blocks(order, 0)
    own = (len(above) + len(pairs)) * LANE + -(-len(pairs) // 8) * 8
    return len(joining_blocks(order)) * LANE, 2 * own


def places():
    rows = lax.broadcasted_iota(jnp.int32, (LANE, LANE), 0)
    cols = lax.broadcasted_iota(jnp.int32, (LANE, LANE), 1)
    return rows, cols


def pack(block, order, a_ref, b_ref):
    rows, cols = places()
    for slot, (i, j) in enumerate(joining_blocks(order)):
        a_ref[slot * LANE : (slot + 1) * LANE, :] = block(i, j)
    top = 0
    for half in range(2):
        above, pairs = half_blocks(order, half)
        values = [block(i, j) for i, j in above]
        values += [jnp.where(rows <= cols, block(i, i), block(j, j)) for i, j in pairs]
        last = [jnp.sum(jnp.where(rows == cols, block(j, j), 0.0), axis=0, keepdims=True) for _, j in pairs]
        values.append(jnp.concatenate(last + [jnp.zeros((-len(pairs) % 8, LANE), jnp.float32)], 0))
        for value in values:
            b_ref[top : top + value.shape[0], :] = value
            top += value.shape[0]


def unpack(a_piece, b_piece, order, out_ref, scale=1.0, shift=0.0):
    rows, cols = places()
    damping = jnp.where(rows == cols, shift, 0.0)

    def put(i, j, value):
        out_ref[i * LANE : (i + 1) * LANE, j * LANE : (j + 1) * LANE] = value

    def put_both(i, j, value):
        put(i, j, value)
        put(j, i, value.T)

    for slot, (i, j) in enumerate(joining_blocks(order)):
        put_both(i, j, a_piece(slot * LANE, (slot + 1) * LANE) * scale)
    top = 0
    for half in range(2):
        above, pairs = half_blocks(order, half)
        for i, j in above:
            put_both(i, j, b_piece(top, top + LANE) * scale)
            top += LANE
        after = top + len(pairs) * LANE
        last = b_piece(after, after + -(-len(pairs) // 8) * 8)
        for k, (i, j) in enumerate(pairs):
            both = b_piece(top, top + LANE)
            turned = both.T
            put(i, i, jnp.where(rows <= cols, both, turned) * scale + damping)
            second = jnp.where(rows > cols, both, jnp.where(rows < cols, turned, last[k : k + 1, :]))
            put(j, j, second * scale + damping)
            top += LANE
        top += last.shape[0]


def stored_block(a_ref, b_ref, order, i, j):
    if i > j:
        return stored_block(a_ref, b_ref, order, j, i).T
    if (i, j) in joining_blocks(order):
        start = joining_blocks(order).index((i, j)) * LANE
        return a_ref[start : start + LANE, :]
    half = i // (order // LANE // 2)
    above, pairs = half_blocks(order, half)
    top = half * part_rows(order)[1] // 2
    if i < j:
        start = top + above.index((i, j)) * LANE
        return b_ref[start : start + LANE, :]
    place = next(k for k, pair in enumerate(pairs) if i in pair)
    start = top + (len(above) + place) * LANE
    both = b_ref[start : start + LANE, :]
    rows, cols = places()
    if i == pairs[place][0]:
        return jnp.where(rows <= cols, both, both.T)
    start = top + (len(above) + len(pairs)) * LANE + place
    return jnp.where(rows > cols, both, jnp.where(rows < cols, both.T, b_ref[start : start + 1, :]))


def halves(value):
    high = value.astype(jnp.bfloat16)
    return high, (value - high.astype(jnp.float32)).astype(jnp.bfloat16)


def times(left, right):
    dot = functools.partial(jnp.dot, preferred_element_type=jnp.float32)
    rows = left[0].shape[0]
    both = dot(jnp.concatenate(left, 0), right[0])
    return both[:rows] + (dot(left[0], right[1]) + both[rows:])


def rows_of(pair, start, stop):
    return pair[0][start:stop, :], pair[1][start:stop, :]


def upper_times(left, right):
    middle = left[0].shape[0] // 2
    top = times(rows_of(left, 0, middle), right)
    corner = times(rows_of(left, middle, 2 * middle), (right[0][:, middle:], right[1][:, middle:]))
    return top, corner


def upper_square(value):
    dot = functools.partial(jnp.dot, preferred_element_type=jnp.float32)
    high, low = value
    middle = high.shape[0] // 2
    mixed = dot(high, low)
    top = dot(high[:middle], high) + (mixed[:middle] + mixed[:, :middle].T)
    corner = mixed[middle:, middle:]
    return top, dot(high[middle:], high[:, middle:]) + (corner + corner.T)


def whole(top, corner):
    middle = corner.shape[0]
    return jnp.concatenate([top, jnp.concatenate([top[:, middle:].T, corner], 1)], 0)


def cov_kernel(x_ref, out_ref):
    x = x_ref[...]
    order = x.shape[1]
    split = part_rows(order)[0]
    total = lax.dot_general(x, x, (((0,), (0,)), ((), ())), preferred_element_type=jnp.float32)
    pack(block_of(total), order, out_ref.at[:split], out_ref.at[split:])


def block_of(value):
    return lambda i, j: value[i * LANE : (i + 1) * LANE, j * LANE : (j + 1) * LANE]


def chip_kernel(kept_ref, other_ref, own_rows_ref, other_rows_ref, chip_ref, rows_ref, outer_ref):
    chip_ref[...] = kept_ref[...] + other_ref[...]
    core = lax.axis_index("grad")
    rows, columns = own_rows_ref.shape

    def put(start, ref):
        for column in range(columns // LANE):
            rows_ref[start : start + rows, :] = ref[:, column * LANE : (column + 1) * LANE]
            start += rows

    for own in range(2):

        @pl.when(core == own)
        def _():
            put(own * rows * columns // LANE, own_rows_ref)
            put((1 - own) * rows * columns // LANE, other_rows_ref)

    used = 2 * rows * columns // LANE
    rows_ref[used:, :] = jnp.zeros((rows_ref.shape[0] - used, LANE), jnp.float32)

    @pl.when(is_middle())
    def _():
        outer_ref[...] = rows_ref[...]

    @pl.when(jnp.logical_not(is_middle()))
    def _():
        outer_ref[...] = chip_ref[...]


def inverse_kernel(scale, order, *refs):
    *sums, rows_ref, a_ref, b_ref, direct_ref, factor_ref = refs
    split = part_rows(order)[0]

    def piece(start, stop):
        total = sums[0][start:stop, :]
        for ref in sums[1:]:
            total = total + ref[start:stop, :]
        return total

    unpack(piece, lambda a, b: piece(split + a, split + b), order, factor_ref, scale, DAMPING)
    factor = factor_ref[...]
    bound = jnp.max(jnp.sum(jnp.abs(factor), axis=0, keepdims=True), axis=1, keepdims=True) + 1e-06
    start = START / bound
    rows = lax.broadcasted_iota(jnp.int32, (order, order), 0)
    cols = lax.broadcasted_iota(jnp.int32, (order, order), 1)
    eye = jnp.where(rows == cols, 1.0, 0.0)
    total = eye - start * factor
    power_halves = halves(total)
    middle = order // 2
    for step in range(1, ITERS):
        power = whole(*upper_square(power_halves))
        power_halves = halves(power)
        top, corner = upper_times(halves(total), power_halves)
        known = total + power
        top, corner = top + known[:middle], corner + known[middle:, middle:]
        if step < ITERS - 1:
            total = whole(top, corner)

    def block(i, j):
        if i < middle // LANE:
            value = block_of(top)(i, j)
        else:
            value = block_of(corner)(i - middle // LANE, j - middle // LANE)
        return start * (value + block_of(eye)(i, j))

    @pl.when(is_middle())
    def _():
        pack(block, order, a_ref, b_ref)
        direct_ref[:split, :] = a_ref[...]
        direct_ref[split:, :] = b_ref[...]

    @pl.when(jnp.logical_not(is_middle()))
    def _():
        a_ref[...] = rows_ref[:split, :]
        b_ref[...] = rows_ref[split:, :]
        direct_ref[...] = rows_ref[...]


def choose_kernel(which, start, *refs):
    *arrays, out_ref = refs
    index = which()
    rows = out_ref.shape[0]
    for place, ref in enumerate(arrays):
        first = 0 if ref.shape[0] == rows else start

        @pl.when(index == place)
        def _():
            out_ref[...] = ref[first : first + rows, :]


def final_kernel(order, spread, *refs):
    own, other, refs = refs[:2], refs[2:4], refs[4:]
    own_rows_ref, other_rows_ref, outer_ref, outer_other_ref, direct_ref, relayed_a, relayed_b, *refs = refs
    out_ref, left_ref, right_ref, tile_ref, result_ref, sems = refs
    core = lax.axis_index("grad")
    position = lax.axis_index("dp") * lax.axis_size("grad") + core
    mine = lax.rem(position, spread)
    rows_dev = out_ref.shape[0]

    def fill(left, right):
        a_ref, b_ref = right
        unpack(lambda start, stop: a_ref[start:stop, :], lambda start, stop: b_ref[start:stop, :], order, right_ref)
        for row in range(order // LANE):

            @pl.when(mine == row)
            def _():
                for column in range(order // LANE):
                    block = stored_block(*left, order, row, column)
                    left_ref[:, column * LANE : (column + 1) * LANE] = block

    @pl.when(core != 0)
    def _():
        fill(own, other)

    @pl.when(core == 0)
    def _():
        fill(other, own)

    def place(position):
        return pl.ds(pl.multiple_of(position * rows_dev, rows_dev), rows_dev)

    tile_ref[place(mine), :] = own_rows_ref[...]
    tile_ref[place(mine ^ 1), :] = other_rows_ref[...]
    here = core == rows_core()
    cases = (
        (False, True, (outer_ref,)),
        (False, False, (outer_other_ref,)),
        (True, True, (direct_ref,)),
        (True, False, (relayed_a, relayed_b)),
    )
    for middle, arrived, parts in cases:

        @pl.when(jnp.logical_and(is_middle() == middle, here == arrived))
        def _():
            start, part = 0, 0
            for turn in range(2):
                for column in range(order // LANE):
                    if start == parts[part].shape[0]:
                        start, part = 0, part + 1
                    tile_ref[place((mine // 2 ^ 1) * 2 + turn), column * LANE : (column + 1) * LANE] = parts[part][
                        start : start + rows_dev, :
                    ]
                    start += rows_dev

    middle = halves(times(halves(left_ref[...]), halves(tile_ref[...])))
    step = order // 2
    copies = []
    for turn in range(2):
        columns = pl.ds(turn * step, step)
        result_ref[turn] = times(middle, halves(right_ref[:, turn * step : (turn + 1) * step]))
        copies.append(pltpu.make_async_copy(result_ref.at[turn], out_ref.at[:, columns], sems.at[turn]))
        copies[-1].start()
    for copy in copies:
        copy.wait()


def call(kernel, shapes, scratch, *args, space=pltpu.VMEM):
    return pl.pallas_call(
        kernel,
        out_shape=[jax.ShapeDtypeStruct(shape, jnp.float32) for shape in shapes],
        out_specs=[pl.BlockSpec(memory_space=space) for shape in shapes],
        scratch_shapes=scratch,
        compiler_params=PARAMS,
    )(*args)


class Plan:
    def __init__(self, groups, dp, cuts):
        self.groups, self.dp, self.cuts = groups, dp, cuts
        self.bases = range(0, dp, QUAD)

    def index(self, z, x, core):
        return (z * self.cuts + x % self.cuts) * 2 + core

    def roots(self, base, x):
        return base + 1 + x % 2, base + 2 - x % 2

    def one_way(self, pairs):
        pairs = list(pairs)
        size = self.dp * self.cuts * 2
        return [(group * size + a, group * size + b) for group in range(self.groups) for a, b in pairs]

    def swaps(self, pairs, abreast=False):
        size = self.dp * self.cuts * 2
        partner = {}
        for a, b in self.one_way(pairs):
            partner[a], partner[b] = b, a

        def pair_up(other):
            for device in range(size * self.groups):
                chosen = other(device)
                if device not in partner and chosen not in partner and chosen < size * self.groups:
                    partner[device], partner[chosen] = chosen, device

        pair_up(lambda device: device ^ 1)
        if abreast and self.cuts % 2 == 0:
            pair_up(lambda device: device ^ 3)
        pair_up(lambda device: (device + size) % (2 * size) + device // (2 * size) * 2 * size)
        return sorted(partner.items())

    def across(self, bit):
        return self.one_way(
            (self.index(z, x, core), self.index(z ^ bit, x, core))
            for z in range(self.dp)
            for x in range(self.cuts)
            for core in range(2)
        )

    def collect(self):
        far, near, outer = [], [], []
        for x in range(self.cuts):
            for base in self.bases:
                left, right = self.roots(base, x)
                left_root, right_root = self.index(left, x, 1), self.index(right, x, 0)
                far.append((self.index(right ^ 1, x, 0), left_root))
                far.append((self.index(left ^ 1, x, 1), right_root))
                near.append((self.index(right, x, 0), left_root))
                outer.append((self.index(left ^ 1, x, 0), left_root))
                outer.append((self.index(right ^ 1, x, 1), right_root))
        return self.one_way(far), self.swaps(near), self.swaps(outer)

    def spread(self):
        hops = [[] for turn in range(1, self.cuts)]
        direct = []
        relays = [[] for turn in range(1, self.cuts)]
        for x in range(self.cuts):
            for base in self.bases:
                left, right = self.roots(base, x)
                right_root, middle = self.index(right, x, 0), self.index(left, x, 0)
                hops[0].append((right_root, middle))
                left_root = self.index(left, x, 1)
                direct.append((right_root, self.index(right ^ 1, x, 0)))
                direct.append((left_root, self.index(left ^ 1, x, 1)))
                relays[0].append((middle, self.index(left ^ 1, x, 0)))
                if x // 2 != base // QUAD:
                    continue
                for turn in range(1, self.cuts):
                    abreast = self.index(left, x + turn, 1)
                    hops[turn - 1].append((left_root, abreast))
                    relays[turn - 1].append((abreast, self.index(left ^ 1, x + turn, 1)))
        return [self.swaps(pairs) for pairs in hops], self.swaps(direct), [self.swaps(pairs, True) for pairs in relays]

    def which(self):
        z, x, core = (lax.axis_index(name) for name in AXES[1:])
        zq, middle = lax.rem(z, QUAD), is_middle()
        block = lax.div(z, 2)
        turn = lax.rem(x + self.cuts - block, self.cuts)
        direct = 2 * self.cuts - 1
        left = jnp.where(middle, turn, jnp.where(turn == 0, direct, self.cuts - 1 + turn))
        right_root = 2 - lax.rem(x, 2)
        right = jnp.where(
            zq == right_root, 0, jnp.where(middle, 1, jnp.where((zq ^ 1) == right_root, direct, self.cuts))
        )
        return jnp.where(core == 1, left, right)


def is_middle():
    zq = lax.rem(lax.axis_index("dp"), QUAD)
    return jnp.logical_or(zq == 1, zq == 2)


def rows_core():
    zq = lax.rem(lax.axis_index("dp"), QUAD)
    left = 1 + lax.rem(lax.axis_index("cuts"), 2)
    return jnp.where(is_middle(), zq == left, (zq ^ 1) != left).astype(jnp.int32)


def swap_cores(array):
    return lax.ppermute(array, "grad", [(0, 1), (1, 0)])


def per_device(acts, outgrads, grads):
    groups, dp, cuts, cores = (lax.axis_size(name) for name in AXES)
    tok_rows, order = acts.shape[1:]
    dev_count = dp * cores
    spread = dev_count // cuts
    plan = Plan(groups, dp, cuts)
    split, rest = part_rows(order)
    shape = (split + rest, LANE)
    acts, outgrads, grads = acts[0], outgrads[0], grads[0]

    core = lax.axis_index("grad")
    (sent,) = call(cov_kernel, [shape], [], jnp.where(core == 0, outgrads, acts))
    (kept,) = call(cov_kernel, [shape], [], jnp.where(core == 0, acts, outgrads))
    other_rows = swap_cores(grads)
    chip, rows, outer = call(chip_kernel, [shape] * 3, [], kept, swap_cores(sent), grads, other_rows)
    bit = QUAD
    while bit < dp:
        chip = chip + lax.ppermute(chip, AXES, plan.across(bit))
        outer = jnp.where(is_middle(), outer, chip)
        bit *= 2
    far, near, outward = plan.collect()
    sums = [
        lax.ppermute(outer, AXES, outward),
        lax.ppermute(chip, AXES, near),
        lax.ppermute(chip, AXES, far),
        swap_cores(chip),
    ]
    outer_rows = sums[0]
    scale = 1.0 / (tok_rows * dev_count)
    square_scratch = pltpu.VMEM((order, order), jnp.float32)
    *inverse, direct = call(
        functools.partial(inverse_kernel, scale, order),
        [(split, LANE), (rest, LANE), shape],
        [square_scratch],
        *sums,
        rows,
    )

    hops, outward, relays = plan.spread()
    hopped = [[lax.ppermute(inverse[0], AXES, pairs) for pairs in hops]]
    direct = lax.ppermute(direct, AXES, outward)
    hopped.append([lax.ppermute(inverse[1], AXES, pairs) for pairs in hops])
    relayed = [[lax.ppermute(array, AXES, pairs) for array, pairs in zip(arrays, relays)] for arrays in hopped]
    relayed[1], direct = lax.optimization_barrier((relayed[1], direct))
    own = []
    for part, start in ((0, 0), (1, split)):
        own += call(
            functools.partial(choose_kernel, plan.which, start),
            [inverse[part].shape],
            [],
            inverse[part],
            *hopped[part],
            *relayed[part],
            direct,
        )
    (out,) = call(
        functools.partial(final_kernel, order, spread),
        [grads.shape],
        [
            pltpu.VMEM((LANE, order), jnp.float32),
            square_scratch,
            square_scratch,
            pltpu.VMEM((2, LANE, order // 2), jnp.float32),
            pltpu.SemaphoreType.DMA((2,)),
        ],
        *own,
        *map(swap_cores, own),
        grads,
        other_rows,
        outer_rows,
        swap_cores(outer_rows),
        direct,
        relayed[0][0],
        relayed[1][0],
        space=pl.ANY,
    )
    return out[None]


def solution(mesh):
    in_specs = (
        P(None, ("groups", "dp", "grad"), "cuts"),
        P(None, ("groups", "dp", "grad"), "cuts"),
        P("groups", ("dp", "grad"), "cuts"),
    )
    out_specs = P("groups", ("dp", "grad"), "cuts")
    return jax.shard_map(
        per_device, mesh=mesh, in_specs=in_specs, out_specs=out_specs, check_vma=False
    )
```

```python
import functools
import jax
import jax.numpy as jnp
from jax import lax
from jax.experimental import pallas as pl
from jax.experimental.pallas import tpu as pltpu
from jax.sharding import PartitionSpec as P

ITERS = 4
DAMPING = 0.5
START = 1.9
LANE = 128
QUAD = 4
AXES = ("groups", "dp", "cuts", "grad")
PARAMS = pltpu.CompilerParams(vmem_limit_bytes=48 * 1024 * 1024)


def half_blocks(order, half):
    count = order // LANE // 2
    own = range(half * count, (half + 1) * count)
    return [(i, j) for i in own for j in own if i < j], [(i, i + 1) for i in own[::2]]


def joining_blocks(order):
    count = order // LANE
    return [(i, j) for i in range(count // 2) for j in range(count // 2, count)]


def part_rows(order):
    above, pairs = half_blocks(order, 0)
    own = (len(above) + len(pairs)) * LANE + -(-len(pairs) // 8) * 8
    return len(joining_blocks(order)) * LANE, 2 * own


def own_start(order, half, second):
    rows = part_rows(order)[1] // 2
    return (half ^ second) * rows if isinstance(second, int) else pl.multiple_of((half ^ second) * rows, 8)


def places():
    rows = lax.broadcasted_iota(jnp.int32, (LANE, LANE), 0)
    cols = lax.broadcasted_iota(jnp.int32, (LANE, LANE), 1)
    return rows, cols


def pack(block, order, a_ref, b_ref, second=0):
    rows, cols = places()
    for slot, (i, j) in enumerate(joining_blocks(order)):
        a_ref[slot * LANE : (slot + 1) * LANE, :] = block(i, j)
    for half in range(2):
        top = own_start(order, half, second)
        above, pairs = half_blocks(order, half)
        values = [block(i, j) for i, j in above]
        values += [jnp.where(rows <= cols, block(i, i), block(j, j)) for i, j in pairs]
        last = [jnp.sum(jnp.where(rows == cols, block(j, j), 0.0), axis=0, keepdims=True) for _, j in pairs]
        values.append(jnp.concatenate(last + [jnp.zeros((-len(pairs) % 8, LANE), jnp.float32)], 0))
        for value in values:
            b_ref[pl.ds(top, value.shape[0]), :] = value
            top += value.shape[0]


def unpack(a_piece, b_piece, order, out_ref, second=0, scale=1.0, shift=0.0):
    rows, cols = places()
    damping = jnp.where(rows == cols, shift, 0.0)

    def put(i, j, value):
        out_ref[i * LANE : (i + 1) * LANE, j * LANE : (j + 1) * LANE] = value

    def put_both(i, j, value):
        put(i, j, value)
        put(j, i, value.T)

    for slot, (i, j) in enumerate(joining_blocks(order)):
        put_both(i, j, a_piece(slot * LANE, LANE) * scale)
    for half in range(2):
        top = own_start(order, half, second)
        above, pairs = half_blocks(order, half)
        for i, j in above:
            put_both(i, j, b_piece(top, LANE) * scale)
            top += LANE
        last = b_piece(top + len(pairs) * LANE, -(-len(pairs) // 8) * 8)
        for k, (i, j) in enumerate(pairs):
            both = b_piece(top, LANE)
            turned = both.T
            put(i, i, jnp.where(rows <= cols, both, turned) * scale + damping)
            after = jnp.where(rows > cols, both, jnp.where(rows < cols, turned, last[k : k + 1, :]))
            put(j, j, after * scale + damping)
            top += LANE


def stored_block(a_ref, b_ref, order, i, j, second):
    if i > j:
        return stored_block(a_ref, b_ref, order, j, i, second).T
    if (i, j) in joining_blocks(order):
        start = joining_blocks(order).index((i, j)) * LANE
        return a_ref[start : start + LANE, :]
    half = i // (order // LANE // 2)
    above, pairs = half_blocks(order, half)
    top = own_start(order, half, second)
    if i < j:
        return b_ref[pl.ds(top + above.index((i, j)) * LANE, LANE), :]
    place = next(k for k, pair in enumerate(pairs) if i in pair)
    both = b_ref[pl.ds(top + (len(above) + place) * LANE, LANE), :]
    rows, cols = places()
    if i == pairs[place][0]:
        return jnp.where(rows <= cols, both, both.T)
    last = b_ref[pl.ds(top + (len(above) + len(pairs)) * LANE, -(-len(pairs) // 8) * 8), :]
    return jnp.where(rows > cols, both, jnp.where(rows < cols, both.T, last[place : place + 1, :]))


def halves(value):
    high = value.astype(jnp.bfloat16)
    return high, (value - high.astype(jnp.float32)).astype(jnp.bfloat16)


def times(left, right):
    dot = functools.partial(jnp.dot, preferred_element_type=jnp.float32)
    rows = left[0].shape[0]
    both = dot(jnp.concatenate(left, 0), right[0])
    return both[:rows] + (dot(left[0], right[1]) + both[rows:])


def rows_of(pair, start, stop):
    return pair[0][start:stop, :], pair[1][start:stop, :]


def upper_times(left, right):
    middle = left[0].shape[0] // 2
    top = times(rows_of(left, 0, middle), right)
    corner = times(rows_of(left, middle, 2 * middle), (right[0][:, middle:], right[1][:, middle:]))
    return top, corner


def upper_square(value):
    dot = functools.partial(jnp.dot, preferred_element_type=jnp.float32)
    high, low = value
    middle = high.shape[0] // 2
    mixed = dot(high, low)
    top = dot(high[:middle], high) + (mixed[:middle] + mixed[:, :middle].T)
    corner = mixed[middle:, middle:]
    return top, dot(high[middle:], high[:, middle:]) + (corner + corner.T)


def whole(top, corner):
    middle = corner.shape[0]
    return jnp.concatenate([top, jnp.concatenate([top[:, middle:].T, corner], 1)], 0)


def cov_kernel(x_ref, out_ref):
    x = x_ref[...]
    order = x.shape[1]
    split = part_rows(order)[0]
    total = lax.dot_general(x, x, (((0,), (0,)), ((), ())), preferred_element_type=jnp.float32)
    pack(block_of(total), order, out_ref.at[:split], out_ref.at[split:])


def block_of(value):
    return lambda i, j: value[i * LANE : (i + 1) * LANE, j * LANE : (j + 1) * LANE]


def chip_kernel(kept_ref, other_ref, own_rows_ref, other_rows_ref, chip_ref, rows_ref, outer_ref):
    chip_ref[...] = kept_ref[...] + other_ref[...]
    core = lax.axis_index("grad")
    rows, columns = own_rows_ref.shape

    def put(start, ref):
        for column in range(columns // LANE):
            rows_ref[start : start + rows, :] = ref[:, column * LANE : (column + 1) * LANE]
            start += rows

    for own in range(2):

        @pl.when(core == own)
        def _():
            put(own * rows * columns // LANE, own_rows_ref)
            put((1 - own) * rows * columns // LANE, other_rows_ref)

    used = 2 * rows * columns // LANE
    rows_ref[used:, :] = jnp.zeros((rows_ref.shape[0] - used, LANE), jnp.float32)

    @pl.when(is_middle())
    def _():
        outer_ref[...] = rows_ref[...]

    @pl.when(jnp.logical_not(is_middle()))
    def _():
        outer_ref[...] = chip_ref[...]


def inverse_kernel(scale, order, *refs):
    *sums, rows_ref, a_ref, b_ref, direct_ref, rest_ref, factor_ref = refs
    split = part_rows(order)[0]

    def piece(start, size):
        total = sums[0][start : start + size, :]
        for ref in sums[1:]:
            total = total + ref[start : start + size, :]
        return total

    unpack(piece, lambda start, size: piece(split + start, size), order, factor_ref, 0, scale, DAMPING)
    factor = factor_ref[...]
    bound = jnp.max(jnp.sum(jnp.abs(factor), axis=0, keepdims=True), axis=1, keepdims=True) + 1e-06
    start = START / bound
    rows = lax.broadcasted_iota(jnp.int32, (order, order), 0)
    cols = lax.broadcasted_iota(jnp.int32, (order, order), 1)
    eye = jnp.where(rows == cols, 1.0, 0.0)
    total = eye - start * factor
    power_halves = halves(total)
    middle = order // 2
    for step in range(1, ITERS):
        power = whole(*upper_square(power_halves))
        power_halves = halves(power)
        top, corner = upper_times(halves(total), power_halves)
        known = total + power
        top, corner = top + known[:middle], corner + known[middle:, middle:]
        if step < ITERS - 1:
            total = whole(top, corner)

    def block(i, j):
        if i < middle // LANE:
            value = block_of(top)(i, j)
        else:
            value = block_of(corner)(i - middle // LANE, j - middle // LANE)
        return start * (value + block_of(eye)(i, j))

    used = direct_ref.shape[0] - split

    @pl.when(is_middle())
    def _():
        pack(block, order, a_ref, b_ref, lax.rem(lax.axis_index("cuts"), 2))
        direct_ref[:split, :] = a_ref[...]
        direct_ref[split:, :] = b_ref[:used, :]
        rest_ref[...] = b_ref[used:, :]

    @pl.when(jnp.logical_not(is_middle()))
    def _():
        a_ref[...] = rows_ref[:split, :]
        b_ref[...] = rows_ref[split:, :]
        direct_ref[...] = rows_ref[: split + used, :]
        rest_ref[...] = rows_ref[:used, :]


def relay_kernel(hopped_ref, rest_ref, out_ref):
    used = rest_ref.shape[0]
    out_ref[:used, :] = hopped_ref[:used, :]
    rest = jnp.logical_and(is_middle(), lax.axis_index("grad") == 1)

    @pl.when(rest)
    def _():
        out_ref[used:, :] = rest_ref[...]

    @pl.when(jnp.logical_not(rest))
    def _():
        out_ref[used:, :] = hopped_ref[used:, :]


def choose_kernel(which, start, *refs):
    *arrays, out_ref = refs
    index = which()
    rows = out_ref.shape[0]
    for place, ref in enumerate(arrays):
        first = start if place == len(arrays) - 1 else 0
        size = min(rows, ref.shape[0] - first)

        @pl.when(index == place)
        def _():
            out_ref[:size, :] = ref[first : first + size, :]
            if size < rows:
                out_ref[size:, :] = jnp.zeros((rows - size, LANE), jnp.float32)


def final_kernel(order, spread, *refs):
    own, other, refs = refs[:2], refs[2:4], refs[4:]
    own_rows_ref, other_rows_ref, outer_ref, outer_other_ref, direct_ref, relayed_a, relayed_b, other_b, *refs = refs
    out_ref, left_ref, right_ref, tile_ref, result_ref, b_ref, sems = refs
    core = lax.axis_index("grad")
    position = lax.axis_index("dp") * lax.axis_size("grad") + core
    mine = lax.rem(position, spread)
    rows_dev = out_ref.shape[0]

    cut = lax.axis_index("cuts")
    zq = lax.rem(lax.axis_index("dp"), QUAD)
    was_direct = jnp.logical_and(jnp.logical_not(is_middle()), (zq ^ 1) == 2 - lax.rem(cut, 2))
    left_second = lax.rem(lax.div(position, spread), 2)

    def fill(left, right):
        used = b_ref.shape[0] // 2
        b_ref[...] = right[1][...]

        @pl.when(was_direct)
        def _():
            b_ref[used:, :] = left[1][used:, :]

        unpack(
            lambda start, size: right[0][pl.ds(start, size), :],
            lambda start, size: b_ref[pl.ds(start, size), :],
            order,
            right_ref,
            lax.rem(cut, 2),
        )
        for row in range(order // LANE):

            @pl.when(mine == row)
            def _():
                for column in range(order // LANE):
                    block = stored_block(*left, order, row, column, left_second)
                    left_ref[:, column * LANE : (column + 1) * LANE] = block

    @pl.when(core != 0)
    def _():
        fill(own, other)

    @pl.when(core == 0)
    def _():
        fill(other, own)

    def place(position):
        return pl.ds(pl.multiple_of(position * rows_dev, rows_dev), rows_dev)

    tile_ref[place(mine), :] = own_rows_ref[...]
    tile_ref[place(mine ^ 1), :] = other_rows_ref[...]
    here = core == rows_core()
    cases = (
        (False, True, (outer_ref,)),
        (False, False, (outer_other_ref,)),
        (True, True, (direct_ref.at[: relayed_a.shape[0]], other_b)),
        (True, False, (relayed_a, relayed_b)),
    )
    for middle, arrived, parts in cases:

        @pl.when(jnp.logical_and(is_middle() == middle, here == arrived))
        def _():
            start, part = 0, 0
            for turn in range(2):
                for column in range(order // LANE):
                    if start == parts[part].shape[0]:
                        start, part = 0, part + 1
                    tile_ref[place((mine // 2 ^ 1) * 2 + turn), column * LANE : (column + 1) * LANE] = parts[part][
                        start : start + rows_dev, :
                    ]
                    start += rows_dev

    middle = halves(times(halves(left_ref[...]), halves(tile_ref[...])))
    step = order // 2
    copies = []
    for turn in range(2):
        columns = pl.ds(turn * step, step)
        result_ref[turn] = times(middle, halves(right_ref[:, turn * step : (turn + 1) * step]))
        copies.append(pltpu.make_async_copy(result_ref.at[turn], out_ref.at[:, columns], sems.at[turn]))
        copies[-1].start()
    for copy in copies:
        copy.wait()


def call(kernel, shapes, scratch, *args, space=pltpu.VMEM):
    return pl.pallas_call(
        kernel,
        out_shape=[jax.ShapeDtypeStruct(shape, jnp.float32) for shape in shapes],
        out_specs=[pl.BlockSpec(memory_space=space) for shape in shapes],
        scratch_shapes=scratch,
        compiler_params=PARAMS,
    )(*args)


class Plan:
    def __init__(self, groups, dp, cuts):
        self.groups, self.dp, self.cuts = groups, dp, cuts
        self.bases = range(0, dp, QUAD)

    def index(self, z, x, core):
        return (z * self.cuts + x % self.cuts) * 2 + core

    def roots(self, base, x):
        return base + 1 + x % 2, base + 2 - x % 2

    def one_way(self, pairs):
        pairs = list(pairs)
        size = self.dp * self.cuts * 2
        return [(group * size + a, group * size + b) for group in range(self.groups) for a, b in pairs]

    def swaps(self, pairs, abreast=False):
        size = self.dp * self.cuts * 2
        partner = {}
        for a, b in self.one_way(pairs):
            partner[a], partner[b] = b, a

        def pair_up(other):
            for device in range(size * self.groups):
                chosen = other(device)
                if device not in partner and chosen not in partner and chosen < size * self.groups:
                    partner[device], partner[chosen] = chosen, device

        pair_up(lambda device: device ^ 1)
        if abreast and self.cuts % 2 == 0:
            pair_up(lambda device: device ^ 3)
        pair_up(lambda device: (device + size) % (2 * size) + device // (2 * size) * 2 * size)
        return sorted(partner.items())

    def across(self, bit):
        return self.one_way(
            (self.index(z, x, core), self.index(z ^ bit, x, core))
            for z in range(self.dp)
            for x in range(self.cuts)
            for core in range(2)
        )

    def collect(self):
        far, near, outer = [], [], []
        for x in range(self.cuts):
            for base in self.bases:
                left, right = self.roots(base, x)
                left_root, right_root = self.index(left, x, 1), self.index(right, x, 0)
                far.append((self.index(right ^ 1, x, 0), left_root))
                far.append((self.index(left ^ 1, x, 1), right_root))
                near.append((self.index(right, x, 0), left_root))
                outer.append((self.index(left ^ 1, x, 0), left_root))
                outer.append((self.index(right ^ 1, x, 1), right_root))
        return self.one_way(far), self.swaps(near), self.swaps(outer)

    def spread(self):
        hops = [[] for turn in range(1, self.cuts)]
        direct = []
        relays = [[] for turn in range(1, self.cuts)]
        for x in range(self.cuts):
            for base in self.bases:
                left, right = self.roots(base, x)
                right_root, middle = self.index(right, x, 0), self.index(left, x, 0)
                hops[0].append((right_root, middle))
                left_root = self.index(left, x, 1)
                direct.append((right_root, self.index(right ^ 1, x, 0)))
                direct.append((left_root, self.index(left ^ 1, x, 1)))
                relays[0].append((middle, self.index(left ^ 1, x, 0)))
                if x // 2 != base // QUAD:
                    continue
                for turn in range(1, self.cuts):
                    abreast = self.index(left, x + turn, 1)
                    hops[turn - 1].append((left_root, abreast))
                    relays[turn - 1].append((abreast, self.index(left ^ 1, x + turn, 1)))
        return [self.swaps(pairs) for pairs in hops], self.swaps(direct), [self.swaps(pairs, True) for pairs in relays]

    def turn(self):
        z, x, core = (lax.axis_index(name) for name in AXES[1:])
        turn = lax.rem(x + self.cuts - lax.div(z, 2), self.cuts)
        return jnp.where(core == 1, jnp.maximum(turn - 1, 0), 0)

    def which(self):
        z, x, core = (lax.axis_index(name) for name in AXES[1:])
        zq, middle = lax.rem(z, QUAD), is_middle()
        block = lax.div(z, 2)
        turn = lax.rem(x + self.cuts - block, self.cuts)
        direct = 2 * self.cuts - 1
        left = jnp.where(middle, turn, jnp.where(turn == 0, direct, self.cuts - 1 + turn))
        right_root = 2 - lax.rem(x, 2)
        right = jnp.where(
            zq == right_root, 0, jnp.where(middle, 1, jnp.where((zq ^ 1) == right_root, direct, self.cuts))
        )
        return jnp.where(core == 1, left, right)


def is_middle():
    zq = lax.rem(lax.axis_index("dp"), QUAD)
    return jnp.logical_or(zq == 1, zq == 2)


def rows_core():
    zq = lax.rem(lax.axis_index("dp"), QUAD)
    left = 1 + lax.rem(lax.axis_index("cuts"), 2)
    return jnp.where(is_middle(), zq == left, (zq ^ 1) != left).astype(jnp.int32)


def swap_cores(array):
    return lax.ppermute(array, "grad", [(0, 1), (1, 0)])


def per_device(acts, outgrads, grads):
    groups, dp, cuts, cores = (lax.axis_size(name) for name in AXES)
    tok_rows, order = acts.shape[1:]
    dev_count = dp * cores
    spread = dev_count // cuts
    plan = Plan(groups, dp, cuts)
    split, rest = part_rows(order)
    shape = (split + rest, LANE)
    acts, outgrads, grads = acts[0], outgrads[0], grads[0]

    core = lax.axis_index("grad")
    (sent,) = call(cov_kernel, [shape], [], jnp.where(core == 0, outgrads, acts))
    (kept,) = call(cov_kernel, [shape], [], jnp.where(core == 0, acts, outgrads))
    other_rows = swap_cores(grads)
    chip, rows, outer = call(chip_kernel, [shape] * 3, [], kept, swap_cores(sent), grads, other_rows)
    bit = QUAD
    while bit < dp:
        chip = chip + lax.ppermute(chip, AXES, plan.across(bit))
        outer = jnp.where(is_middle(), outer, chip)
        bit *= 2
    far, near, outward = plan.collect()
    sums = [
        lax.ppermute(outer, AXES, outward),
        lax.ppermute(chip, AXES, near),
        lax.ppermute(chip, AXES, far),
        swap_cores(chip),
    ]
    outer_rows = sums[0]
    scale = 1.0 / (tok_rows * dev_count)
    square_scratch = pltpu.VMEM((order, order), jnp.float32)
    *inverse, direct, rest_own = call(
        functools.partial(inverse_kernel, scale, order),
        [(split, LANE), (rest, LANE), (split + rest // 2, LANE), (rest // 2, LANE)],
        [square_scratch],
        *sums,
        rows,
    )

    hops, outward, relays = plan.spread()
    hopped = [[lax.ppermute(inverse[0], AXES, pairs) for pairs in hops]]
    direct = lax.ppermute(direct, AXES, outward)
    hopped.append([lax.ppermute(inverse[1], AXES, pairs) for pairs in hops])
    rest_own = swap_cores(rest_own)
    carried = [
        hopped[0],
        [call(relay_kernel, [array.shape], [], array, rest_own)[0] for array in hopped[1]],
    ]
    relayed = [[lax.ppermute(array, AXES, pairs) for array, pairs in zip(arrays, relays)] for arrays in carried]
    relayed[1], direct = lax.optimization_barrier((relayed[1], direct))
    arrived = [
        arrays[0] if cuts == 2 else call(functools.partial(choose_kernel, plan.turn, 0), [arrays[0].shape], [], *arrays)[0]
        for arrays in relayed
    ]
    own = []
    for part, start in ((0, 0), (1, split)):
        own += call(
            functools.partial(choose_kernel, plan.which, start),
            [inverse[part].shape],
            [],
            inverse[part],
            *hopped[part],
            *relayed[part],
            direct,
        )
    (out,) = call(
        functools.partial(final_kernel, order, spread),
        [grads.shape],
        [
            pltpu.VMEM((LANE, order), jnp.float32),
            square_scratch,
            square_scratch,
            pltpu.VMEM((2, LANE, order // 2), jnp.float32),
            pltpu.VMEM((rest, LANE), jnp.float32),
            pltpu.SemaphoreType.DMA((2,)),
        ],
        *own,
        *map(swap_cores, own),
        grads,
        other_rows,
        outer_rows,
        swap_cores(outer_rows),
        direct,
        *arrived,
        swap_cores(arrived[1]),
        space=pl.ANY,
    )
    return out[None]


def solution(mesh):
    in_specs = (
        P(None, ("groups", "dp", "grad"), "cuts"),
        P(None, ("groups", "dp", "grad"), "cuts"),
        P("groups", ("dp", "grad"), "cuts"),
    )
    out_specs = P("groups", ("dp", "grad"), "cuts")
    return jax.shard_map(
        per_device, mesh=mesh, in_specs=in_specs, out_specs=out_specs, check_vma=False
    )
```

```python
import functools
import jax
import jax.numpy as jnp
from jax import lax
from jax.experimental import pallas as pl
from jax.experimental.pallas import tpu as pltpu
from jax.sharding import PartitionSpec as P

ITERS = 4
DAMPING = 0.5
START = 1.9
LANE = 128
QUAD = 4
AXES = ("groups", "dp", "cuts", "grad")
PARAMS = pltpu.CompilerParams(vmem_limit_bytes=48 * 1024 * 1024)


def half_blocks(order, half):
    count = order // LANE // 2
    own = range(half * count, (half + 1) * count)
    return [(i, j) for i in own for j in own if i < j], [(i, i + 1) for i in own[::2]]


def joining_blocks(order):
    count = order // LANE
    return [(i, j) for i in range(count // 2) for j in range(count // 2, count)]


def part_rows(order):
    above, pairs = half_blocks(order, 0)
    own = (len(above) + len(pairs)) * LANE + -(-len(pairs) // 8) * 8
    return len(joining_blocks(order)) * LANE, 2 * own


def own_start(order, half, second):
    rows = part_rows(order)[1] // 2
    return (half ^ second) * rows if isinstance(second, int) else pl.multiple_of((half ^ second) * rows, 8)


def places():
    rows = lax.broadcasted_iota(jnp.int32, (LANE, LANE), 0)
    cols = lax.broadcasted_iota(jnp.int32, (LANE, LANE), 1)
    return rows, cols


def pack(block, order, a_ref, b_ref, second=0):
    rows, cols = places()
    for slot, (i, j) in enumerate(joining_blocks(order)):
        a_ref[slot * LANE : (slot + 1) * LANE, :] = block(i, j)
    for half in range(2):
        top = own_start(order, half, second)
        above, pairs = half_blocks(order, half)
        values = [block(i, j) for i, j in above]
        values += [jnp.where(rows <= cols, block(i, i), block(j, j)) for i, j in pairs]
        last = [jnp.sum(jnp.where(rows == cols, block(j, j), 0.0), axis=0, keepdims=True) for _, j in pairs]
        values.append(jnp.concatenate(last + [jnp.zeros((-len(pairs) % 8, LANE), jnp.float32)], 0))
        for value in values:
            b_ref[pl.ds(top, value.shape[0]), :] = value
            top += value.shape[0]


def unpack(a_piece, b_piece, order, out_ref, second=0, scale=1.0, shift=0.0):
    rows, cols = places()
    damping = jnp.where(rows == cols, shift, 0.0)

    def put(i, j, value):
        out_ref[i * LANE : (i + 1) * LANE, j * LANE : (j + 1) * LANE] = value

    def put_both(i, j, value):
        put(i, j, value)
        put(j, i, value.T)

    for slot, (i, j) in enumerate(joining_blocks(order)):
        put_both(i, j, a_piece(slot * LANE, LANE) * scale)
    for half in range(2):
        top = own_start(order, half, second)
        above, pairs = half_blocks(order, half)
        for i, j in above:
            put_both(i, j, b_piece(top, LANE) * scale)
            top += LANE
        last = b_piece(top + len(pairs) * LANE, -(-len(pairs) // 8) * 8)
        for k, (i, j) in enumerate(pairs):
            both = b_piece(top, LANE)
            turned = both.T
            put(i, i, jnp.where(rows <= cols, both, turned) * scale + damping)
            after = jnp.where(rows > cols, both, jnp.where(rows < cols, turned, last[k : k + 1, :]))
            put(j, j, after * scale + damping)
            top += LANE


def stored_block(a_ref, b_ref, order, i, j, second):
    if i > j:
        return stored_block(a_ref, b_ref, order, j, i, second).T
    if (i, j) in joining_blocks(order):
        start = joining_blocks(order).index((i, j)) * LANE
        return a_ref[start : start + LANE, :]
    half = i // (order // LANE // 2)
    above, pairs = half_blocks(order, half)
    top = own_start(order, half, second)
    if i < j:
        return b_ref[pl.ds(top + above.index((i, j)) * LANE, LANE), :]
    place = next(k for k, pair in enumerate(pairs) if i in pair)
    both = b_ref[pl.ds(top + (len(above) + place) * LANE, LANE), :]
    rows, cols = places()
    if i == pairs[place][0]:
        return jnp.where(rows <= cols, both, both.T)
    last = b_ref[pl.ds(top + (len(above) + len(pairs)) * LANE, -(-len(pairs) // 8) * 8), :]
    return jnp.where(rows > cols, both, jnp.where(rows < cols, both.T, last[place : place + 1, :]))


def halves(value):
    high = value.astype(jnp.bfloat16)
    return high, (value - high.astype(jnp.float32)).astype(jnp.bfloat16)


def times(left, right):
    dot = functools.partial(jnp.dot, preferred_element_type=jnp.float32)
    rows = left[0].shape[0]
    both = dot(jnp.concatenate(left, 0), right[0])
    return both[:rows] + (dot(left[0], right[1]) + both[rows:])


def rows_of(pair, start, stop):
    return pair[0][start:stop, :], pair[1][start:stop, :]


def upper_times(left, right):
    middle = left[0].shape[0] // 2
    top = times(rows_of(left, 0, middle), right)
    corner = times(rows_of(left, middle, 2 * middle), (right[0][:, middle:], right[1][:, middle:]))
    return top, corner


def upper_square(value):
    dot = functools.partial(jnp.dot, preferred_element_type=jnp.float32)
    high, low = value
    middle = high.shape[0] // 2
    mixed = dot(high, low)
    top = dot(high[:middle], high) + (mixed[:middle] + mixed[:, :middle].T)
    corner = mixed[middle:, middle:]
    return top, dot(high[middle:], high[:, middle:]) + (corner + corner.T)


def whole(top, corner):
    middle = corner.shape[0]
    return jnp.concatenate([top, jnp.concatenate([top[:, middle:].T, corner], 1)], 0)


def cov_kernel(x_ref, out_ref):
    x = x_ref[...]
    order = x.shape[1]
    split = part_rows(order)[0]
    total = lax.dot_general(x, x, (((0,), (0,)), ((), ())), preferred_element_type=jnp.float32)
    pack(block_of(total), order, out_ref.at[:split], out_ref.at[split:])


def block_of(value):
    return lambda i, j: value[i * LANE : (i + 1) * LANE, j * LANE : (j + 1) * LANE]


def chip_kernel(kept_ref, other_ref, own_rows_ref, other_rows_ref, chip_ref, rows_ref, outer_ref):
    chip_ref[...] = kept_ref[...] + other_ref[...]
    core = lax.axis_index("grad")
    rows, columns = own_rows_ref.shape

    def put(start, ref):
        for column in range(columns // LANE):
            rows_ref[start : start + rows, :] = ref[:, column * LANE : (column + 1) * LANE]
            start += rows

    for own in range(2):

        @pl.when(core == own)
        def _():
            put(own * rows * columns // LANE, own_rows_ref)
            put((1 - own) * rows * columns // LANE, other_rows_ref)

    used = 2 * rows * columns // LANE
    rows_ref[used:, :] = jnp.zeros((rows_ref.shape[0] - used, LANE), jnp.float32)

    @pl.when(is_middle())
    def _():
        outer_ref[...] = rows_ref[...]

    @pl.when(jnp.logical_not(is_middle()))
    def _():
        outer_ref[...] = chip_ref[...]


def inverse_kernel(scale, order, *refs):
    *sums, rows_ref, a_ref, b_ref, direct_ref, rest_ref, factor_ref = refs
    split = part_rows(order)[0]

    def piece(start, size):
        total = sums[0][start : start + size, :]
        for ref in sums[1:]:
            total = total + ref[start : start + size, :]
        return total

    unpack(piece, lambda start, size: piece(split + start, size), order, factor_ref, 0, scale, DAMPING)
    factor = factor_ref[...]
    bound = jnp.max(jnp.sum(jnp.abs(factor), axis=0, keepdims=True), axis=1, keepdims=True) + 1e-06
    start = START / bound
    rows = lax.broadcasted_iota(jnp.int32, (order, order), 0)
    cols = lax.broadcasted_iota(jnp.int32, (order, order), 1)
    eye = jnp.where(rows == cols, 1.0, 0.0)
    total = eye - start * factor
    power_halves = halves(total)
    middle = order // 2
    for step in range(1, ITERS):
        power = whole(*upper_square(power_halves))
        power_halves = halves(power)
        top, corner = upper_times(halves(total), power_halves)
        known = total + power
        top, corner = top + known[:middle], corner + known[middle:, middle:]
        if step < ITERS - 1:
            total = whole(top, corner)

    def block(i, j):
        if i < middle // LANE:
            value = block_of(top)(i, j)
        else:
            value = block_of(corner)(i - middle // LANE, j - middle // LANE)
        return start * (value + block_of(eye)(i, j))

    used = direct_ref.shape[0] - split

    @pl.when(is_middle())
    def _():
        pack(block, order, a_ref, b_ref, lax.rem(lax.axis_index("cuts"), 2))
        direct_ref[:split, :] = a_ref[...]
        direct_ref[split:, :] = b_ref[:used, :]
        rest_ref[...] = b_ref[used:, :]

    @pl.when(jnp.logical_not(is_middle()))
    def _():
        a_ref[...] = rows_ref[:split, :]
        b_ref[...] = rows_ref[split:, :]
        direct_ref[...] = rows_ref[: split + used, :]
        rest_ref[...] = rows_ref[:used, :]


def relay_kernel(hopped_ref, rest_ref, out_ref):
    used = rest_ref.shape[0]
    out_ref[:used, :] = hopped_ref[:used, :]
    rest = jnp.logical_and(is_middle(), lax.axis_index("grad") == 1)

    @pl.when(rest)
    def _():
        out_ref[used:, :] = rest_ref[...]

    @pl.when(jnp.logical_not(rest))
    def _():
        out_ref[used:, :] = hopped_ref[used:, :]


def choose_kernel(which, start, *refs):
    *arrays, out_ref = refs
    index = which()
    rows = out_ref.shape[0]
    for place, ref in enumerate(arrays):
        first = start if place == len(arrays) - 1 else 0
        size = min(rows, ref.shape[0] - first)

        @pl.when(index == place)
        def _():
            out_ref[:size, :] = ref[first : first + size, :]
            if size < rows:
                out_ref[size:, :] = jnp.zeros((rows - size, LANE), jnp.float32)


def fill_left(order, mine, a_ref, b_ref, left_ref):
    second = lax.rem(lax.div(lax.axis_index("dp"), 2), 2)
    for row in range(order // LANE):

        @pl.when(mine == row)
        def _():
            for column in range(order // LANE):
                block = stored_block(a_ref, b_ref, order, row, column, second)
                left_ref[:, column * LANE : (column + 1) * LANE] = block


def fill_right(order, a_ref, b_ref, left_b_ref, joined_ref, right_ref):
    cut = lax.axis_index("cuts")
    zq = lax.rem(lax.axis_index("dp"), QUAD)
    was_direct = jnp.logical_and(jnp.logical_not(is_middle()), (zq ^ 1) == 2 - lax.rem(cut, 2))
    used = joined_ref.shape[0] // 2
    joined_ref[...] = b_ref[...]

    @pl.when(was_direct)
    def _():
        joined_ref[used:, :] = left_b_ref[used:, :]

    unpack(
        lambda start, size: a_ref[pl.ds(start, size), :],
        lambda start, size: joined_ref[pl.ds(start, size), :],
        order,
        right_ref,
        lax.rem(cut, 2),
    )


def place_of_rows(spread):
    core = lax.axis_index("grad")
    return core, lax.rem(lax.axis_index("dp") * lax.axis_size("grad") + core, spread)


def first_kernel(order, spread, own_a, own_b, other_b, *refs):
    own_rows_ref, other_rows_ref, outer_ref, outer_other_ref, direct_ref, relayed_a, relayed_b, relayed_other, *refs = refs
    left_out, right_out, left_ref, right_ref, tile_ref, joined_ref = refs
    core, mine = place_of_rows(spread)
    rows_dev = own_rows_ref.shape[0]

    def place(position):
        return pl.ds(pl.multiple_of(position * rows_dev, rows_dev), rows_dev)

    tile_ref[place(mine), :] = own_rows_ref[...]
    tile_ref[place(mine ^ 1), :] = other_rows_ref[...]
    here = core == rows_core()
    cases = (
        (False, True, (outer_ref,)),
        (False, False, (outer_other_ref,)),
        (True, True, (direct_ref.at[: relayed_a.shape[0]], relayed_other)),
        (True, False, (relayed_a, relayed_b)),
    )
    for middle, arrived, parts in cases:

        @pl.when(jnp.logical_and(is_middle() == middle, here == arrived))
        def _():
            start, part = 0, 0
            for turn in range(2):
                for column in range(order // LANE):
                    if start == parts[part].shape[0]:
                        start, part = 0, part + 1
                    tile_ref[place((mine // 2 ^ 1) * 2 + turn), column * LANE : (column + 1) * LANE] = parts[part][
                        start : start + rows_dev, :
                    ]
                    start += rows_dev

    @pl.when(core != 0)
    def _():
        fill_left(order, mine, own_a, own_b, left_ref)
        left_out[...] = times(halves(left_ref[...]), halves(tile_ref[...]))

    @pl.when(core == 0)
    def _():
        fill_right(order, own_a, own_b, other_b, joined_ref, right_ref)
        right_out[...] = times(halves(tile_ref[...]), halves(right_ref[...]))


def last_kernel(order, spread, own_b, other_a, other_b, first_left, first_right, out_ref, *refs):
    left_ref, right_ref, joined_ref, result_ref, sems = refs
    core, mine = place_of_rows(spread)
    step = order // 2

    def finish(left, right_ref):
        copies = []
        for turn in range(2):
            columns = pl.ds(turn * step, step)
            result_ref[turn] = times(left, halves(right_ref[:, turn * step : (turn + 1) * step]))
            copies.append(pltpu.make_async_copy(result_ref.at[turn], out_ref.at[:, columns], sems.at[turn]))
            copies[-1].start()
        for copy in copies:
            copy.wait()

    @pl.when(core != 0)
    def _():
        fill_right(order, other_a, other_b, own_b, joined_ref, right_ref)
        finish(halves(first_left[...]), right_ref)

    @pl.when(core == 0)
    def _():
        fill_left(order, mine, other_a, other_b, left_ref)
        finish(halves(left_ref[...]), first_right)


def call(kernel, shapes, scratch, *args, space=pltpu.VMEM):
    return pl.pallas_call(
        kernel,
        out_shape=[jax.ShapeDtypeStruct(shape, jnp.float32) for shape in shapes],
        out_specs=[pl.BlockSpec(memory_space=space) for shape in shapes],
        scratch_shapes=scratch,
        compiler_params=PARAMS,
    )(*args)


class Plan:
    def __init__(self, groups, dp, cuts):
        self.groups, self.dp, self.cuts = groups, dp, cuts
        self.bases = range(0, dp, QUAD)

    def index(self, z, x, core):
        return (z * self.cuts + x % self.cuts) * 2 + core

    def roots(self, base, x):
        return base + 1 + x % 2, base + 2 - x % 2

    def one_way(self, pairs):
        pairs = list(pairs)
        size = self.dp * self.cuts * 2
        return [(group * size + a, group * size + b) for group in range(self.groups) for a, b in pairs]

    def swaps(self, pairs, abreast=False):
        size = self.dp * self.cuts * 2
        partner = {}
        for a, b in self.one_way(pairs):
            partner[a], partner[b] = b, a

        def pair_up(other):
            for device in range(size * self.groups):
                chosen = other(device)
                if device not in partner and chosen not in partner and chosen < size * self.groups:
                    partner[device], partner[chosen] = chosen, device

        pair_up(lambda device: device ^ 1)
        if abreast and self.cuts % 2 == 0:
            pair_up(lambda device: device ^ 3)
        pair_up(lambda device: (device + size) % (2 * size) + device // (2 * size) * 2 * size)
        return sorted(partner.items())

    def across(self, bit):
        return self.one_way(
            (self.index(z, x, core), self.index(z ^ bit, x, core))
            for z in range(self.dp)
            for x in range(self.cuts)
            for core in range(2)
        )

    def collect(self):
        far, near, outer = [], [], []
        for x in range(self.cuts):
            for base in self.bases:
                left, right = self.roots(base, x)
                left_root, right_root = self.index(left, x, 1), self.index(right, x, 0)
                far.append((self.index(right ^ 1, x, 0), left_root))
                far.append((self.index(left ^ 1, x, 1), right_root))
                near.append((self.index(right, x, 0), left_root))
                outer.append((self.index(left ^ 1, x, 0), left_root))
                outer.append((self.index(right ^ 1, x, 1), right_root))
        return self.one_way(far), self.swaps(near), self.swaps(outer)

    def spread(self):
        hops = [[] for turn in range(1, self.cuts)]
        direct = []
        relays = [[] for turn in range(1, self.cuts)]
        for x in range(self.cuts):
            for base in self.bases:
                left, right = self.roots(base, x)
                right_root, middle = self.index(right, x, 0), self.index(left, x, 0)
                hops[0].append((right_root, middle))
                left_root = self.index(left, x, 1)
                direct.append((right_root, self.index(right ^ 1, x, 0)))
                direct.append((left_root, self.index(left ^ 1, x, 1)))
                relays[0].append((middle, self.index(left ^ 1, x, 0)))
                if x // 2 != base // QUAD:
                    continue
                for turn in range(1, self.cuts):
                    abreast = self.index(left, x + turn, 1)
                    hops[turn - 1].append((left_root, abreast))
                    relays[turn - 1].append((abreast, self.index(left ^ 1, x + turn, 1)))
        return [self.swaps(pairs) for pairs in hops], self.swaps(direct), [self.swaps(pairs, True) for pairs in relays]

    def turn(self):
        z, x, core = (lax.axis_index(name) for name in AXES[1:])
        turn = lax.rem(x + self.cuts - lax.div(z, 2), self.cuts)
        return jnp.where(core == 1, jnp.maximum(turn - 1, 0), 0)

    def which(self):
        z, x, core = (lax.axis_index(name) for name in AXES[1:])
        zq, middle = lax.rem(z, QUAD), is_middle()
        block = lax.div(z, 2)
        turn = lax.rem(x + self.cuts - block, self.cuts)
        direct = 2 * self.cuts - 1
        left = jnp.where(middle, turn, jnp.where(turn == 0, direct, self.cuts - 1 + turn))
        right_root = 2 - lax.rem(x, 2)
        right = jnp.where(
            zq == right_root, 0, jnp.where(middle, 1, jnp.where((zq ^ 1) == right_root, direct, self.cuts))
        )
        return jnp.where(core == 1, left, right)


def is_middle():
    zq = lax.rem(lax.axis_index("dp"), QUAD)
    return jnp.logical_or(zq == 1, zq == 2)


def rows_core():
    zq = lax.rem(lax.axis_index("dp"), QUAD)
    left = 1 + lax.rem(lax.axis_index("cuts"), 2)
    return jnp.where(is_middle(), zq == left, (zq ^ 1) != left).astype(jnp.int32)


def swap_cores(array):
    return lax.ppermute(array, "grad", [(0, 1), (1, 0)])


def per_device(acts, outgrads, grads):
    groups, dp, cuts, cores = (lax.axis_size(name) for name in AXES)
    tok_rows, order = acts.shape[1:]
    dev_count = dp * cores
    spread = dev_count // cuts
    plan = Plan(groups, dp, cuts)
    split, rest = part_rows(order)
    shape = (split + rest, LANE)
    acts, outgrads, grads = acts[0], outgrads[0], grads[0]

    core = lax.axis_index("grad")
    (sent,) = call(cov_kernel, [shape], [], jnp.where(core == 0, outgrads, acts))
    (kept,) = call(cov_kernel, [shape], [], jnp.where(core == 0, acts, outgrads))
    other_rows = swap_cores(grads)
    chip, rows, outer = call(chip_kernel, [shape] * 3, [], kept, swap_cores(sent), grads, other_rows)
    bit = QUAD
    while bit < dp:
        chip = chip + lax.ppermute(chip, AXES, plan.across(bit))
        outer = jnp.where(is_middle(), outer, chip)
        bit *= 2
    far, near, outward = plan.collect()
    sums = [
        lax.ppermute(outer, AXES, outward),
        lax.ppermute(chip, AXES, near),
        lax.ppermute(chip, AXES, far),
        swap_cores(chip),
    ]
    outer_rows = sums[0]
    scale = 1.0 / (tok_rows * dev_count)
    square_scratch = pltpu.VMEM((order, order), jnp.float32)
    *inverse, direct, rest_own = call(
        functools.partial(inverse_kernel, scale, order),
        [(split, LANE), (rest, LANE), (split + rest // 2, LANE), (rest // 2, LANE)],
        [square_scratch],
        *sums,
        rows,
    )

    hops, outward, relays = plan.spread()
    hopped = [[lax.ppermute(inverse[0], AXES, pairs) for pairs in hops]]
    direct = lax.ppermute(direct, AXES, outward)
    hopped.append([lax.ppermute(inverse[1], AXES, pairs) for pairs in hops])
    rest_own = swap_cores(rest_own)
    carried = [
        hopped[0],
        [call(relay_kernel, [array.shape], [], array, rest_own)[0] for array in hopped[1]],
    ]
    relayed = [[lax.ppermute(array, AXES, pairs) for array, pairs in zip(arrays, relays)] for arrays in carried]
    relayed[1], direct = lax.optimization_barrier((relayed[1], direct))
    arrived = [
        arrays[0] if cuts == 2 else call(functools.partial(choose_kernel, plan.turn, 0), [arrays[0].shape], [], *arrays)[0]
        for arrays in relayed
    ]
    own = []
    for part, start in ((0, 0), (1, split)):
        own += call(
            functools.partial(choose_kernel, plan.which, start),
            [inverse[part].shape],
            [],
            inverse[part],
            *hopped[part],
            *relayed[part],
            direct,
        )
    other_a, other_b = map(swap_cores, own)
    left_scratch = pltpu.VMEM((LANE, order), jnp.float32)
    joined_scratch = pltpu.VMEM((rest, LANE), jnp.float32)
    first = call(
        functools.partial(first_kernel, order, spread),
        [(LANE, order), (order, order)],
        [left_scratch, square_scratch, square_scratch, joined_scratch],
        *own,
        other_b,
        grads,
        other_rows,
        outer_rows,
        swap_cores(outer_rows),
        direct,
        *arrived,
        swap_cores(arrived[1]),
    )
    (out,) = call(
        functools.partial(last_kernel, order, spread),
        [grads.shape],
        [
            left_scratch,
            square_scratch,
            joined_scratch,
            pltpu.VMEM((2, LANE, order // 2), jnp.float32),
            pltpu.SemaphoreType.DMA((2,)),
        ],
        own[1],
        other_a,
        other_b,
        *first,
        space=pl.ANY,
    )
    return out[None]


def solution(mesh):
    in_specs = (
        P(None, ("groups", "dp", "grad"), "cuts"),
        P(None, ("groups", "dp", "grad"), "cuts"),
        P("groups", ("dp", "grad"), "cuts"),
    )
    out_specs = P("groups", ("dp", "grad"), "cuts")
    return jax.shard_map(
        per_device, mesh=mesh, in_specs=in_specs, out_specs=out_specs, check_vma=False
    )
```

```python
import functools
import jax
import jax.numpy as jnp
from jax import lax
from jax.experimental import pallas as pl
from jax.experimental.pallas import tpu as pltpu
from jax.sharding import PartitionSpec as P

ITERS = 4
DAMPING = 0.5
START = 1.9
LANE = 128
QUAD = 4
AXES = ("groups", "dp", "cuts", "grad")
PARAMS = pltpu.CompilerParams(vmem_limit_bytes=48 * 1024 * 1024)


def half_blocks(order, half):
    count = order // LANE // 2
    own = range(half * count, (half + 1) * count)
    return [(i, j) for i in own for j in own if i < j], [(i, i + 1) for i in own[::2]]


def joining_blocks(order):
    count = order // LANE
    return [(i, j) for i in range(count // 2) for j in range(count // 2, count)]


def part_rows(order):
    above, pairs = half_blocks(order, 0)
    own = (len(above) + len(pairs)) * LANE + -(-len(pairs) // 8) * 8
    return len(joining_blocks(order)) * LANE, 2 * own


def own_start(order, half, second):
    rows = part_rows(order)[1] // 2
    return (half ^ second) * rows if isinstance(second, int) else pl.multiple_of((half ^ second) * rows, 8)


def places():
    rows = lax.broadcasted_iota(jnp.int32, (LANE, LANE), 0)
    cols = lax.broadcasted_iota(jnp.int32, (LANE, LANE), 1)
    return rows, cols


def pack(block, order, a_ref, b_ref, second=0):
    rows, cols = places()
    for slot, (i, j) in enumerate(joining_blocks(order)):
        a_ref[slot * LANE : (slot + 1) * LANE, :] = block(i, j)
    for half in range(2):
        top = own_start(order, half, second)
        above, pairs = half_blocks(order, half)
        values = [block(i, j) for i, j in above]
        values += [jnp.where(rows <= cols, block(i, i), block(j, j)) for i, j in pairs]
        last = [jnp.sum(jnp.where(rows == cols, block(j, j), 0.0), axis=0, keepdims=True) for _, j in pairs]
        values.append(jnp.concatenate(last + [jnp.zeros((-len(pairs) % 8, LANE), jnp.float32)], 0))
        for value in values:
            b_ref[pl.ds(top, value.shape[0]), :] = value
            top += value.shape[0]


def unpack(a_piece, b_piece, order, out_ref, second=0, scale=1.0, shift=0.0):
    rows, cols = places()
    damping = jnp.where(rows == cols, shift, 0.0)

    def put(i, j, value):
        out_ref[i * LANE : (i + 1) * LANE, j * LANE : (j + 1) * LANE] = value

    def put_both(i, j, value):
        put(i, j, value)
        put(j, i, value.T)

    for slot, (i, j) in enumerate(joining_blocks(order)):
        put_both(i, j, a_piece(slot * LANE, LANE) * scale)
    for half in range(2):
        top = own_start(order, half, second)
        above, pairs = half_blocks(order, half)
        for i, j in above:
            put_both(i, j, b_piece(top, LANE) * scale)
            top += LANE
        last = b_piece(top + len(pairs) * LANE, -(-len(pairs) // 8) * 8)
        for k, (i, j) in enumerate(pairs):
            both = b_piece(top, LANE)
            turned = both.T
            put(i, i, jnp.where(rows <= cols, both, turned) * scale + damping)
            after = jnp.where(rows > cols, both, jnp.where(rows < cols, turned, last[k : k + 1, :]))
            put(j, j, after * scale + damping)
            top += LANE


def stored_block(a_ref, b_ref, order, i, j, second):
    if i > j:
        return stored_block(a_ref, b_ref, order, j, i, second).T
    if (i, j) in joining_blocks(order):
        start = joining_blocks(order).index((i, j)) * LANE
        return a_ref[start : start + LANE, :]
    half = i // (order // LANE // 2)
    above, pairs = half_blocks(order, half)
    top = own_start(order, half, second)
    if i < j:
        return b_ref[pl.ds(top + above.index((i, j)) * LANE, LANE), :]
    place = next(k for k, pair in enumerate(pairs) if i in pair)
    both = b_ref[pl.ds(top + (len(above) + place) * LANE, LANE), :]
    rows, cols = places()
    if i == pairs[place][0]:
        return jnp.where(rows <= cols, both, both.T)
    last = b_ref[pl.ds(top + (len(above) + len(pairs)) * LANE, -(-len(pairs) // 8) * 8), :]
    return jnp.where(rows > cols, both, jnp.where(rows < cols, both.T, last[place : place + 1, :]))


def halves(value):
    high = value.astype(jnp.bfloat16)
    return high, (value - high.astype(jnp.float32)).astype(jnp.bfloat16)


def times(left, right):
    dot = functools.partial(jnp.dot, preferred_element_type=jnp.float32)
    rows = left[0].shape[0]
    both = dot(jnp.concatenate(left, 0), right[0])
    return both[:rows] + (dot(left[0], right[1]) + both[rows:])


def rows_of(pair, start, stop):
    return pair[0][start:stop, :], pair[1][start:stop, :]


def upper_times(left, right):
    middle = left[0].shape[0] // 2
    top = times(rows_of(left, 0, middle), right)
    corner = times(rows_of(left, middle, 2 * middle), (right[0][:, middle:], right[1][:, middle:]))
    return top, corner


def upper_square(value):
    dot = functools.partial(jnp.dot, preferred_element_type=jnp.float32)
    high, low = value
    middle = high.shape[0] // 2
    mixed = dot(high, low)
    top = dot(high[:middle], high) + (mixed[:middle] + mixed[:, :middle].T)
    corner = mixed[middle:, middle:]
    return top, dot(high[middle:], high[:, middle:]) + (corner + corner.T)


def whole(top, corner):
    middle = corner.shape[0]
    return jnp.concatenate([top, jnp.concatenate([top[:, middle:].T, corner], 1)], 0)


def cov_kernel(x_ref, out_ref):
    x = x_ref[...]
    order = x.shape[1]
    split = part_rows(order)[0]
    total = lax.dot_general(x, x, (((0,), (0,)), ((), ())), preferred_element_type=jnp.float32)
    pack(block_of(total), order, out_ref.at[:split], out_ref.at[split:])


def block_of(value):
    return lambda i, j: value[i * LANE : (i + 1) * LANE, j * LANE : (j + 1) * LANE]


def chip_kernel(kept_ref, other_ref, own_rows_ref, other_rows_ref, chip_ref, rows_ref, outer_ref):
    chip_ref[...] = kept_ref[...] + other_ref[...]
    core = lax.axis_index("grad")
    rows, columns = own_rows_ref.shape

    def put(start, ref):
        for column in range(columns // LANE):
            rows_ref[start : start + rows, :] = ref[:, column * LANE : (column + 1) * LANE]
            start += rows

    for own in range(2):

        @pl.when(core == own)
        def _():
            put(own * rows * columns // LANE, own_rows_ref)
            put((1 - own) * rows * columns // LANE, other_rows_ref)

    used = 2 * rows * columns // LANE
    rows_ref[used:, :] = jnp.zeros((rows_ref.shape[0] - used, LANE), jnp.float32)

    @pl.when(is_middle())
    def _():
        outer_ref[...] = rows_ref[...]

    @pl.when(jnp.logical_not(is_middle()))
    def _():
        outer_ref[...] = chip_ref[...]


def inverse_kernel(scale, order, *refs):
    *sums, rows_ref, a_ref, b_ref, direct_ref, rest_ref, factor_ref = refs
    split = part_rows(order)[0]

    def piece(start, size):
        total = sums[0][start : start + size, :]
        for ref in sums[1:]:
            total = total + ref[start : start + size, :]
        return total

    unpack(piece, lambda start, size: piece(split + start, size), order, factor_ref, 0, scale, DAMPING)
    factor = factor_ref[...]
    bound = jnp.max(jnp.sum(jnp.abs(factor), axis=0, keepdims=True), axis=1, keepdims=True) + 1e-06
    start = START / bound
    rows = lax.broadcasted_iota(jnp.int32, (order, order), 0)
    cols = lax.broadcasted_iota(jnp.int32, (order, order), 1)
    eye = jnp.where(rows == cols, 1.0, 0.0)
    total = eye - start * factor
    power_halves = halves(total)
    middle = order // 2
    for step in range(1, ITERS):
        power = whole(*upper_square(power_halves))
        power_halves = halves(power)
        top, corner = upper_times(halves(total), power_halves)
        known = total + power
        top, corner = top + known[:middle], corner + known[middle:, middle:]
        if step < ITERS - 1:
            total = whole(top, corner)

    def block(i, j):
        if i < middle // LANE:
            value = block_of(top)(i, j)
        else:
            value = block_of(corner)(i - middle // LANE, j - middle // LANE)
        return start * (value + block_of(eye)(i, j))

    used = direct_ref.shape[0] - split

    @pl.when(is_middle())
    def _():
        pack(block, order, a_ref, b_ref, lax.rem(lax.axis_index("cuts"), 2))
        direct_ref[:split, :] = a_ref[...]
        direct_ref[split:, :] = b_ref[:used, :]
        rest_ref[...] = b_ref[used:, :]

    @pl.when(jnp.logical_not(is_middle()))
    def _():
        a_ref[...] = rows_ref[:split, :]
        b_ref[...] = rows_ref[split:, :]
        direct_ref[...] = rows_ref[: split + used, :]
        rest_ref[...] = rows_ref[:used, :]


def relay_kernel(hopped_ref, rest_ref, out_ref):
    used = rest_ref.shape[0]
    out_ref[:used, :] = hopped_ref[:used, :]
    rest = jnp.logical_and(is_middle(), lax.axis_index("grad") == 1)

    @pl.when(rest)
    def _():
        out_ref[used:, :] = rest_ref[...]

    @pl.when(jnp.logical_not(rest))
    def _():
        out_ref[used:, :] = hopped_ref[used:, :]


def choose_kernel(which, start, *refs):
    *arrays, out_ref = refs
    index = which()
    rows = out_ref.shape[0]
    for place, ref in enumerate(arrays):
        first = start if place == len(arrays) - 1 else 0
        size = min(rows, ref.shape[0] - first)

        @pl.when(index == place)
        def _():
            out_ref[:size, :] = ref[first : first + size, :]
            if size < rows:
                out_ref[size:, :] = jnp.zeros((rows - size, LANE), jnp.float32)


def fill_left(order, mine, a_ref, b_ref, left_ref):
    second = lax.rem(lax.div(lax.axis_index("dp"), 2), 2)
    for row in range(order // LANE):

        @pl.when(mine == row)
        def _():
            for column in range(order // LANE):
                block = stored_block(a_ref, b_ref, order, row, column, second)
                left_ref[:, column * LANE : (column + 1) * LANE] = block


def fill_right(order, a_ref, b_ref, left_b_ref, joined_ref, right_ref):
    cut = lax.axis_index("cuts")
    zq = lax.rem(lax.axis_index("dp"), QUAD)
    was_direct = jnp.logical_and(jnp.logical_not(is_middle()), (zq ^ 1) == 2 - lax.rem(cut, 2))
    used = joined_ref.shape[0] // 2
    joined_ref[...] = b_ref[...]

    @pl.when(was_direct)
    def _():
        joined_ref[used:, :] = left_b_ref[used:, :]

    unpack(
        lambda start, size: a_ref[pl.ds(start, size), :],
        lambda start, size: joined_ref[pl.ds(start, size), :],
        order,
        right_ref,
        lax.rem(cut, 2),
    )


def place_of_rows(spread):
    core = lax.axis_index("grad")
    return core, lax.rem(lax.axis_index("dp") * lax.axis_size("grad") + core, spread)


def first_kernel(order, spread, own_a, own_b, other_b, *refs):
    own_rows_ref, other_rows_ref, outer_ref, outer_other_ref, direct_ref, relayed_a, relayed_b, relayed_other, *refs = refs
    left_out, right_out, left_ref, right_ref, tile_ref, joined_ref = refs
    core, mine = place_of_rows(spread)
    rows_dev = own_rows_ref.shape[0]

    def place(position):
        return pl.ds(pl.multiple_of(position * rows_dev, rows_dev), rows_dev)

    tile_ref[place(mine), :] = own_rows_ref[...]
    tile_ref[place(mine ^ 1), :] = other_rows_ref[...]
    here = core == rows_core()
    cases = (
        (False, True, (outer_ref,)),
        (False, False, (outer_other_ref,)),
        (True, True, (direct_ref.at[: relayed_a.shape[0]], relayed_other)),
        (True, False, (relayed_a, relayed_b)),
    )
    for middle, arrived, parts in cases:

        @pl.when(jnp.logical_and(is_middle() == middle, here == arrived))
        def _():
            start, part = 0, 0
            for turn in range(2):
                for column in range(order // LANE):
                    if start == parts[part].shape[0]:
                        start, part = 0, part + 1
                    tile_ref[place((mine // 2 ^ 1) * 2 + turn), column * LANE : (column + 1) * LANE] = parts[part][
                        start : start + rows_dev, :
                    ]
                    start += rows_dev

    @pl.when(core != 0)
    def _():
        fill_left(order, mine, own_a, own_b, left_ref)
        left_out[...] = times(halves(left_ref[...]), halves(tile_ref[...]))

    @pl.when(core == 0)
    def _():
        fill_right(order, own_a, own_b, other_b, joined_ref, right_ref)
        right_out[...] = times(halves(tile_ref[...]), halves(right_ref[...]))


def last_kernel(order, spread, own_b, other_a, other_b, first_left, first_right, out_ref, *refs):
    left_ref, right_ref, joined_ref, result_ref, sems = refs
    core, mine = place_of_rows(spread)
    step = order // 2

    def finish(left, right_ref):
        copies = []
        for turn in range(2):
            columns = pl.ds(turn * step, step)
            result_ref[turn] = times(left, halves(right_ref[:, turn * step : (turn + 1) * step]))
            copies.append(pltpu.make_async_copy(result_ref.at[turn], out_ref.at[:, columns], sems.at[turn]))
            copies[-1].start()
        for copy in copies:
            copy.wait()

    @pl.when(core != 0)
    def _():
        fill_right(order, other_a, other_b, own_b, joined_ref, right_ref)
        finish(halves(first_left[...]), right_ref)

    @pl.when(core == 0)
    def _():
        fill_left(order, mine, other_a, other_b, left_ref)
        finish(halves(left_ref[...]), first_right)


def call(kernel, shapes, scratch, *args, space=pltpu.VMEM):
    return pl.pallas_call(
        kernel,
        out_shape=[jax.ShapeDtypeStruct(shape, jnp.float32) for shape in shapes],
        out_specs=[pl.BlockSpec(memory_space=space) for shape in shapes],
        scratch_shapes=scratch,
        compiler_params=PARAMS,
    )(*args)


class Plan:
    def __init__(self, groups, dp, cuts):
        self.groups, self.dp, self.cuts = groups, dp, cuts
        self.bases = range(0, dp, QUAD)

    def index(self, z, x, core):
        return (z * self.cuts + x % self.cuts) * 2 + core

    def roots(self, base, x):
        return base + 1 + x % 2, base + 2 - x % 2

    def one_way(self, pairs):
        pairs = list(pairs)
        size = self.dp * self.cuts * 2
        return [(group * size + a, group * size + b) for group in range(self.groups) for a, b in pairs]

    def whole(self, edges, abreast=False):
        size = self.dp * self.cuts * 2
        target = dict(self.one_way(edges))

        def pair_up(other):
            for device in range(size * self.groups):
                chosen = other(device)
                if device not in target and chosen not in target and chosen < size * self.groups:
                    target[device], target[chosen] = chosen, device

        pair_up(lambda device: device ^ 1)
        if abreast and self.cuts % 2 == 0:
            pair_up(lambda device: device ^ 3)
        pair_up(lambda device: (device + size) % (2 * size) + device // (2 * size) * 2 * size)
        return sorted(target.items())

    def swaps(self, pairs):
        return self.whole([edge for a, b in pairs for edge in ((a, b), (b, a))])

    def loops(self, pairs):
        edges = []
        for a, b in pairs:
            if (a ^ 1, b ^ 1) in pairs:
                edges += [(a, b), (b, a)]
            else:
                edges += [(a, b), (b, b ^ 1), (b ^ 1, a ^ 1), (a ^ 1, a)]
        return self.whole(edges)

    def across(self, bit):
        return self.one_way(
            (self.index(z, x, core), self.index(z ^ bit, x, core))
            for z in range(self.dp)
            for x in range(self.cuts)
            for core in range(2)
        )

    def collect(self):
        far, near, outer = [], [], []
        for x in range(self.cuts):
            for base in self.bases:
                left, right = self.roots(base, x)
                left_root, right_root = self.index(left, x, 1), self.index(right, x, 0)
                right_far, left_far = self.index(left ^ 1, x, 1), self.index(right ^ 1, x, 0)
                far += [(left_far, left_root), (left_root, right_far), (right_far, right_root), (right_root, left_far)]
                near.append((self.index(right, x, 0), left_root))
                outer.append((self.index(left ^ 1, x, 0), left_root))
                outer.append((self.index(right ^ 1, x, 1), right_root))
        return self.whole(far, True), self.swaps(near), self.loops(outer)

    def spread(self):
        hops = [[] for turn in range(1, self.cuts)]
        direct = []
        relays = [[] for turn in range(1, self.cuts)]
        for x in range(self.cuts):
            for base in self.bases:
                left, right = self.roots(base, x)
                right_root, middle = self.index(right, x, 0), self.index(left, x, 0)
                hops[0].append((right_root, middle))
                left_root = self.index(left, x, 1)
                direct.append((right_root, self.index(right ^ 1, x, 0)))
                direct.append((left_root, self.index(left ^ 1, x, 1)))
                relays[0].append((middle, self.index(left ^ 1, x, 0)))
                if x // 2 != base // QUAD:
                    continue
                for turn in range(1, self.cuts):
                    abreast = self.index(left, x + turn, 1)
                    hops[turn - 1].append((left_root, abreast))
                    relays[turn - 1].append((abreast, self.index(left ^ 1, x + turn, 1)))
        return [self.swaps(pairs) for pairs in hops], self.loops(direct), [self.loops(pairs) for pairs in relays]

    def turn(self):
        z, x, core = (lax.axis_index(name) for name in AXES[1:])
        turn = lax.rem(x + self.cuts - lax.div(z, 2), self.cuts)
        return jnp.where(lax.rem(z, QUAD) == 1 + lax.rem(x, 2), 0, jnp.maximum(turn - 1, 0))

    def which(self):
        z, x, core = (lax.axis_index(name) for name in AXES[1:])
        zq, middle = lax.rem(z, QUAD), is_middle()
        block = lax.div(z, 2)
        turn = lax.rem(x + self.cuts - block, self.cuts)
        direct = 2 * self.cuts - 1
        left = jnp.where(middle, turn, jnp.where(turn == 0, direct, self.cuts - 1 + turn))
        right_root = 2 - lax.rem(x, 2)
        right = jnp.where(
            zq == right_root, 0, jnp.where(middle, 1, jnp.where((zq ^ 1) == right_root, direct, self.cuts))
        )
        return jnp.where(core == 1, left, right)


def is_middle():
    zq = lax.rem(lax.axis_index("dp"), QUAD)
    return jnp.logical_or(zq == 1, zq == 2)


def rows_core():
    zq = lax.rem(lax.axis_index("dp"), QUAD)
    left = 1 + lax.rem(lax.axis_index("cuts"), 2)
    return jnp.where(is_middle(), zq != left, (zq ^ 1) == left).astype(jnp.int32)


def swap_cores(array):
    return lax.ppermute(array, "grad", [(0, 1), (1, 0)])


def per_device(acts, outgrads, grads):
    groups, dp, cuts, cores = (lax.axis_size(name) for name in AXES)
    tok_rows, order = acts.shape[1:]
    dev_count = dp * cores
    spread = dev_count // cuts
    plan = Plan(groups, dp, cuts)
    split, rest = part_rows(order)
    shape = (split + rest, LANE)
    acts, outgrads, grads = acts[0], outgrads[0], grads[0]

    core = lax.axis_index("grad")
    (sent,) = call(cov_kernel, [shape], [], jnp.where(core == 0, outgrads, acts))
    (kept,) = call(cov_kernel, [shape], [], jnp.where(core == 0, acts, outgrads))
    other_rows = swap_cores(grads)
    chip, rows, outer = call(chip_kernel, [shape] * 3, [], kept, swap_cores(sent), grads, other_rows)
    bit = QUAD
    while bit < dp:
        chip = chip + lax.ppermute(chip, AXES, plan.across(bit))
        outer = jnp.where(is_middle(), outer, chip)
        bit *= 2
    far, near, outward = plan.collect()
    sums = [
        lax.ppermute(outer, AXES, outward),
        lax.ppermute(chip, AXES, near),
        lax.ppermute(chip, AXES, far),
        swap_cores(chip),
    ]
    outer_rows = sums[0]
    scale = 1.0 / (tok_rows * dev_count)
    square_scratch = pltpu.VMEM((order, order), jnp.float32)
    *inverse, direct, rest_own = call(
        functools.partial(inverse_kernel, scale, order),
        [(split, LANE), (rest, LANE), (split + rest // 2, LANE), (rest // 2, LANE)],
        [square_scratch],
        *sums,
        rows,
    )

    hops, outward, relays = plan.spread()
    hopped = [[lax.ppermute(inverse[0], AXES, pairs) for pairs in hops]]
    direct = lax.ppermute(direct, AXES, outward)
    hopped.append([lax.ppermute(inverse[1], AXES, pairs) for pairs in hops])
    rest_own = swap_cores(rest_own)
    carried = [
        hopped[0],
        [call(relay_kernel, [array.shape], [], array, rest_own)[0] for array in hopped[1]],
    ]
    relayed = [[lax.ppermute(array, AXES, pairs) for array, pairs in zip(arrays, relays)] for arrays in carried]
    relayed[1], direct = lax.optimization_barrier((relayed[1], direct))
    arrived = [
        arrays[0] if cuts == 2 else call(functools.partial(choose_kernel, plan.turn, 0), [arrays[0].shape], [], *arrays)[0]
        for arrays in relayed
    ]
    own = []
    for part, start in ((0, 0), (1, split)):
        own += call(
            functools.partial(choose_kernel, plan.which, start),
            [inverse[part].shape],
            [],
            inverse[part],
            *hopped[part],
            *relayed[part],
            direct,
        )
    other_a, other_b = map(swap_cores, own)
    left_scratch = pltpu.VMEM((LANE, order), jnp.float32)
    joined_scratch = pltpu.VMEM((rest, LANE), jnp.float32)
    first = call(
        functools.partial(first_kernel, order, spread),
        [(LANE, order), (order, order)],
        [left_scratch, square_scratch, square_scratch, joined_scratch],
        *own,
        other_b,
        grads,
        other_rows,
        outer_rows,
        swap_cores(outer_rows),
        direct,
        *arrived,
        swap_cores(arrived[1]),
    )
    (out,) = call(
        functools.partial(last_kernel, order, spread),
        [grads.shape],
        [
            left_scratch,
            square_scratch,
            joined_scratch,
            pltpu.VMEM((2, LANE, order // 2), jnp.float32),
            pltpu.SemaphoreType.DMA((2,)),
        ],
        own[1],
        other_a,
        other_b,
        *first,
        space=pl.ANY,
    )
    return out[None]


def solution(mesh):
    in_specs = (
        P(None, ("groups", "dp", "grad"), "cuts"),
        P(None, ("groups", "dp", "grad"), "cuts"),
        P("groups", ("dp", "grad"), "cuts"),
    )
    out_specs = P("groups", ("dp", "grad"), "cuts")
    return jax.shard_map(
        per_device, mesh=mesh, in_specs=in_specs, out_specs=out_specs, check_vma=False
    )
```

```python
import functools
import jax
import jax.numpy as jnp
from jax import lax
from jax.experimental import pallas as pl
from jax.experimental.pallas import tpu as pltpu
from jax.sharding import PartitionSpec as P

ITERS = 4
DAMPING = 0.5
START = 1.9
LANE = 128
QUAD = 4
AXES = ("groups", "dp", "cuts", "grad")
PARAMS = pltpu.CompilerParams(vmem_limit_bytes=48 * 1024 * 1024)


def half_blocks(order, half):
    count = order // LANE // 2
    own = range(half * count, (half + 1) * count)
    return [(i, j) for i in own for j in own if i < j], [(i, i + 1) for i in own[::2]]


def joining_blocks(order):
    count = order // LANE
    return [(i, j) for i in range(count // 2) for j in range(count // 2, count)]


def part_rows(order):
    above, pairs = half_blocks(order, 0)
    own = (len(above) + len(pairs)) * LANE + -(-len(pairs) // 8) * 8
    return len(joining_blocks(order)) * LANE, 2 * own


def own_start(order, half, second):
    rows = part_rows(order)[1] // 2
    return (half ^ second) * rows if isinstance(second, int) else pl.multiple_of((half ^ second) * rows, 8)


def places():
    rows = lax.broadcasted_iota(jnp.int32, (LANE, LANE), 0)
    cols = lax.broadcasted_iota(jnp.int32, (LANE, LANE), 1)
    return rows, cols


def pack(block, order, a_ref, b_ref, second=0):
    rows, cols = places()
    for slot, (i, j) in enumerate(joining_blocks(order)):
        a_ref[slot * LANE : (slot + 1) * LANE, :] = block(i, j)
    for half in range(2):
        top = own_start(order, half, second)
        above, pairs = half_blocks(order, half)
        values = [block(i, j) for i, j in above]
        values += [jnp.where(rows <= cols, block(i, i), block(j, j)) for i, j in pairs]
        last = [jnp.sum(jnp.where(rows == cols, block(j, j), 0.0), axis=0, keepdims=True) for _, j in pairs]
        values.append(jnp.concatenate(last + [jnp.zeros((-len(pairs) % 8, LANE), jnp.float32)], 0))
        for value in values:
            b_ref[pl.ds(top, value.shape[0]), :] = value
            top += value.shape[0]


def unpack(a_piece, b_piece, order, out_ref, second=0, scale=1.0, shift=0.0):
    rows, cols = places()
    damping = jnp.where(rows == cols, shift, 0.0)

    def put(i, j, value):
        out_ref[i * LANE : (i + 1) * LANE, j * LANE : (j + 1) * LANE] = value

    def put_both(i, j, value):
        put(i, j, value)
        put(j, i, value.T)

    for slot, (i, j) in enumerate(joining_blocks(order)):
        put_both(i, j, a_piece(slot * LANE, LANE) * scale)
    for half in range(2):
        top = own_start(order, half, second)
        above, pairs = half_blocks(order, half)
        for i, j in above:
            put_both(i, j, b_piece(top, LANE) * scale)
            top += LANE
        last = b_piece(top + len(pairs) * LANE, -(-len(pairs) // 8) * 8)
        for k, (i, j) in enumerate(pairs):
            both = b_piece(top, LANE)
            turned = both.T
            put(i, i, jnp.where(rows <= cols, both, turned) * scale + damping)
            after = jnp.where(rows > cols, both, jnp.where(rows < cols, turned, last[k : k + 1, :]))
            put(j, j, after * scale + damping)
            top += LANE


def stored_block(a_ref, b_ref, order, i, j, second):
    if i > j:
        return stored_block(a_ref, b_ref, order, j, i, second).T
    if (i, j) in joining_blocks(order):
        start = joining_blocks(order).index((i, j)) * LANE
        return a_ref[start : start + LANE, :]
    half = i // (order // LANE // 2)
    above, pairs = half_blocks(order, half)
    top = own_start(order, half, second)
    if i < j:
        return b_ref[pl.ds(top + above.index((i, j)) * LANE, LANE), :]
    place = next(k for k, pair in enumerate(pairs) if i in pair)
    both = b_ref[pl.ds(top + (len(above) + place) * LANE, LANE), :]
    rows, cols = places()
    if i == pairs[place][0]:
        return jnp.where(rows <= cols, both, both.T)
    last = b_ref[pl.ds(top + (len(above) + len(pairs)) * LANE, -(-len(pairs) // 8) * 8), :]
    return jnp.where(rows > cols, both, jnp.where(rows < cols, both.T, last[place : place + 1, :]))


def halves(value):
    high = value.astype(jnp.bfloat16)
    return high, (value - high.astype(jnp.float32)).astype(jnp.bfloat16)


def times(left, right):
    dot = functools.partial(jnp.dot, preferred_element_type=jnp.float32)
    rows = left[0].shape[0]
    both = dot(jnp.concatenate(left, 0), right[0])
    return both[:rows] + (dot(left[0], right[1]) + both[rows:])


def rows_of(pair, start, stop):
    return pair[0][start:stop, :], pair[1][start:stop, :]


def upper_times(left, right):
    middle = left[0].shape[0] // 2
    top = times(rows_of(left, 0, middle), right)
    corner = times(rows_of(left, middle, 2 * middle), (right[0][:, middle:], right[1][:, middle:]))
    return top, corner


def upper_square(value):
    dot = functools.partial(jnp.dot, preferred_element_type=jnp.float32)
    high, low = value
    middle = high.shape[0] // 2
    mixed = dot(high, low)
    top = dot(high[:middle], high) + (mixed[:middle] + mixed[:, :middle].T)
    corner = mixed[middle:, middle:]
    return top, dot(high[middle:], high[:, middle:]) + (corner + corner.T)


def whole(top, corner):
    middle = corner.shape[0]
    return jnp.concatenate([top, jnp.concatenate([top[:, middle:].T, corner], 1)], 0)


def cov_kernel(x_ref, out_ref):
    x = x_ref[...]
    order = x.shape[1]
    split = part_rows(order)[0]
    total = lax.dot_general(x, x, (((0,), (0,)), ((), ())), preferred_element_type=jnp.float32)
    pack(block_of(total), order, out_ref.at[:split], out_ref.at[split:])


def block_of(value):
    return lambda i, j: value[i * LANE : (i + 1) * LANE, j * LANE : (j + 1) * LANE]


def chip_kernel(kept_ref, other_ref, own_rows_ref, other_rows_ref, chip_ref, rows_ref, outer_ref):
    chip_ref[...] = kept_ref[...] + other_ref[...]
    core = lax.axis_index("grad")
    rows, columns = own_rows_ref.shape

    def put(start, ref):
        for column in range(columns // LANE):
            rows_ref[start : start + rows, :] = ref[:, column * LANE : (column + 1) * LANE]
            start += rows

    for own in range(2):

        @pl.when(core == own)
        def _():
            put(own * rows * columns // LANE, own_rows_ref)
            put((1 - own) * rows * columns // LANE, other_rows_ref)

    used = 2 * rows * columns // LANE
    rows_ref[used:, :] = jnp.zeros((rows_ref.shape[0] - used, LANE), jnp.float32)

    @pl.when(is_middle())
    def _():
        outer_ref[...] = rows_ref[...]

    @pl.when(jnp.logical_not(is_middle()))
    def _():
        outer_ref[...] = chip_ref[...]


def inverse_kernel(scale, order, *refs):
    *sums, rows_ref, a_ref, b_ref, direct_ref, rest_ref, factor_ref = refs
    split = part_rows(order)[0]

    def piece(start, size):
        total = sums[0][start : start + size, :]
        for ref in sums[1:]:
            total = total + ref[start : start + size, :]
        return total

    unpack(piece, lambda start, size: piece(split + start, size), order, factor_ref, 0, scale, DAMPING)
    factor = factor_ref[...]
    bound = jnp.max(jnp.sum(jnp.abs(factor), axis=0, keepdims=True), axis=1, keepdims=True) + 1e-06
    start = START / bound
    rows = lax.broadcasted_iota(jnp.int32, (order, order), 0)
    cols = lax.broadcasted_iota(jnp.int32, (order, order), 1)
    eye = jnp.where(rows == cols, 1.0, 0.0)
    total = eye - start * factor
    power_halves = halves(total)
    middle = order // 2
    for step in range(1, ITERS):
        power = whole(*upper_square(power_halves))
        power_halves = halves(power)
        top, corner = upper_times(halves(total), power_halves)
        known = total + power
        top, corner = top + known[:middle], corner + known[middle:, middle:]
        if step < ITERS - 1:
            total = whole(top, corner)

    def block(i, j):
        if i < middle // LANE:
            value = block_of(top)(i, j)
        else:
            value = block_of(corner)(i - middle // LANE, j - middle // LANE)
        return start * (value + block_of(eye)(i, j))

    used = direct_ref.shape[0] - split

    @pl.when(is_middle())
    def _():
        pack(block, order, a_ref, b_ref, lax.rem(lax.axis_index("cuts"), 2))
        direct_ref[:split, :] = a_ref[...]
        direct_ref[split:, :] = b_ref[:used, :]
        rest_ref[...] = b_ref[used:, :]

    @pl.when(jnp.logical_not(is_middle()))
    def _():
        a_ref[...] = rows_ref[:split, :]
        b_ref[...] = rows_ref[split:, :]
        direct_ref[...] = rows_ref[: split + used, :]
        rest_ref[...] = rows_ref[:used, :]


def relay_kernel(hopped_ref, rest_ref, out_ref):
    used = rest_ref.shape[0]
    out_ref[:used, :] = hopped_ref[:used, :]
    rest = jnp.logical_and(is_middle(), lax.axis_index("grad") == 1)

    @pl.when(rest)
    def _():
        out_ref[used:, :] = rest_ref[...]

    @pl.when(jnp.logical_not(rest))
    def _():
        out_ref[used:, :] = hopped_ref[used:, :]


def choose_kernel(which, start, *refs):
    *arrays, out_ref = refs
    index = which()
    rows = out_ref.shape[0]
    for place, ref in enumerate(arrays):
        first = start if place == len(arrays) - 1 else 0
        size = min(rows, ref.shape[0] - first)

        @pl.when(index == place)
        def _():
            out_ref[:size, :] = ref[first : first + size, :]
            if size < rows:
                out_ref[size:, :] = jnp.zeros((rows - size, LANE), jnp.float32)


def fill_left(order, mine, a_ref, b_ref, left_ref):
    second = lax.rem(lax.div(lax.axis_index("dp"), 2), 2)
    for row in range(order // LANE):

        @pl.when(mine == row)
        def _():
            for column in range(order // LANE):
                block = stored_block(a_ref, b_ref, order, row, column, second)
                left_ref[:, column * LANE : (column + 1) * LANE] = block


def fill_right(order, a_ref, b_ref, left_b_ref, joined_ref, right_ref):
    cut = lax.axis_index("cuts")
    zq = lax.rem(lax.axis_index("dp"), QUAD)
    was_direct = jnp.logical_and(jnp.logical_not(is_middle()), (zq ^ 1) == 2 - lax.rem(cut, 2))
    used = joined_ref.shape[0] // 2
    joined_ref[...] = b_ref[...]

    @pl.when(was_direct)
    def _():
        joined_ref[used:, :] = left_b_ref[used:, :]

    unpack(
        lambda start, size: a_ref[pl.ds(start, size), :],
        lambda start, size: joined_ref[pl.ds(start, size), :],
        order,
        right_ref,
        lax.rem(cut, 2),
    )


def place_of_rows(spread):
    core = lax.axis_index("grad")
    return core, lax.rem(lax.axis_index("dp") * lax.axis_size("grad") + core, spread)


def first_kernel(order, spread, own_a, own_b, other_b, *refs):
    own_rows_ref, other_rows_ref, outer_ref, outer_other_ref, direct_ref, relayed_a, relayed_b, relayed_other, *refs = refs
    left_out, right_out, left_ref, right_ref, tile_ref, joined_ref = refs
    core, mine = place_of_rows(spread)
    rows_dev = own_rows_ref.shape[0]

    def place(position):
        return pl.ds(pl.multiple_of(position * rows_dev, rows_dev), rows_dev)

    tile_ref[place(mine), :] = own_rows_ref[...]
    tile_ref[place(mine ^ 1), :] = other_rows_ref[...]
    here = core == rows_core()
    cases = (
        (False, True, (outer_ref,)),
        (False, False, (outer_other_ref,)),
        (True, True, (direct_ref.at[: relayed_a.shape[0]], relayed_other)),
        (True, False, (relayed_a, relayed_b)),
    )
    for middle, arrived, parts in cases:

        @pl.when(jnp.logical_and(is_middle() == middle, here == arrived))
        def _():
            start, part = 0, 0
            for turn in range(2):
                for column in range(order // LANE):
                    if start == parts[part].shape[0]:
                        start, part = 0, part + 1
                    tile_ref[place((mine // 2 ^ 1) * 2 + turn), column * LANE : (column + 1) * LANE] = parts[part][
                        start : start + rows_dev, :
                    ]
                    start += rows_dev

    @pl.when(core != 0)
    def _():
        fill_left(order, mine, own_a, own_b, left_ref)
        left_out[...] = times(halves(left_ref[...]), halves(tile_ref[...]))

    @pl.when(core == 0)
    def _():
        fill_right(order, own_a, own_b, other_b, joined_ref, right_ref)
        right_out[...] = times(halves(tile_ref[...]), halves(right_ref[...]))


def last_kernel(order, spread, own_b, other_a, other_b, first_left, first_right, out_ref, *refs):
    left_ref, right_ref, joined_ref, result_ref, sems = refs
    core, mine = place_of_rows(spread)
    step = order // 2

    def finish(left, right_ref):
        copies = []
        for turn in range(2):
            columns = pl.ds(turn * step, step)
            result_ref[turn] = times(left, halves(right_ref[:, turn * step : (turn + 1) * step]))
            copies.append(pltpu.make_async_copy(result_ref.at[turn], out_ref.at[:, columns], sems.at[turn]))
            copies[-1].start()
        for copy in copies:
            copy.wait()

    @pl.when(core != 0)
    def _():
        fill_right(order, other_a, other_b, own_b, joined_ref, right_ref)
        finish(halves(first_left[...]), right_ref)

    @pl.when(core == 0)
    def _():
        fill_left(order, mine, other_a, other_b, left_ref)
        finish(halves(left_ref[...]), first_right)


def call(kernel, shapes, scratch, *args, space=pltpu.VMEM):
    return pl.pallas_call(
        kernel,
        out_shape=[jax.ShapeDtypeStruct(shape, jnp.float32) for shape in shapes],
        out_specs=[pl.BlockSpec(memory_space=space) for shape in shapes],
        scratch_shapes=scratch,
        compiler_params=PARAMS,
    )(*args)


class Plan:
    def __init__(self, groups, dp, cuts):
        self.groups, self.dp, self.cuts = groups, dp, cuts
        self.bases = range(0, dp, QUAD)

    def index(self, z, x, core):
        return (z * self.cuts + x % self.cuts) * 2 + core

    def roots(self, base, x):
        return base + 1 + x % 2, base + 2 - x % 2

    def one_way(self, pairs):
        pairs = list(pairs)
        size = self.dp * self.cuts * 2
        return [(group * size + a, group * size + b) for group in range(self.groups) for a, b in pairs]

    def whole(self, edges, abreast=False):
        size = self.dp * self.cuts * 2
        target = dict(self.one_way(edges))

        def pair_up(other):
            for device in range(size * self.groups):
                chosen = other(device)
                if device not in target and chosen not in target and chosen < size * self.groups:
                    target[device], target[chosen] = chosen, device

        pair_up(lambda device: device ^ 1)
        if abreast and self.cuts % 2 == 0:
            pair_up(lambda device: device ^ 3)
        pair_up(lambda device: (device + size) % (2 * size) + device // (2 * size) * 2 * size)
        return sorted(target.items())

    def swaps(self, pairs):
        return self.whole([edge for a, b in pairs for edge in ((a, b), (b, a))])

    def chains(self, pairs):
        to, of = dict(pairs), {b: a for a, b in pairs}
        edges = list(pairs)
        for device in sorted(set(to) | set(of)):
            if device in of and device not in to:
                if device ^ 1 in of or device ^ 1 not in to:
                    return self.swaps(pairs)
                edges.append((device, device ^ 1))
            elif device in to and device not in of and (device ^ 1 in to or device ^ 1 not in of):
                return self.swaps(pairs)
        return self.whole(edges)

    def loops(self, pairs):
        edges = []
        for a, b in pairs:
            if (a ^ 1, b ^ 1) in pairs:
                edges += [(a, b), (b, a)]
            else:
                edges += [(a, b), (b, b ^ 1), (b ^ 1, a ^ 1), (a ^ 1, a)]
        return self.whole(edges)

    def across(self, bit):
        return self.one_way(
            (self.index(z, x, core), self.index(z ^ bit, x, core))
            for z in range(self.dp)
            for x in range(self.cuts)
            for core in range(2)
        )

    def collect(self):
        far, near, outer = [], [], []
        for x in range(self.cuts):
            for base in self.bases:
                left, right = self.roots(base, x)
                left_root, right_root = self.index(left, x, 1), self.index(right, x, 0)
                right_far, left_far = self.index(left ^ 1, x, 1), self.index(right ^ 1, x, 0)
                far += [(left_far, left_root), (left_root, right_far), (right_far, right_root), (right_root, left_far)]
                near.append((self.index(right, x, 0), left_root))
                outer.append((self.index(left ^ 1, x, 0), left_root))
                outer.append((self.index(right ^ 1, x, 1), right_root))
        return self.whole(far, True), self.swaps(near), self.loops(outer)

    def spread(self):
        hops = [[] for turn in range(1, self.cuts)]
        direct = []
        relays = [[] for turn in range(1, self.cuts)]
        for x in range(self.cuts):
            for base in self.bases:
                left, right = self.roots(base, x)
                right_root, middle = self.index(right, x, 0), self.index(left, x, 0)
                hops[0].append((right_root, middle))
                left_root = self.index(left, x, 1)
                direct.append((right_root, self.index(right ^ 1, x, 0)))
                direct.append((left_root, self.index(left ^ 1, x, 1)))
                relays[0].append((middle, self.index(left ^ 1, x, 0)))
                if x // 2 != base // QUAD:
                    continue
                for turn in range(1, self.cuts):
                    abreast = self.index(left, x + turn, 1)
                    hops[turn - 1].append((left_root, abreast))
                    relays[turn - 1].append((abreast, self.index(left ^ 1, x + turn, 1)))
        return [self.chains(pairs) for pairs in hops], self.loops(direct), [self.loops(pairs) for pairs in relays]

    def turn(self):
        z, x, core = (lax.axis_index(name) for name in AXES[1:])
        turn = lax.rem(x + self.cuts - lax.div(z, 2), self.cuts)
        return jnp.where(lax.rem(z, QUAD) == 1 + lax.rem(x, 2), 0, jnp.maximum(turn - 1, 0))

    def which(self):
        z, x, core = (lax.axis_index(name) for name in AXES[1:])
        zq, middle = lax.rem(z, QUAD), is_middle()
        block = lax.div(z, 2)
        turn = lax.rem(x + self.cuts - block, self.cuts)
        direct = 2 * self.cuts - 1
        left = jnp.where(middle, turn, jnp.where(turn == 0, direct, self.cuts - 1 + turn))
        right_root = 2 - lax.rem(x, 2)
        right = jnp.where(
            zq == right_root, 0, jnp.where(middle, 1, jnp.where((zq ^ 1) == right_root, direct, self.cuts))
        )
        return jnp.where(core == 1, left, right)


def is_middle():
    zq = lax.rem(lax.axis_index("dp"), QUAD)
    return jnp.logical_or(zq == 1, zq == 2)


def rows_core():
    zq = lax.rem(lax.axis_index("dp"), QUAD)
    left = 1 + lax.rem(lax.axis_index("cuts"), 2)
    return jnp.where(is_middle(), zq != left, (zq ^ 1) == left).astype(jnp.int32)


def swap_cores(array):
    return lax.ppermute(array, "grad", [(0, 1), (1, 0)])


def per_device(acts, outgrads, grads):
    groups, dp, cuts, cores = (lax.axis_size(name) for name in AXES)
    tok_rows, order = acts.shape[1:]
    dev_count = dp * cores
    spread = dev_count // cuts
    plan = Plan(groups, dp, cuts)
    split, rest = part_rows(order)
    shape = (split + rest, LANE)
    acts, outgrads, grads = acts[0], outgrads[0], grads[0]

    core = lax.axis_index("grad")
    (sent,) = call(cov_kernel, [shape], [], jnp.where(core == 0, outgrads, acts))
    (kept,) = call(cov_kernel, [shape], [], jnp.where(core == 0, acts, outgrads))
    other_rows = swap_cores(grads)
    chip, rows, outer = call(chip_kernel, [shape] * 3, [], kept, swap_cores(sent), grads, other_rows)
    bit = QUAD
    while bit < dp:
        chip = chip + lax.ppermute(chip, AXES, plan.across(bit))
        outer = jnp.where(is_middle(), outer, chip)
        bit *= 2
    far, near, outward = plan.collect()
    sums = [
        lax.ppermute(outer, AXES, outward),
        lax.ppermute(chip, AXES, near),
        lax.ppermute(chip, AXES, far),
        swap_cores(chip),
    ]
    outer_rows = sums[0]
    scale = 1.0 / (tok_rows * dev_count)
    square_scratch = pltpu.VMEM((order, order), jnp.float32)
    *inverse, direct, rest_own = call(
        functools.partial(inverse_kernel, scale, order),
        [(split, LANE), (rest, LANE), (split + rest // 2, LANE), (rest // 2, LANE)],
        [square_scratch],
        *sums,
        rows,
    )

    hops, outward, relays = plan.spread()
    hopped = [[lax.ppermute(inverse[0], AXES, pairs) for pairs in hops]]
    direct = lax.ppermute(direct, AXES, outward)
    hopped.append([lax.ppermute(inverse[1], AXES, pairs) for pairs in hops])
    rest_own = swap_cores(rest_own)
    carried = [
        hopped[0],
        [call(relay_kernel, [array.shape], [], array, rest_own)[0] for array in hopped[1]],
    ]
    relayed = [[lax.ppermute(array, AXES, pairs) for array, pairs in zip(arrays, relays)] for arrays in carried]
    relayed[1], direct = lax.optimization_barrier((relayed[1], direct))
    arrived = [
        arrays[0] if cuts == 2 else call(functools.partial(choose_kernel, plan.turn, 0), [arrays[0].shape], [], *arrays)[0]
        for arrays in relayed
    ]
    own = []
    for part, start in ((0, 0), (1, split)):
        own += call(
            functools.partial(choose_kernel, plan.which, start),
            [inverse[part].shape],
            [],
            inverse[part],
            *hopped[part],
            *relayed[part],
            direct,
        )
    other_a, other_b = map(swap_cores, own)
    left_scratch = pltpu.VMEM((LANE, order), jnp.float32)
    joined_scratch = pltpu.VMEM((rest, LANE), jnp.float32)
    first = call(
        functools.partial(first_kernel, order, spread),
        [(LANE, order), (order, order)],
        [left_scratch, square_scratch, square_scratch, joined_scratch],
        *own,
        other_b,
        grads,
        other_rows,
        outer_rows,
        swap_cores(outer_rows),
        direct,
        *arrived,
        swap_cores(arrived[1]),
    )
    (out,) = call(
        functools.partial(last_kernel, order, spread),
        [grads.shape],
        [
            left_scratch,
            square_scratch,
            joined_scratch,
            pltpu.VMEM((2, LANE, order // 2), jnp.float32),
            pltpu.SemaphoreType.DMA((2,)),
        ],
        own[1],
        other_a,
        other_b,
        *first,
        space=pl.ANY,
    )
    return out[None]


def solution(mesh):
    in_specs = (
        P(None, ("groups", "dp", "grad"), "cuts"),
        P(None, ("groups", "dp", "grad"), "cuts"),
        P("groups", ("dp", "grad"), "cuts"),
    )
    out_specs = P("groups", ("dp", "grad"), "cuts")
    return jax.shard_map(
        per_device, mesh=mesh, in_specs=in_specs, out_specs=out_specs, check_vma=False
    )
```

```python
import functools
import jax
import jax.numpy as jnp
from jax import lax
from jax.experimental import pallas as pl
from jax.experimental.pallas import tpu as pltpu
from jax.sharding import PartitionSpec as P

ITERS = 4
DAMPING = 0.5
START = 1.9
LANE = 128
QUAD = 4
AXES = ("groups", "dp", "cuts", "grad")
PARAMS = pltpu.CompilerParams(vmem_limit_bytes=48 * 1024 * 1024)


def half_blocks(order, half):
    count = order // LANE // 2
    own = range(half * count, (half + 1) * count)
    return [(i, j) for i in own for j in own if i < j], [(i, i + 1) for i in own[::2]]


def joining_blocks(order):
    count = order // LANE
    return [(i, j) for i in range(count // 2) for j in range(count // 2, count)]


def part_rows(order):
    above, pairs = half_blocks(order, 0)
    own = (len(above) + len(pairs)) * LANE + -(-len(pairs) // 8) * 8
    return len(joining_blocks(order)) * LANE, 2 * own


def own_start(order, half, second):
    rows = part_rows(order)[1] // 2
    return (half ^ second) * rows if isinstance(second, int) else pl.multiple_of((half ^ second) * rows, 8)


def places():
    rows = lax.broadcasted_iota(jnp.int32, (LANE, LANE), 0)
    cols = lax.broadcasted_iota(jnp.int32, (LANE, LANE), 1)
    return rows, cols


def pack(block, order, a_ref, b_ref, second=0):
    rows, cols = places()
    for slot, (i, j) in enumerate(joining_blocks(order)):
        a_ref[slot * LANE : (slot + 1) * LANE, :] = block(i, j)
    for half in range(2):
        top = own_start(order, half, second)
        above, pairs = half_blocks(order, half)
        values = [block(i, j) for i, j in above]
        values += [jnp.where(rows <= cols, block(i, i), block(j, j)) for i, j in pairs]
        last = [jnp.sum(jnp.where(rows == cols, block(j, j), 0.0), axis=0, keepdims=True) for _, j in pairs]
        values.append(jnp.concatenate(last + [jnp.zeros((-len(pairs) % 8, LANE), jnp.float32)], 0))
        for value in values:
            b_ref[pl.ds(top, value.shape[0]), :] = value
            top += value.shape[0]


def unpack(a_piece, b_piece, order, out_ref, second=0, scale=1.0, shift=0.0):
    rows, cols = places()
    damping = jnp.where(rows == cols, shift, 0.0)

    def put(i, j, value):
        out_ref[i * LANE : (i + 1) * LANE, j * LANE : (j + 1) * LANE] = value

    def put_both(i, j, value):
        put(i, j, value)
        put(j, i, value.T)

    for slot, (i, j) in enumerate(joining_blocks(order)):
        put_both(i, j, a_piece(slot * LANE, LANE) * scale)
    for half in range(2):
        top = own_start(order, half, second)
        above, pairs = half_blocks(order, half)
        for i, j in above:
            put_both(i, j, b_piece(top, LANE) * scale)
            top += LANE
        last = b_piece(top + len(pairs) * LANE, -(-len(pairs) // 8) * 8)
        for k, (i, j) in enumerate(pairs):
            both = b_piece(top, LANE)
            turned = both.T
            put(i, i, jnp.where(rows <= cols, both, turned) * scale + damping)
            after = jnp.where(rows > cols, both, jnp.where(rows < cols, turned, last[k : k + 1, :]))
            put(j, j, after * scale + damping)
            top += LANE


def stored_block(a_ref, b_ref, order, i, j, second):
    if i > j:
        return stored_block(a_ref, b_ref, order, j, i, second).T
    if (i, j) in joining_blocks(order):
        start = joining_blocks(order).index((i, j)) * LANE
        return a_ref[start : start + LANE, :]
    half = i // (order // LANE // 2)
    above, pairs = half_blocks(order, half)
    top = own_start(order, half, second)
    if i < j:
        return b_ref[pl.ds(top + above.index((i, j)) * LANE, LANE), :]
    place = next(k for k, pair in enumerate(pairs) if i in pair)
    both = b_ref[pl.ds(top + (len(above) + place) * LANE, LANE), :]
    rows, cols = places()
    if i == pairs[place][0]:
        return jnp.where(rows <= cols, both, both.T)
    last = b_ref[pl.ds(top + (len(above) + len(pairs)) * LANE, -(-len(pairs) // 8) * 8), :]
    return jnp.where(rows > cols, both, jnp.where(rows < cols, both.T, last[place : place + 1, :]))


def halves(value):
    high = value.astype(jnp.bfloat16)
    return high, (value - high.astype(jnp.float32)).astype(jnp.bfloat16)


def times(left, right):
    dot = functools.partial(jnp.dot, preferred_element_type=jnp.float32)
    rows = left[0].shape[0]
    both = dot(jnp.concatenate(left, 0), right[0])
    return both[:rows] + (dot(left[0], right[1]) + both[rows:])


def rows_of(pair, start, stop):
    return pair[0][start:stop, :], pair[1][start:stop, :]


def upper_times(left, right):
    middle = left[0].shape[0] // 2
    top = times(rows_of(left, 0, middle), right)
    corner = times(rows_of(left, middle, 2 * middle), (right[0][:, middle:], right[1][:, middle:]))
    return top, corner


def upper_square(value):
    dot = functools.partial(jnp.dot, preferred_element_type=jnp.float32)
    high, low = value
    middle = high.shape[0] // 2
    mixed = dot(high, low)
    top = dot(high[:middle], high) + (mixed[:middle] + mixed[:, :middle].T)
    corner = mixed[middle:, middle:]
    return top, dot(high[middle:], high[:, middle:]) + (corner + corner.T)


def whole(top, corner):
    middle = corner.shape[0]
    return jnp.concatenate([top, jnp.concatenate([top[:, middle:].T, corner], 1)], 0)


def cov_kernel(x_ref, out_ref):
    x = x_ref[...]
    order = x.shape[1]
    split = part_rows(order)[0]
    total = lax.dot_general(x, x, (((0,), (0,)), ((), ())), preferred_element_type=jnp.float32)
    pack(block_of(total), order, out_ref.at[:split], out_ref.at[split:])


def block_of(value):
    return lambda i, j: value[i * LANE : (i + 1) * LANE, j * LANE : (j + 1) * LANE]


def put_rows(out_ref, start, rows_ref):
    rows, columns = rows_ref.shape
    for column in range(columns // LANE):
        out_ref[start : start + rows, :] = rows_ref[:, column * LANE : (column + 1) * LANE]
        start += rows


def chip_kernel(kept_ref, other_ref, rows_ref, chip_ref, outer_ref):
    chip_ref[...] = kept_ref[...] + other_ref[...]

    @pl.when(is_middle())
    def _():
        used = rows_ref.shape[0] * rows_ref.shape[1] // LANE
        put_rows(outer_ref, 0, rows_ref)
        outer_ref[used:, :] = jnp.zeros((outer_ref.shape[0] - used, LANE), jnp.float32)

    @pl.when(jnp.logical_not(is_middle()))
    def _():
        outer_ref[...] = chip_ref[...]


def inverse_kernel(scale, order, *refs):
    *sums, own_rows_ref, other_rows_ref, a_ref, b_ref, direct_ref, rest_ref, gathered_ref, factor_ref, rows_ref = refs
    split = part_rows(order)[0]

    def piece(start, size):
        total = sums[0][start : start + size, :]
        for ref in sums[1:]:
            total = total + ref[start : start + size, :]
        return total

    unpack(piece, lambda start, size: piece(split + start, size), order, factor_ref, 0, scale, DAMPING)
    factor = factor_ref[...]
    bound = jnp.max(jnp.sum(jnp.abs(factor), axis=0, keepdims=True), axis=1, keepdims=True) + 1e-06
    start = START / bound
    rows = lax.broadcasted_iota(jnp.int32, (order, order), 0)
    cols = lax.broadcasted_iota(jnp.int32, (order, order), 1)
    eye = jnp.where(rows == cols, 1.0, 0.0)
    total = eye - start * factor
    power_halves = halves(total)
    middle = order // 2
    for step in range(1, ITERS):
        power = whole(*upper_square(power_halves))
        power_halves = halves(power)
        top, corner = upper_times(halves(total), power_halves)
        known = total + power
        top, corner = top + known[:middle], corner + known[middle:, middle:]
        if step < ITERS - 1:
            total = whole(top, corner)

    def block(i, j):
        if i < middle // LANE:
            value = block_of(top)(i, j)
        else:
            value = block_of(corner)(i - middle // LANE, j - middle // LANE)
        return start * (value + block_of(eye)(i, j))

    used = direct_ref.shape[0] - split

    @pl.when(is_middle())
    def _():
        pack(block, order, a_ref, b_ref, lax.rem(lax.axis_index("cuts"), 2))
        direct_ref[:split, :] = a_ref[...]
        direct_ref[split:, :] = b_ref[:used, :]
        rest_ref[...] = b_ref[used:, :]

    @pl.when(jnp.logical_not(is_middle()))
    def _():
        core = lax.axis_index("grad")
        size = own_rows_ref.shape[0] * own_rows_ref.shape[1] // LANE
        rows_ref[2 * size :, :] = jnp.zeros((rows_ref.shape[0] - 2 * size, LANE), jnp.float32)
        for mine in range(2):

            @pl.when(core == mine)
            def _():
                put_rows(rows_ref, mine * size, own_rows_ref)
                put_rows(rows_ref, (1 - mine) * size, other_rows_ref)

            @pl.when(rows_core() == mine)
            def _():
                outer, far = sums[0][:size, :], sums[2][:size, :]
                gathered_ref[:size, :] = outer if mine else far
                gathered_ref[size:, :] = far if mine else outer

        a_ref[...] = rows_ref[:split, :]
        b_ref[...] = rows_ref[split:, :]
        direct_ref[...] = rows_ref[: split + used, :]
        rest_ref[...] = rows_ref[:used, :]


def relay_kernel(hopped_ref, rest_ref, out_ref):
    used = rest_ref.shape[0]
    out_ref[:used, :] = hopped_ref[:used, :]
    rest = jnp.logical_and(is_middle(), lax.axis_index("grad") == 1)

    @pl.when(rest)
    def _():
        out_ref[used:, :] = rest_ref[...]

    @pl.when(jnp.logical_not(rest))
    def _():
        out_ref[used:, :] = hopped_ref[used:, :]


def choose_kernel(which, start, *refs):
    *arrays, out_ref = refs
    index = which()
    rows = out_ref.shape[0]
    for place, ref in enumerate(arrays):
        first = start if place == len(arrays) - 1 else 0
        size = min(rows, ref.shape[0] - first)

        @pl.when(index == place)
        def _():
            out_ref[:size, :] = ref[first : first + size, :]
            if size < rows:
                out_ref[size:, :] = jnp.zeros((rows - size, LANE), jnp.float32)


def fill_left(order, mine, a_ref, b_ref, left_ref):
    second = lax.rem(lax.div(lax.axis_index("dp"), 2), 2)
    for row in range(order // LANE):

        @pl.when(mine == row)
        def _():
            for column in range(order // LANE):
                block = stored_block(a_ref, b_ref, order, row, column, second)
                left_ref[:, column * LANE : (column + 1) * LANE] = block


def fill_right(order, a_ref, b_ref, left_b_ref, joined_ref, right_ref):
    cut = lax.axis_index("cuts")
    zq = lax.rem(lax.axis_index("dp"), QUAD)
    was_direct = jnp.logical_and(jnp.logical_not(is_middle()), (zq ^ 1) == 2 - lax.rem(cut, 2))
    used = joined_ref.shape[0] // 2
    joined_ref[...] = b_ref[...]

    @pl.when(was_direct)
    def _():
        joined_ref[used:, :] = left_b_ref[used:, :]

    unpack(
        lambda start, size: a_ref[pl.ds(start, size), :],
        lambda start, size: joined_ref[pl.ds(start, size), :],
        order,
        right_ref,
        lax.rem(cut, 2),
    )


def place_of_rows(spread):
    core = lax.axis_index("grad")
    return core, lax.rem(lax.axis_index("dp") * lax.axis_size("grad") + core, spread)


def first_kernel(order, spread, own_a, own_b, other_b, *refs):
    own_rows_ref, other_rows_ref, outer_ref, outer_other_ref, direct_ref, relayed_a, relayed_b, relayed_other, *refs = refs
    left_out, right_out, left_ref, right_ref, tile_ref, joined_ref = refs
    core, mine = place_of_rows(spread)
    rows_dev = own_rows_ref.shape[0]

    def place(position):
        return pl.ds(pl.multiple_of(position * rows_dev, rows_dev), rows_dev)

    tile_ref[place(mine), :] = own_rows_ref[...]
    tile_ref[place(mine ^ 1), :] = other_rows_ref[...]
    here = core == rows_core()
    cases = (
        (False, True, (outer_ref,)),
        (False, False, (outer_other_ref,)),
        (True, True, (direct_ref.at[: relayed_a.shape[0]], relayed_other)),
        (True, False, (relayed_a, relayed_b)),
    )
    for middle, arrived, parts in cases:

        @pl.when(jnp.logical_and(is_middle() == middle, here == arrived))
        def _():
            start, part = 0, 0
            for turn in range(2):
                for column in range(order // LANE):
                    if start == parts[part].shape[0]:
                        start, part = 0, part + 1
                    tile_ref[place((mine // 2 ^ 1) * 2 + turn), column * LANE : (column + 1) * LANE] = parts[part][
                        start : start + rows_dev, :
                    ]
                    start += rows_dev

    @pl.when(core != 0)
    def _():
        fill_left(order, mine, own_a, own_b, left_ref)
        left_out[...] = times(halves(left_ref[...]), halves(tile_ref[...]))

    @pl.when(core == 0)
    def _():
        fill_right(order, own_a, own_b, other_b, joined_ref, right_ref)
        right_out[...] = times(halves(tile_ref[...]), halves(right_ref[...]))


def last_kernel(order, spread, own_b, other_a, other_b, first_left, first_right, out_ref, *refs):
    left_ref, right_ref, joined_ref, result_ref, sems = refs
    core, mine = place_of_rows(spread)
    step = order // 2

    def finish(left, right_ref):
        copies = []
        for turn in range(2):
            columns = pl.ds(turn * step, step)
            result_ref[turn] = times(left, halves(right_ref[:, turn * step : (turn + 1) * step]))
            copies.append(pltpu.make_async_copy(result_ref.at[turn], out_ref.at[:, columns], sems.at[turn]))
            copies[-1].start()
        for copy in copies:
            copy.wait()

    @pl.when(core != 0)
    def _():
        fill_right(order, other_a, other_b, own_b, joined_ref, right_ref)
        finish(halves(first_left[...]), right_ref)

    @pl.when(core == 0)
    def _():
        fill_left(order, mine, other_a, other_b, left_ref)
        finish(halves(left_ref[...]), first_right)


def call(kernel, shapes, scratch, *args, space=pltpu.VMEM):
    return pl.pallas_call(
        kernel,
        out_shape=[jax.ShapeDtypeStruct(shape, jnp.float32) for shape in shapes],
        out_specs=[pl.BlockSpec(memory_space=space) for shape in shapes],
        scratch_shapes=scratch,
        compiler_params=PARAMS,
    )(*args)


class Plan:
    def __init__(self, groups, dp, cuts):
        self.groups, self.dp, self.cuts = groups, dp, cuts
        self.bases = range(0, dp, QUAD)

    def index(self, z, x, core):
        return (z * self.cuts + x % self.cuts) * 2 + core

    def roots(self, base, x):
        return base + 1 + x % 2, base + 2 - x % 2

    def one_way(self, pairs):
        pairs = list(pairs)
        size = self.dp * self.cuts * 2
        return [(group * size + a, group * size + b) for group in range(self.groups) for a, b in pairs]

    def whole(self, edges, abreast=False):
        size = self.dp * self.cuts * 2
        target = dict(self.one_way(edges))

        def pair_up(other):
            for device in range(size * self.groups):
                chosen = other(device)
                if device not in target and chosen not in target and chosen < size * self.groups:
                    target[device], target[chosen] = chosen, device

        pair_up(lambda device: device ^ 1)
        if abreast and self.cuts % 2 == 0:
            pair_up(lambda device: device ^ 3)
        pair_up(lambda device: (device + size) % (2 * size) + device // (2 * size) * 2 * size)
        return sorted(target.items())

    def swaps(self, pairs):
        return self.whole([edge for a, b in pairs for edge in ((a, b), (b, a))])

    def chains(self, pairs):
        to, of = dict(pairs), {b: a for a, b in pairs}
        edges = list(pairs)
        for device in sorted(set(to) | set(of)):
            if device in of and device not in to:
                if device ^ 1 in of or device ^ 1 not in to:
                    return self.swaps(pairs)
                edges.append((device, device ^ 1))
            elif device in to and device not in of and (device ^ 1 in to or device ^ 1 not in of):
                return self.swaps(pairs)
        return self.whole(edges)

    def loops(self, pairs):
        edges = []
        for a, b in pairs:
            if (a ^ 1, b ^ 1) in pairs:
                edges += [(a, b), (b, a)]
            else:
                edges += [(a, b), (b, b ^ 1), (b ^ 1, a ^ 1), (a ^ 1, a)]
        return self.whole(edges)

    def across(self, bit):
        return self.one_way(
            (self.index(z, x, core), self.index(z ^ bit, x, core))
            for z in range(self.dp)
            for x in range(self.cuts)
            for core in range(2)
        )

    def collect(self):
        far, near, outer = [], [], []
        for x in range(self.cuts):
            for base in self.bases:
                left, right = self.roots(base, x)
                left_root, right_root = self.index(left, x, 1), self.index(right, x, 0)
                right_far, left_far = self.index(left ^ 1, x, 1), self.index(right ^ 1, x, 0)
                far += [(left_far, left_root), (left_root, right_far), (right_far, right_root), (right_root, left_far)]
                near.append((self.index(right, x, 0), left_root))
                outer.append((self.index(left ^ 1, x, 0), left_root))
                outer.append((self.index(right ^ 1, x, 1), right_root))
        return self.whole(far, True), self.swaps(near), self.loops(outer)

    def spread(self):
        hops = [[] for turn in range(1, self.cuts)]
        direct = []
        relays = [[] for turn in range(1, self.cuts)]
        for x in range(self.cuts):
            for base in self.bases:
                left, right = self.roots(base, x)
                right_root, middle = self.index(right, x, 0), self.index(left, x, 0)
                hops[0].append((right_root, middle))
                left_root = self.index(left, x, 1)
                direct.append((right_root, self.index(right ^ 1, x, 0)))
                direct.append((left_root, self.index(left ^ 1, x, 1)))
                relays[0].append((middle, self.index(left ^ 1, x, 0)))
                if x // 2 != base // QUAD:
                    continue
                for turn in range(1, self.cuts):
                    abreast = self.index(left, x + turn, 1)
                    hops[turn - 1].append((left_root, abreast))
                    relays[turn - 1].append((abreast, self.index(left ^ 1, x + turn, 1)))
        return [self.chains(pairs) for pairs in hops], self.loops(direct), [self.loops(pairs) for pairs in relays]

    def turn(self):
        z, x, core = (lax.axis_index(name) for name in AXES[1:])
        turn = lax.rem(x + self.cuts - lax.div(z, 2), self.cuts)
        return jnp.where(lax.rem(z, QUAD) == 1 + lax.rem(x, 2), 0, jnp.maximum(turn - 1, 0))

    def which(self):
        z, x, core = (lax.axis_index(name) for name in AXES[1:])
        zq, middle = lax.rem(z, QUAD), is_middle()
        block = lax.div(z, 2)
        turn = lax.rem(x + self.cuts - block, self.cuts)
        direct = 2 * self.cuts - 1
        left = jnp.where(middle, turn, jnp.where(turn == 0, direct, self.cuts - 1 + turn))
        right_root = 2 - lax.rem(x, 2)
        right = jnp.where(
            zq == right_root, 0, jnp.where(middle, 1, jnp.where((zq ^ 1) == right_root, direct, self.cuts))
        )
        return jnp.where(core == 1, left, right)


def is_middle():
    zq = lax.rem(lax.axis_index("dp"), QUAD)
    return jnp.logical_or(zq == 1, zq == 2)


def rows_core():
    zq = lax.rem(lax.axis_index("dp"), QUAD)
    left = 1 + lax.rem(lax.axis_index("cuts"), 2)
    return jnp.where(is_middle(), zq != left, (zq ^ 1) == left).astype(jnp.int32)


def swap_cores(array):
    return lax.ppermute(array, "grad", [(0, 1), (1, 0)])


def per_device(acts, outgrads, grads):
    groups, dp, cuts, cores = (lax.axis_size(name) for name in AXES)
    tok_rows, order = acts.shape[1:]
    dev_count = dp * cores
    spread = dev_count // cuts
    plan = Plan(groups, dp, cuts)
    split, rest = part_rows(order)
    shape = (split + rest, LANE)
    acts, outgrads, grads = acts[0], outgrads[0], grads[0]

    core = lax.axis_index("grad")
    (sent,) = call(cov_kernel, [shape], [], jnp.where(core == 0, outgrads, acts))
    (kept,) = call(cov_kernel, [shape], [], jnp.where(core == 0, acts, outgrads))
    other_rows = swap_cores(grads)
    chip, outer = call(chip_kernel, [shape] * 2, [], kept, swap_cores(sent), grads)
    bit = QUAD
    while bit < dp:
        chip = chip + lax.ppermute(chip, AXES, plan.across(bit))
        outer = jnp.where(is_middle(), outer, chip)
        bit *= 2
    far, near, outward = plan.collect()
    sums = [
        lax.ppermute(outer, AXES, outward),
        lax.ppermute(chip, AXES, near),
        lax.ppermute(outer, AXES, far),
        swap_cores(chip),
    ]
    scale = 1.0 / (tok_rows * dev_count)
    square_scratch = pltpu.VMEM((order, order), jnp.float32)
    gathered = (2 * grads.size // LANE, LANE)
    *inverse, direct, rest_own, outer_rows = call(
        functools.partial(inverse_kernel, scale, order),
        [(split, LANE), (rest, LANE), (split + rest - rest // 2, LANE), (rest // 2, LANE), gathered],
        [square_scratch, pltpu.VMEM(shape, jnp.float32)],
        *sums,
        grads,
        other_rows,
    )

    hops, outward, relays = plan.spread()
    hopped = [[lax.ppermute(inverse[0], AXES, pairs) for pairs in hops]]
    direct = lax.ppermute(direct, AXES, outward)
    hopped.append([lax.ppermute(inverse[1], AXES, pairs) for pairs in hops])
    rest_own = swap_cores(rest_own)
    carried = [
        hopped[0],
        [call(relay_kernel, [array.shape], [], array, rest_own)[0] for array in hopped[1]],
    ]
    relayed = [[lax.ppermute(array, AXES, pairs) for array, pairs in zip(arrays, relays)] for arrays in carried]
    relayed[1], direct = lax.optimization_barrier((relayed[1], direct))
    arrived = [
        arrays[0] if cuts == 2 else call(functools.partial(choose_kernel, plan.turn, 0), [arrays[0].shape], [], *arrays)[0]
        for arrays in relayed
    ]
    own = []
    for part, start in ((0, 0), (1, split)):
        own += call(
            functools.partial(choose_kernel, plan.which, start),
            [inverse[part].shape],
            [],
            inverse[part],
            *hopped[part],
            *relayed[part],
            direct,
        )
    other_a, other_b = map(swap_cores, own)
    left_scratch = pltpu.VMEM((LANE, order), jnp.float32)
    joined_scratch = pltpu.VMEM((rest, LANE), jnp.float32)
    first = call(
        functools.partial(first_kernel, order, spread),
        [(LANE, order), (order, order)],
        [left_scratch, square_scratch, square_scratch, joined_scratch],
        *own,
        other_b,
        grads,
        other_rows,
        outer_rows,
        swap_cores(outer_rows),
        direct,
        *arrived,
        swap_cores(arrived[1]),
    )
    (out,) = call(
        functools.partial(last_kernel, order, spread),
        [grads.shape],
        [
            left_scratch,
            square_scratch,
            joined_scratch,
            pltpu.VMEM((2, LANE, order // 2), jnp.float32),
            pltpu.SemaphoreType.DMA((2,)),
        ],
        own[1],
        other_a,
        other_b,
        *first,
        space=pl.ANY,
    )
    return out[None]


def solution(mesh):
    in_specs = (
        P(None, ("groups", "dp", "grad"), "cuts"),
        P(None, ("groups", "dp", "grad"), "cuts"),
        P("groups", ("dp", "grad"), "cuts"),
    )
    out_specs = P("groups", ("dp", "grad"), "cuts")
    return jax.shard_map(
        per_device, mesh=mesh, in_specs=in_specs, out_specs=out_specs, check_vma=False
    )
```

```python
import functools
import jax
import jax.numpy as jnp
from jax import lax
from jax.experimental import pallas as pl
from jax.experimental.pallas import tpu as pltpu
from jax.sharding import PartitionSpec as P

ITERS = 4
DAMPING = 0.5
START = 1.9
LANE = 128
QUAD = 4
AXES = ("groups", "dp", "cuts", "grad")
PARAMS = pltpu.CompilerParams(vmem_limit_bytes=48 * 1024 * 1024)


def half_blocks(order, half):
    count = order // LANE // 2
    own = range(half * count, (half + 1) * count)
    return [(i, j) for i in own for j in own if i < j], [(i, i + 1) for i in own[::2]]


def joining_blocks(order):
    count = order // LANE
    return [(i, j) for i in range(count // 2) for j in range(count // 2, count)]


def part_rows(order):
    above, pairs = half_blocks(order, 0)
    own = (len(above) + len(pairs)) * LANE + -(-len(pairs) // 8) * 8
    return len(joining_blocks(order)) * LANE, 2 * own


def own_start(order, half, second):
    rows = part_rows(order)[1] // 2
    return (half ^ second) * rows if isinstance(second, int) else pl.multiple_of((half ^ second) * rows, 8)


def places():
    rows = lax.broadcasted_iota(jnp.int32, (LANE, LANE), 0)
    cols = lax.broadcasted_iota(jnp.int32, (LANE, LANE), 1)
    return rows, cols


def pack(block, order, a_ref, b_ref, second=0):
    rows, cols = places()
    for slot, (i, j) in enumerate(joining_blocks(order)):
        a_ref[slot * LANE : (slot + 1) * LANE, :] = block(i, j)
    for half in range(2):
        top = own_start(order, half, second)
        above, pairs = half_blocks(order, half)
        values = [block(i, j) for i, j in above]
        values += [jnp.where(rows <= cols, block(i, i), block(j, j)) for i, j in pairs]
        last = [jnp.sum(jnp.where(rows == cols, block(j, j), 0.0), axis=0, keepdims=True) for _, j in pairs]
        values.append(jnp.concatenate(last + [jnp.zeros((-len(pairs) % 8, LANE), jnp.float32)], 0))
        for value in values:
            b_ref[pl.ds(top, value.shape[0]), :] = value
            top += value.shape[0]


def unpack(a_piece, b_piece, order, out_ref, second=0, scale=1.0, shift=0.0):
    rows, cols = places()
    damping = jnp.where(rows == cols, shift, 0.0)

    def put(i, j, value):
        out_ref[i * LANE : (i + 1) * LANE, j * LANE : (j + 1) * LANE] = value

    def put_both(i, j, value):
        put(i, j, value)
        put(j, i, value.T)

    for slot, (i, j) in enumerate(joining_blocks(order)):
        put_both(i, j, a_piece(slot * LANE, LANE) * scale)
    for half in range(2):
        top = own_start(order, half, second)
        above, pairs = half_blocks(order, half)
        for i, j in above:
            put_both(i, j, b_piece(top, LANE) * scale)
            top += LANE
        last = b_piece(top + len(pairs) * LANE, -(-len(pairs) // 8) * 8)
        for k, (i, j) in enumerate(pairs):
            both = b_piece(top, LANE)
            turned = both.T
            put(i, i, jnp.where(rows <= cols, both, turned) * scale + damping)
            after = jnp.where(rows > cols, both, jnp.where(rows < cols, turned, last[k : k + 1, :]))
            put(j, j, after * scale + damping)
            top += LANE


def stored_block(a_ref, b_ref, order, i, j, second):
    if i > j:
        return stored_block(a_ref, b_ref, order, j, i, second).T
    if (i, j) in joining_blocks(order):
        start = joining_blocks(order).index((i, j)) * LANE
        return a_ref[start : start + LANE, :]
    half = i // (order // LANE // 2)
    above, pairs = half_blocks(order, half)
    top = own_start(order, half, second)
    if i < j:
        return b_ref[pl.ds(top + above.index((i, j)) * LANE, LANE), :]
    place = next(k for k, pair in enumerate(pairs) if i in pair)
    both = b_ref[pl.ds(top + (len(above) + place) * LANE, LANE), :]
    rows, cols = places()
    if i == pairs[place][0]:
        return jnp.where(rows <= cols, both, both.T)
    last = b_ref[pl.ds(top + (len(above) + len(pairs)) * LANE, -(-len(pairs) // 8) * 8), :]
    return jnp.where(rows > cols, both, jnp.where(rows < cols, both.T, last[place : place + 1, :]))


def halves(value):
    high = value.astype(jnp.bfloat16)
    return high, (value - high.astype(jnp.float32)).astype(jnp.bfloat16)


def times(left, right):
    dot = functools.partial(jnp.dot, preferred_element_type=jnp.float32)
    rows = left[0].shape[0]
    both = dot(jnp.concatenate(left, 0), right[0])
    return both[:rows] + (dot(left[0], right[1]) + both[rows:])


def rows_of(pair, start, stop):
    return pair[0][start:stop, :], pair[1][start:stop, :]


def upper_times(left, right):
    middle = left[0].shape[0] // 2
    top = times(rows_of(left, 0, middle), right)
    corner = times(rows_of(left, middle, 2 * middle), (right[0][:, middle:], right[1][:, middle:]))
    return top, corner


def upper_square(value):
    dot = functools.partial(jnp.dot, preferred_element_type=jnp.float32)
    high, low = value
    middle = high.shape[0] // 2
    mixed = dot(high, low)
    top = dot(high[:middle], high) + (mixed[:middle] + mixed[:, :middle].T)
    corner = mixed[middle:, middle:]
    return top, dot(high[middle:], high[:, middle:]) + (corner + corner.T)


def whole(top, corner):
    middle = corner.shape[0]
    return jnp.concatenate([top, jnp.concatenate([top[:, middle:].T, corner], 1)], 0)


def cov_kernel(x_ref, out_ref):
    x = x_ref[...]
    order = x.shape[1]
    split = part_rows(order)[0]
    total = lax.dot_general(x, x, (((0,), (0,)), ((), ())), preferred_element_type=jnp.float32)
    pack(block_of(total), order, out_ref.at[:split], out_ref.at[split:])


def block_of(value):
    return lambda i, j: value[i * LANE : (i + 1) * LANE, j * LANE : (j + 1) * LANE]


def put_rows(out_ref, start, rows_ref):
    rows, columns = rows_ref.shape
    for column in range(columns // LANE):
        out_ref[start : start + rows, :] = rows_ref[:, column * LANE : (column + 1) * LANE]
        start += rows


def chip_kernel(kept_ref, other_ref, rows_ref, chip_ref, outer_ref):
    chip_ref[...] = kept_ref[...] + other_ref[...]

    @pl.when(is_middle())
    def _():
        used = rows_ref.shape[0] * rows_ref.shape[1] // LANE
        put_rows(outer_ref, 0, rows_ref)
        outer_ref[used:, :] = jnp.zeros((outer_ref.shape[0] - used, LANE), jnp.float32)

    @pl.when(jnp.logical_not(is_middle()))
    def _():
        outer_ref[...] = chip_ref[...]


def inverse_kernel(scale, order, *refs):
    *sums, own_rows_ref, other_rows_ref, a_ref, b_ref, direct_ref, gathered_ref, factor_ref, rows_ref = refs
    split = part_rows(order)[0]

    def piece(start, size):
        total = sums[0][start : start + size, :]
        for ref in sums[1:]:
            total = total + ref[start : start + size, :]
        return total

    unpack(piece, lambda start, size: piece(split + start, size), order, factor_ref, 0, scale, DAMPING)
    factor = factor_ref[...]
    bound = jnp.max(jnp.sum(jnp.abs(factor), axis=0, keepdims=True), axis=1, keepdims=True) + 1e-06
    start = START / bound
    rows = lax.broadcasted_iota(jnp.int32, (order, order), 0)
    cols = lax.broadcasted_iota(jnp.int32, (order, order), 1)
    eye = jnp.where(rows == cols, 1.0, 0.0)
    total = eye - start * factor
    power_halves = halves(total)
    middle = order // 2
    for step in range(1, ITERS):
        power = whole(*upper_square(power_halves))
        power_halves = halves(power)
        top, corner = upper_times(halves(total), power_halves)
        known = total + power
        top, corner = top + known[:middle], corner + known[middle:, middle:]
        if step < ITERS - 1:
            total = whole(top, corner)

    def block(i, j):
        if i < middle // LANE:
            value = block_of(top)(i, j)
        else:
            value = block_of(corner)(i - middle // LANE, j - middle // LANE)
        return start * (value + block_of(eye)(i, j))

    @pl.when(is_middle())
    def _():
        pack(block, order, a_ref, b_ref, lax.rem(lax.axis_index("cuts"), 2))
        direct_ref[:split, :] = a_ref[...]
        direct_ref[split:, :] = b_ref[...]

    @pl.when(jnp.logical_not(is_middle()))
    def _():
        core = lax.axis_index("grad")
        size = own_rows_ref.shape[0] * own_rows_ref.shape[1] // LANE
        rows_ref[2 * size :, :] = jnp.zeros((rows_ref.shape[0] - 2 * size, LANE), jnp.float32)
        for mine in range(2):

            @pl.when(core == mine)
            def _():
                put_rows(rows_ref, mine * size, own_rows_ref)
                put_rows(rows_ref, (1 - mine) * size, other_rows_ref)

            @pl.when(rows_core() == mine)
            def _():
                outer, far = sums[0][:size, :], sums[2][:size, :]
                gathered_ref[:size, :] = outer if mine else far
                gathered_ref[size:, :] = far if mine else outer

        a_ref[...] = rows_ref[:split, :]
        b_ref[...] = rows_ref[split:, :]
        direct_ref[...] = rows_ref[...]


def choose_kernel(which, start, *refs):
    *arrays, out_ref = refs
    index = which()
    rows = out_ref.shape[0]
    for place, ref in enumerate(arrays):
        first = start if place == len(arrays) - 1 else 0

        @pl.when(index == place)
        def _():
            out_ref[...] = ref[first : first + rows, :]


def fill_left(order, mine, a_ref, b_ref, left_ref):
    second = lax.rem(lax.div(lax.axis_index("dp"), 2), 2)
    for row in range(order // LANE):

        @pl.when(mine == row)
        def _():
            for column in range(order // LANE):
                block = stored_block(a_ref, b_ref, order, row, column, second)
                left_ref[:, column * LANE : (column + 1) * LANE] = block


def fill_right(order, a_ref, b_ref, right_ref):
    unpack(
        lambda start, size: a_ref[pl.ds(start, size), :],
        lambda start, size: b_ref[pl.ds(start, size), :],
        order,
        right_ref,
        lax.rem(lax.axis_index("cuts"), 2),
    )


def place_of_rows(spread):
    core = lax.axis_index("grad")
    return core, lax.rem(lax.axis_index("dp") * lax.axis_size("grad") + core, spread)


def first_kernel(order, spread, own_a, own_b, *refs):
    own_rows_ref, other_rows_ref, outer_ref, outer_other_ref, direct_ref, relayed_a, relayed_b, relayed_other, *refs = refs
    left_out, right_out, left_ref, right_ref, tile_ref = refs
    core, mine = place_of_rows(spread)
    rows_dev = own_rows_ref.shape[0]

    def place(position):
        return pl.ds(pl.multiple_of(position * rows_dev, rows_dev), rows_dev)

    tile_ref[place(mine), :] = own_rows_ref[...]
    tile_ref[place(mine ^ 1), :] = other_rows_ref[...]
    here = core == rows_core()
    cases = (
        (False, True, (outer_ref,)),
        (False, False, (outer_other_ref,)),
        (True, True, (direct_ref.at[: relayed_a.shape[0]], relayed_other)),
        (True, False, (relayed_a, relayed_b)),
    )
    for middle, arrived, parts in cases:

        @pl.when(jnp.logical_and(is_middle() == middle, here == arrived))
        def _():
            start, part = 0, 0
            for turn in range(2):
                for column in range(order // LANE):
                    if start == parts[part].shape[0]:
                        start, part = 0, part + 1
                    tile_ref[place((mine // 2 ^ 1) * 2 + turn), column * LANE : (column + 1) * LANE] = parts[part][
                        start : start + rows_dev, :
                    ]
                    start += rows_dev

    @pl.when(core != 0)
    def _():
        fill_left(order, mine, own_a, own_b, left_ref)
        left_out[...] = times(halves(left_ref[...]), halves(tile_ref[...]))

    @pl.when(core == 0)
    def _():
        fill_right(order, own_a, own_b, right_ref)
        right_out[...] = times(halves(tile_ref[...]), halves(right_ref[...]))


def last_kernel(order, spread, other_a, other_b, first_left, first_right, out_ref, *refs):
    left_ref, right_ref, result_ref, sems = refs
    core, mine = place_of_rows(spread)
    step = order // 2

    def finish(left, right_ref):
        copies = []
        for turn in range(2):
            columns = pl.ds(turn * step, step)
            result_ref[turn] = times(left, halves(right_ref[:, turn * step : (turn + 1) * step]))
            copies.append(pltpu.make_async_copy(result_ref.at[turn], out_ref.at[:, columns], sems.at[turn]))
            copies[-1].start()
        for copy in copies:
            copy.wait()

    @pl.when(core != 0)
    def _():
        fill_right(order, other_a, other_b, right_ref)
        finish(halves(first_left[...]), right_ref)

    @pl.when(core == 0)
    def _():
        fill_left(order, mine, other_a, other_b, left_ref)
        finish(halves(left_ref[...]), first_right)


def call(kernel, shapes, scratch, *args, space=pltpu.VMEM):
    return pl.pallas_call(
        kernel,
        out_shape=[jax.ShapeDtypeStruct(shape, jnp.float32) for shape in shapes],
        out_specs=[pl.BlockSpec(memory_space=space) for shape in shapes],
        scratch_shapes=scratch,
        compiler_params=PARAMS,
    )(*args)


class Plan:
    def __init__(self, groups, dp, cuts):
        self.groups, self.dp, self.cuts = groups, dp, cuts
        self.bases = range(0, dp, QUAD)

    def index(self, z, x, core):
        return (z * self.cuts + x % self.cuts) * 2 + core

    def roots(self, base, x):
        return base + 1 + x % 2, base + 2 - x % 2

    def one_way(self, pairs):
        pairs = list(pairs)
        size = self.dp * self.cuts * 2
        return [(group * size + a, group * size + b) for group in range(self.groups) for a, b in pairs]

    def whole(self, edges, abreast=False):
        size = self.dp * self.cuts * 2
        target = dict(self.one_way(edges))

        def pair_up(other):
            for device in range(size * self.groups):
                chosen = other(device)
                if device not in target and chosen not in target and chosen < size * self.groups:
                    target[device], target[chosen] = chosen, device

        pair_up(lambda device: device ^ 1)
        if abreast and self.cuts % 2 == 0:
            pair_up(lambda device: device ^ 3)
        pair_up(lambda device: (device + size) % (2 * size) + device // (2 * size) * 2 * size)
        return sorted(target.items())

    def swaps(self, pairs):
        return self.whole([edge for a, b in pairs for edge in ((a, b), (b, a))])

    def chains(self, pairs):
        to, of = dict(pairs), {b: a for a, b in pairs}
        edges = list(pairs)
        for device in sorted(set(to) | set(of)):
            if device in of and device not in to:
                if device ^ 1 in of or device ^ 1 not in to:
                    return self.swaps(pairs)
                edges.append((device, device ^ 1))
            elif device in to and device not in of and (device ^ 1 in to or device ^ 1 not in of):
                return self.swaps(pairs)
        return self.whole(edges)

    def loops(self, pairs):
        edges = []
        for a, b in pairs:
            if (a ^ 1, b ^ 1) in pairs:
                edges += [(a, b), (b, a)]
            else:
                edges += [(a, b), (b, b ^ 1), (b ^ 1, a ^ 1), (a ^ 1, a)]
        return self.whole(edges)

    def across(self, bit):
        return self.one_way(
            (self.index(z, x, core), self.index(z ^ bit, x, core))
            for z in range(self.dp)
            for x in range(self.cuts)
            for core in range(2)
        )

    def collect(self):
        far, near, outer = [], [], []
        for x in range(self.cuts):
            for base in self.bases:
                left, right = self.roots(base, x)
                left_root, right_root = self.index(left, x, 1), self.index(right, x, 0)
                right_far, left_far = self.index(left ^ 1, x, 1), self.index(right ^ 1, x, 0)
                far += [(left_far, left_root), (left_root, right_far), (right_far, right_root), (right_root, left_far)]
                near.append((self.index(right, x, 0), left_root))
                outer.append((self.index(left ^ 1, x, 0), left_root))
                outer.append((self.index(right ^ 1, x, 1), right_root))
        return self.whole(far, True), self.swaps(near), self.loops(outer)

    def spread(self):
        hops = [[] for turn in range(1, self.cuts)]
        direct = []
        relays = [[] for turn in range(1, self.cuts)]
        for x in range(self.cuts):
            for base in self.bases:
                left, right = self.roots(base, x)
                right_root, middle = self.index(right, x, 0), self.index(left, x, 0)
                hops[0].append((right_root, middle))
                left_root = self.index(left, x, 1)
                direct.append((right_root, self.index(right ^ 1, x, 0)))
                direct.append((left_root, self.index(left ^ 1, x, 1)))
                relays[0].append((middle, self.index(left ^ 1, x, 0)))
                if x // 2 != base // QUAD:
                    continue
                for turn in range(1, self.cuts):
                    abreast = self.index(left, x + turn, 1)
                    hops[turn - 1].append((left_root, abreast))
                    relays[turn - 1].append((abreast, self.index(left ^ 1, x + turn, 1)))
        return [self.chains(pairs) for pairs in hops], self.loops(direct), [self.loops(pairs) for pairs in relays]

    def turn(self):
        z, x, core = (lax.axis_index(name) for name in AXES[1:])
        turn = lax.rem(x + self.cuts - lax.div(z, 2), self.cuts)
        return jnp.where(lax.rem(z, QUAD) == 1 + lax.rem(x, 2), 0, jnp.maximum(turn - 1, 0))

    def which(self):
        z, x, core = (lax.axis_index(name) for name in AXES[1:])
        zq, middle = lax.rem(z, QUAD), is_middle()
        block = lax.div(z, 2)
        turn = lax.rem(x + self.cuts - block, self.cuts)
        direct = 2 * self.cuts - 1
        left = jnp.where(middle, turn, jnp.where(turn == 0, direct, self.cuts - 1 + turn))
        right_root = 2 - lax.rem(x, 2)
        right = jnp.where(
            zq == right_root, 0, jnp.where(middle, 1, jnp.where((zq ^ 1) == right_root, direct, self.cuts))
        )
        return jnp.where(core == 1, left, right)


def is_middle():
    zq = lax.rem(lax.axis_index("dp"), QUAD)
    return jnp.logical_or(zq == 1, zq == 2)


def rows_core():
    zq = lax.rem(lax.axis_index("dp"), QUAD)
    left = 1 + lax.rem(lax.axis_index("cuts"), 2)
    return jnp.where(is_middle(), zq != left, (zq ^ 1) == left).astype(jnp.int32)


def swap_cores(array):
    return lax.ppermute(array, "grad", [(0, 1), (1, 0)])


def per_device(acts, outgrads, grads):
    groups, dp, cuts, cores = (lax.axis_size(name) for name in AXES)
    tok_rows, order = acts.shape[1:]
    dev_count = dp * cores
    spread = dev_count // cuts
    plan = Plan(groups, dp, cuts)
    split, rest = part_rows(order)
    shape = (split + rest, LANE)
    acts, outgrads, grads = acts[0], outgrads[0], grads[0]

    core = lax.axis_index("grad")
    (sent,) = call(cov_kernel, [shape], [], jnp.where(core == 0, outgrads, acts))
    (kept,) = call(cov_kernel, [shape], [], jnp.where(core == 0, acts, outgrads))
    other_rows = swap_cores(grads)
    chip, outer = call(chip_kernel, [shape] * 2, [], kept, swap_cores(sent), grads)
    bit = QUAD
    while bit < dp:
        chip = chip + lax.ppermute(chip, AXES, plan.across(bit))
        outer = jnp.where(is_middle(), outer, chip)
        bit *= 2
    far, near, outward = plan.collect()
    sums = [
        lax.ppermute(outer, AXES, outward),
        lax.ppermute(chip, AXES, near),
        lax.ppermute(outer, AXES, far),
        swap_cores(chip),
    ]
    scale = 1.0 / (tok_rows * dev_count)
    square_scratch = pltpu.VMEM((order, order), jnp.float32)
    gathered = (2 * grads.size // LANE, LANE)
    *inverse, direct, outer_rows = call(
        functools.partial(inverse_kernel, scale, order),
        [(split, LANE), (rest, LANE), shape, gathered],
        [square_scratch, pltpu.VMEM(shape, jnp.float32)],
        *sums,
        grads,
        other_rows,
    )

    hops, outward, relays = plan.spread()
    hopped = [[lax.ppermute(inverse[0], AXES, pairs) for pairs in hops]]
    direct = lax.ppermute(direct, AXES, outward)
    hopped.append([lax.ppermute(inverse[1], AXES, pairs) for pairs in hops])
    relayed = [[lax.ppermute(array, AXES, pairs) for array, pairs in zip(arrays, relays)] for arrays in hopped]
    relayed[1], direct = lax.optimization_barrier((relayed[1], direct))
    arrived = [
        arrays[0] if cuts == 2 else call(functools.partial(choose_kernel, plan.turn, 0), [arrays[0].shape], [], *arrays)[0]
        for arrays in relayed
    ]
    own = []
    for part, start in ((0, 0), (1, split)):
        own += call(
            functools.partial(choose_kernel, plan.which, start),
            [inverse[part].shape],
            [],
            inverse[part],
            *hopped[part],
            *relayed[part],
            direct,
        )
    other_a, other_b = map(swap_cores, own)
    left_scratch = pltpu.VMEM((LANE, order), jnp.float32)
    first = call(
        functools.partial(first_kernel, order, spread),
        [(LANE, order), (order, order)],
        [left_scratch, square_scratch, square_scratch],
        *own,
        grads,
        other_rows,
        outer_rows,
        swap_cores(outer_rows),
        direct,
        *arrived,
        swap_cores(arrived[1]),
    )
    (out,) = call(
        functools.partial(last_kernel, order, spread),
        [grads.shape],
        [
            left_scratch,
            square_scratch,
            pltpu.VMEM((2, LANE, order // 2), jnp.float32),
            pltpu.SemaphoreType.DMA((2,)),
        ],
        other_a,
        other_b,
        *first,
        space=pl.ANY,
    )
    return out[None]


def solution(mesh):
    in_specs = (
        P(None, ("groups", "dp", "grad"), "cuts"),
        P(None, ("groups", "dp", "grad"), "cuts"),
        P("groups", ("dp", "grad"), "cuts"),
    )
    out_specs = P("groups", ("dp", "grad"), "cuts")
    return jax.shard_map(
        per_device, mesh=mesh, in_specs=in_specs, out_specs=out_specs, check_vma=False
    )
```

```python
import functools
import jax
import jax.numpy as jnp
from jax import lax
from jax.experimental import pallas as pl
from jax.experimental.pallas import tpu as pltpu
from jax.sharding import PartitionSpec as P

ITERS = 4
DAMPING = 0.5
START = 1.9
LANE = 128
QUAD = 4
AXES = ("groups", "dp", "cuts", "grad")
PARAMS = pltpu.CompilerParams(vmem_limit_bytes=48 * 1024 * 1024)


def half_blocks(order, half):
    count = order // LANE // 2
    own = range(half * count, (half + 1) * count)
    return [(i, j) for i in own for j in own if i < j], [(i, i + 1) for i in own[::2]]


def joining_blocks(order):
    count = order // LANE
    return [(i, j) for i in range(count // 2) for j in range(count // 2, count)]


def part_rows(order):
    above, pairs = half_blocks(order, 0)
    own = (len(above) + len(pairs)) * LANE + -(-len(pairs) // 8) * 8
    return len(joining_blocks(order)) * LANE, 2 * own


def own_start(order, half, second):
    rows = part_rows(order)[1] // 2
    return (half ^ second) * rows if isinstance(second, int) else pl.multiple_of((half ^ second) * rows, 8)


def places():
    rows = lax.broadcasted_iota(jnp.int32, (LANE, LANE), 0)
    cols = lax.broadcasted_iota(jnp.int32, (LANE, LANE), 1)
    return rows, cols


def pack(block, order, a_ref, b_ref, second=0):
    rows, cols = places()
    for slot, (i, j) in enumerate(joining_blocks(order)):
        a_ref[slot * LANE : (slot + 1) * LANE, :] = block(i, j)
    for half in range(2):
        top = own_start(order, half, second)
        above, pairs = half_blocks(order, half)
        values = [block(i, j) for i, j in above]
        values += [jnp.where(rows <= cols, block(i, i), block(j, j)) for i, j in pairs]
        last = [jnp.sum(jnp.where(rows == cols, block(j, j), 0.0), axis=0, keepdims=True) for _, j in pairs]
        values.append(jnp.concatenate(last + [jnp.zeros((-len(pairs) % 8, LANE), jnp.float32)], 0))
        for value in values:
            b_ref[pl.ds(top, value.shape[0]), :] = value
            top += value.shape[0]


def unpack(a_piece, b_piece, order, out_ref, second=0, scale=1.0, shift=0.0):
    for slot, (i, j) in enumerate(joining_blocks(order)):
        value = a_piece(slot * LANE, LANE) * scale
        put_block(out_ref, i, j, value)
        put_block(out_ref, j, i, value.T)
    unpack_own(b_piece, order, out_ref, second, scale, shift)


def put_block(out_ref, i, j, value):
    out_ref[i * LANE : (i + 1) * LANE, j * LANE : (j + 1) * LANE] = value


def unpack_own(b_piece, order, out_ref, second=0, scale=1.0, shift=0.0):
    rows, cols = places()
    damping = jnp.where(rows == cols, shift, 0.0)
    for half in range(2):
        top = own_start(order, half, second)
        above, pairs = half_blocks(order, half)
        for i, j in above:
            value = b_piece(top, LANE) * scale
            put_block(out_ref, i, j, value)
            put_block(out_ref, j, i, value.T)
            top += LANE
        last = b_piece(top + len(pairs) * LANE, -(-len(pairs) // 8) * 8)
        for k, (i, j) in enumerate(pairs):
            both = b_piece(top, LANE)
            turned = both.T
            put_block(out_ref, i, i, jnp.where(rows <= cols, both, turned) * scale + damping)
            after = jnp.where(rows > cols, both, jnp.where(rows < cols, turned, last[k : k + 1, :]))
            put_block(out_ref, j, j, after * scale + damping)
            top += LANE


def stored_block(a_ref, b_ref, order, i, j, second):
    if i > j:
        return stored_block(a_ref, b_ref, order, j, i, second).T
    if (i, j) in joining_blocks(order):
        start = joining_blocks(order).index((i, j)) * LANE
        return a_ref[start : start + LANE, :]
    half = i // (order // LANE // 2)
    above, pairs = half_blocks(order, half)
    top = own_start(order, half, second)
    if i < j:
        return b_ref[pl.ds(top + above.index((i, j)) * LANE, LANE), :]
    place = next(k for k, pair in enumerate(pairs) if i in pair)
    both = b_ref[pl.ds(top + (len(above) + place) * LANE, LANE), :]
    rows, cols = places()
    if i == pairs[place][0]:
        return jnp.where(rows <= cols, both, both.T)
    last = b_ref[pl.ds(top + (len(above) + len(pairs)) * LANE, -(-len(pairs) // 8) * 8), :]
    return jnp.where(rows > cols, both, jnp.where(rows < cols, both.T, last[place : place + 1, :]))


def halves(value):
    high = value.astype(jnp.bfloat16)
    return high, (value - high.astype(jnp.float32)).astype(jnp.bfloat16)


def times(left, right, turned=False):
    dims = (((1,), (1 if turned else 0,)), ((), ()))
    dot = functools.partial(lax.dot_general, dimension_numbers=dims, preferred_element_type=jnp.float32)
    rows = left[0].shape[0]
    both = dot(jnp.concatenate(left, 0), right[0])
    return both[:rows] + (dot(left[0], right[1]) + both[rows:])


def rows_of(pair, start, stop):
    return pair[0][start:stop, :], pair[1][start:stop, :]


def upper_times(left, right):
    middle = left[0].shape[0] // 2
    top = times(rows_of(left, 0, middle), right)
    corner = times(rows_of(left, middle, 2 * middle), (right[0][:, middle:], right[1][:, middle:]))
    return top, corner


def upper_square(value):
    dot = functools.partial(jnp.dot, preferred_element_type=jnp.float32)
    high, low = value
    middle = high.shape[0] // 2
    mixed = dot(high, low)
    top = dot(high[:middle], high) + (mixed[:middle] + mixed[:, :middle].T)
    corner = mixed[middle:, middle:]
    return top, dot(high[middle:], high[:, middle:]) + (corner + corner.T)


def whole(top, corner):
    middle = corner.shape[0]
    return jnp.concatenate([top, jnp.concatenate([top[:, middle:].T, corner], 1)], 0)


def cov_kernel(x_ref, out_ref):
    x = x_ref[...]
    order = x.shape[1]
    split = part_rows(order)[0]
    total = lax.dot_general(x, x, (((0,), (0,)), ((), ())), preferred_element_type=jnp.float32)
    pack(block_of(total), order, out_ref.at[:split], out_ref.at[split:])


def block_of(value):
    return lambda i, j: value[i * LANE : (i + 1) * LANE, j * LANE : (j + 1) * LANE]


def put_rows(out_ref, start, rows_ref):
    rows, columns = rows_ref.shape
    for column in range(columns // LANE):
        out_ref[start : start + rows, :] = rows_ref[:, column * LANE : (column + 1) * LANE]
        start += rows


def chip_kernel(kept_ref, other_ref, rows_ref, chip_ref, outer_ref):
    chip_ref[...] = kept_ref[...] + other_ref[...]

    @pl.when(is_middle())
    def _():
        used = rows_ref.shape[0] * rows_ref.shape[1] // LANE
        put_rows(outer_ref, 0, rows_ref)
        outer_ref[used:, :] = jnp.zeros((outer_ref.shape[0] - used, LANE), jnp.float32)

    @pl.when(jnp.logical_not(is_middle()))
    def _():
        outer_ref[...] = chip_ref[...]


def inverse_kernel(scale, order, *refs):
    *sums, own_rows_ref, other_rows_ref, a_ref, b_ref, direct_ref, gathered_ref, factor_ref, rows_ref = refs
    split = part_rows(order)[0]

    def piece(start, size):
        total = sums[0][start : start + size, :]
        for ref in sums[1:]:
            total = total + ref[start : start + size, :]
        return total

    unpack(piece, lambda start, size: piece(split + start, size), order, factor_ref, 0, scale, DAMPING)
    factor = factor_ref[...]
    bound = jnp.max(jnp.sum(jnp.abs(factor), axis=0, keepdims=True), axis=1, keepdims=True) + 1e-06
    start = START / bound
    rows = lax.broadcasted_iota(jnp.int32, (order, order), 0)
    cols = lax.broadcasted_iota(jnp.int32, (order, order), 1)
    eye = jnp.where(rows == cols, 1.0, 0.0)
    total = eye - start * factor
    power_halves = halves(total)
    middle = order // 2
    for step in range(1, ITERS):
        power = whole(*upper_square(power_halves))
        power_halves = halves(power)
        top, corner = upper_times(halves(total), power_halves)
        known = total + power
        top, corner = top + known[:middle], corner + known[middle:, middle:]
        if step < ITERS - 1:
            total = whole(top, corner)

    def block(i, j):
        if i < middle // LANE:
            value = block_of(top)(i, j)
        else:
            value = block_of(corner)(i - middle // LANE, j - middle // LANE)
        return start * (value + block_of(eye)(i, j))

    @pl.when(is_middle())
    def _():
        pack(block, order, a_ref, b_ref, lax.rem(lax.axis_index("cuts"), 2))
        direct_ref[:split, :] = a_ref[...]
        direct_ref[split:, :] = b_ref[...]

    @pl.when(jnp.logical_not(is_middle()))
    def _():
        core = lax.axis_index("grad")
        size = own_rows_ref.shape[0] * own_rows_ref.shape[1] // LANE
        rows_ref[2 * size :, :] = jnp.zeros((rows_ref.shape[0] - 2 * size, LANE), jnp.float32)
        for mine in range(2):

            @pl.when(core == mine)
            def _():
                put_rows(rows_ref, mine * size, own_rows_ref)
                put_rows(rows_ref, (1 - mine) * size, other_rows_ref)

            @pl.when(rows_core() == mine)
            def _():
                outer, far = sums[0][:size, :], sums[2][:size, :]
                gathered_ref[:size, :] = outer if mine else far
                gathered_ref[size:, :] = far if mine else outer

        a_ref[...] = rows_ref[:split, :]
        b_ref[...] = rows_ref[split:, :]
        direct_ref[...] = rows_ref[...]


def choose_kernel(which, start, *refs):
    *arrays, out_ref = refs
    index = which()
    rows = out_ref.shape[0]
    for place, ref in enumerate(arrays):
        first = start if place == len(arrays) - 1 else 0

        @pl.when(index == place)
        def _():
            out_ref[...] = ref[first : first + rows, :]


def fill_left(order, mine, a_ref, b_ref, left_ref):
    second = lax.rem(lax.div(lax.axis_index("dp"), 2), 2)
    for row in range(order // LANE):

        @pl.when(mine == row)
        def _():
            for column in range(order // LANE):
                block = stored_block(a_ref, b_ref, order, row, column, second)
                left_ref[:, column * LANE : (column + 1) * LANE] = block


def fill_right(order, a_ref, b_ref, right_ref):
    unpack(
        lambda start, size: a_ref[pl.ds(start, size), :],
        lambda start, size: b_ref[pl.ds(start, size), :],
        order,
        right_ref,
        lax.rem(lax.axis_index("cuts"), 2),
    )


def place_of_rows(spread):
    core = lax.axis_index("grad")
    return core, lax.rem(lax.axis_index("dp") * lax.axis_size("grad") + core, spread)


def first_kernel(order, spread, own_a, own_b, other_b, *refs):
    own_rows_ref, other_rows_ref, outer_ref, outer_other_ref, direct_ref, relayed_a, relayed_b, relayed_other, *refs = refs
    left_out, high_out, low_out, left_ref, right_ref, tile_ref = refs
    core, mine = place_of_rows(spread)
    rows_dev = own_rows_ref.shape[0]

    def place(position):
        return pl.ds(pl.multiple_of(position * rows_dev, rows_dev), rows_dev)

    tile_ref[place(mine), :] = own_rows_ref[...]
    tile_ref[place(mine ^ 1), :] = other_rows_ref[...]
    here = core == rows_core()
    cases = (
        (False, True, (outer_ref,)),
        (False, False, (outer_other_ref,)),
        (True, True, (direct_ref.at[: relayed_a.shape[0]], relayed_other)),
        (True, False, (relayed_a, relayed_b)),
    )
    for middle, arrived, parts in cases:

        @pl.when(jnp.logical_and(is_middle() == middle, here == arrived))
        def _():
            start, part = 0, 0
            for turn in range(2):
                for column in range(order // LANE):
                    if start == parts[part].shape[0]:
                        start, part = 0, part + 1
                    tile_ref[place((mine // 2 ^ 1) * 2 + turn), column * LANE : (column + 1) * LANE] = parts[part][
                        start : start + rows_dev, :
                    ]
                    start += rows_dev

    @pl.when(core != 0)
    def _():
        fill_left(order, mine, own_a, own_b, left_ref)
        left_out[...] = times(halves(left_ref[...]), halves(tile_ref[...]))
        second = lax.rem(lax.axis_index("cuts"), 2)
        unpack_own(lambda start, size: other_b[pl.ds(start, size), :], order, right_ref, second)
        for own in (slice(0, order // 2), slice(order // 2, order)):
            high_out[own, own], low_out[own, own] = halves(right_ref[own, own])

    @pl.when(core == 0)
    def _():
        fill_right(order, own_a, own_b, right_ref)
        high_out[...], low_out[...] = halves(times(halves(tile_ref[...]), halves(right_ref[...])))


def last_kernel(order, spread, other_a, other_b, first_left, high_ref, low_ref, out_ref, left_ref, result_ref, sems):
    core, mine = place_of_rows(spread)
    step = order // 2
    parts = (slice(0, step), slice(step, order))

    def finish(columns):
        copies = []
        for turn in range(2):
            result_ref[turn] = columns(turn)
            target = out_ref.at[:, pl.ds(turn * step, step)]
            copies.append(pltpu.make_async_copy(result_ref.at[turn], target, sems.at[turn]))
            copies[-1].start()
        for copy in copies:
            copy.wait()

    @pl.when(core != 0)
    def _():
        count = step // LANE
        blocks = [other_a[slot * LANE : (slot + 1) * LANE, :] for slot in range(count * count)]
        rows = [jnp.concatenate(blocks[row * count : (row + 1) * count], 1) for row in range(count)]
        joining = halves(jnp.concatenate(rows, 0))
        left = halves(first_left[...])
        left = [(left[0][:, part], left[1][:, part]) for part in parts]

        def columns(turn):
            own = high_ref[parts[turn], parts[turn]], low_ref[parts[turn], parts[turn]]
            return times(left[turn], own) + times(left[1 - turn], joining, turn == 0)

        finish(columns)

    @pl.when(core == 0)
    def _():
        fill_left(order, mine, other_a, other_b, left_ref)
        left = halves(left_ref[...])
        finish(lambda turn: times(left, (high_ref[:, parts[turn]], low_ref[:, parts[turn]])))


def call(kernel, shapes, scratch, *args, space=pltpu.VMEM):
    return pl.pallas_call(
        kernel,
        out_shape=[jax.ShapeDtypeStruct(shape[:2], *shape[2:] or (jnp.float32,)) for shape in shapes],
        out_specs=[pl.BlockSpec(memory_space=space) for shape in shapes],
        scratch_shapes=scratch,
        compiler_params=PARAMS,
    )(*args)


class Plan:
    def __init__(self, groups, dp, cuts):
        self.groups, self.dp, self.cuts = groups, dp, cuts
        self.bases = range(0, dp, QUAD)

    def index(self, z, x, core):
        return (z * self.cuts + x % self.cuts) * 2 + core

    def roots(self, base, x):
        return base + 1 + x % 2, base + 2 - x % 2

    def one_way(self, pairs):
        pairs = list(pairs)
        size = self.dp * self.cuts * 2
        return [(group * size + a, group * size + b) for group in range(self.groups) for a, b in pairs]

    def whole(self, edges, abreast=False):
        size = self.dp * self.cuts * 2
        target = dict(self.one_way(edges))

        def pair_up(other):
            for device in range(size * self.groups):
                chosen = other(device)
                if device not in target and chosen not in target and chosen < size * self.groups:
                    target[device], target[chosen] = chosen, device

        pair_up(lambda device: device ^ 1)
        if abreast and self.cuts % 2 == 0:
            pair_up(lambda device: device ^ 3)
        pair_up(lambda device: (device + size) % (2 * size) + device // (2 * size) * 2 * size)
        return sorted(target.items())

    def swaps(self, pairs):
        return self.whole([edge for a, b in pairs for edge in ((a, b), (b, a))])

    def chains(self, pairs):
        to, of = dict(pairs), {b: a for a, b in pairs}
        edges = list(pairs)
        for device in sorted(set(to) | set(of)):
            if device in of and device not in to:
                if device ^ 1 in of or device ^ 1 not in to:
                    return self.swaps(pairs)
                edges.append((device, device ^ 1))
            elif device in to and device not in of and (device ^ 1 in to or device ^ 1 not in of):
                return self.swaps(pairs)
        return self.whole(edges)

    def loops(self, pairs):
        edges = []
        for a, b in pairs:
            if (a ^ 1, b ^ 1) in pairs:
                edges += [(a, b), (b, a)]
            else:
                edges += [(a, b), (b, b ^ 1), (b ^ 1, a ^ 1), (a ^ 1, a)]
        return self.whole(edges)

    def across(self, bit):
        return self.one_way(
            (self.index(z, x, core), self.index(z ^ bit, x, core))
            for z in range(self.dp)
            for x in range(self.cuts)
            for core in range(2)
        )

    def collect(self):
        far, near, outer = [], [], []
        for x in range(self.cuts):
            for base in self.bases:
                left, right = self.roots(base, x)
                left_root, right_root = self.index(left, x, 1), self.index(right, x, 0)
                right_far, left_far = self.index(left ^ 1, x, 1), self.index(right ^ 1, x, 0)
                far += [(left_far, left_root), (left_root, right_far), (right_far, right_root), (right_root, left_far)]
                near.append((self.index(right, x, 0), left_root))
                outer.append((self.index(left ^ 1, x, 0), left_root))
                outer.append((self.index(right ^ 1, x, 1), right_root))
        return self.whole(far, True), self.swaps(near), self.loops(outer)

    def spread(self):
        hops = [[] for turn in range(1, self.cuts)]
        direct = []
        relays = [[] for turn in range(1, self.cuts)]
        for x in range(self.cuts):
            for base in self.bases:
                left, right = self.roots(base, x)
                right_root, middle = self.index(right, x, 0), self.index(left, x, 0)
                hops[0].append((right_root, middle))
                left_root = self.index(left, x, 1)
                direct.append((right_root, self.index(right ^ 1, x, 0)))
                direct.append((left_root, self.index(left ^ 1, x, 1)))
                relays[0].append((middle, self.index(left ^ 1, x, 0)))
                if x // 2 != base // QUAD:
                    continue
                for turn in range(1, self.cuts):
                    abreast = self.index(left, x + turn, 1)
                    hops[turn - 1].append((left_root, abreast))
                    relays[turn - 1].append((abreast, self.index(left ^ 1, x + turn, 1)))
        return [self.chains(pairs) for pairs in hops], self.loops(direct), [self.loops(pairs) for pairs in relays]

    def turn(self):
        z, x, core = (lax.axis_index(name) for name in AXES[1:])
        turn = lax.rem(x + self.cuts - lax.div(z, 2), self.cuts)
        return jnp.where(lax.rem(z, QUAD) == 1 + lax.rem(x, 2), 0, jnp.maximum(turn - 1, 0))

    def which(self):
        z, x, core = (lax.axis_index(name) for name in AXES[1:])
        zq, middle = lax.rem(z, QUAD), is_middle()
        block = lax.div(z, 2)
        turn = lax.rem(x + self.cuts - block, self.cuts)
        direct = 2 * self.cuts - 1
        left = jnp.where(middle, turn, jnp.where(turn == 0, direct, self.cuts - 1 + turn))
        right_root = 2 - lax.rem(x, 2)
        right = jnp.where(
            zq == right_root, 0, jnp.where(middle, 1, jnp.where((zq ^ 1) == right_root, direct, self.cuts))
        )
        return jnp.where(core == 1, left, right)


def is_middle():
    zq = lax.rem(lax.axis_index("dp"), QUAD)
    return jnp.logical_or(zq == 1, zq == 2)


def rows_core():
    zq = lax.rem(lax.axis_index("dp"), QUAD)
    left = 1 + lax.rem(lax.axis_index("cuts"), 2)
    return jnp.where(is_middle(), zq != left, (zq ^ 1) == left).astype(jnp.int32)


def swap_cores(array):
    return lax.ppermute(array, "grad", [(0, 1), (1, 0)])


def per_device(acts, outgrads, grads):
    groups, dp, cuts, cores = (lax.axis_size(name) for name in AXES)
    tok_rows, order = acts.shape[1:]
    dev_count = dp * cores
    spread = dev_count // cuts
    plan = Plan(groups, dp, cuts)
    split, rest = part_rows(order)
    shape = (split + rest, LANE)
    acts, outgrads, grads = acts[0], outgrads[0], grads[0]

    core = lax.axis_index("grad")
    (sent,) = call(cov_kernel, [shape], [], jnp.where(core == 0, outgrads, acts))
    (kept,) = call(cov_kernel, [shape], [], jnp.where(core == 0, acts, outgrads))
    other_rows = swap_cores(grads)
    chip, outer = call(chip_kernel, [shape] * 2, [], kept, swap_cores(sent), grads)
    bit = QUAD
    while bit < dp:
        chip = chip + lax.ppermute(chip, AXES, plan.across(bit))
        outer = jnp.where(is_middle(), outer, chip)
        bit *= 2
    far, near, outward = plan.collect()
    sums = [
        lax.ppermute(outer, AXES, outward),
        lax.ppermute(chip, AXES, near),
        lax.ppermute(outer, AXES, far),
        swap_cores(chip),
    ]
    scale = 1.0 / (tok_rows * dev_count)
    square_scratch = pltpu.VMEM((order, order), jnp.float32)
    gathered = (2 * grads.size // LANE, LANE)
    *inverse, direct, outer_rows = call(
        functools.partial(inverse_kernel, scale, order),
        [(split, LANE), (rest, LANE), shape, gathered],
        [square_scratch, pltpu.VMEM(shape, jnp.float32)],
        *sums,
        grads,
        other_rows,
    )

    hops, outward, relays = plan.spread()
    hopped = [[lax.ppermute(inverse[0], AXES, pairs) for pairs in hops]]
    direct = lax.ppermute(direct, AXES, outward)
    hopped.append([lax.ppermute(inverse[1], AXES, pairs) for pairs in hops])
    relayed = [[lax.ppermute(array, AXES, pairs) for array, pairs in zip(arrays, relays)] for arrays in hopped]
    relayed[1], direct = lax.optimization_barrier((relayed[1], direct))
    arrived = [
        arrays[0] if cuts == 2 else call(functools.partial(choose_kernel, plan.turn, 0), [arrays[0].shape], [], *arrays)[0]
        for arrays in relayed
    ]
    own = []
    for part, start in ((0, 0), (1, split)):
        own += call(
            functools.partial(choose_kernel, plan.which, start),
            [inverse[part].shape],
            [],
            inverse[part],
            *hopped[part],
            *relayed[part],
            direct,
        )
    other_a, other_b = map(swap_cores, own)
    left_scratch = pltpu.VMEM((LANE, order), jnp.float32)
    first = call(
        functools.partial(first_kernel, order, spread),
        [(LANE, order), (order, order, jnp.bfloat16), (order, order, jnp.bfloat16)],
        [left_scratch, square_scratch, square_scratch],
        *own,
        other_b,
        grads,
        other_rows,
        outer_rows,
        swap_cores(outer_rows),
        direct,
        *arrived,
        swap_cores(arrived[1]),
    )
    (out,) = call(
        functools.partial(last_kernel, order, spread),
        [grads.shape],
        [
            left_scratch,
            pltpu.VMEM((2, LANE, order // 2), jnp.float32),
            pltpu.SemaphoreType.DMA((2,)),
        ],
        other_a,
        other_b,
        *first,
        space=pl.ANY,
    )
    return out[None]


def solution(mesh):
    in_specs = (
        P(None, ("groups", "dp", "grad"), "cuts"),
        P(None, ("groups", "dp", "grad"), "cuts"),
        P("groups", ("dp", "grad"), "cuts"),
    )
    out_specs = P("groups", ("dp", "grad"), "cuts")
    return jax.shard_map(
        per_device, mesh=mesh, in_specs=in_specs, out_specs=out_specs, check_vma=False
    )
```

```python
import functools
import jax
import jax.numpy as jnp
from jax import lax
from jax.experimental import pallas as pl
from jax.experimental.pallas import tpu as pltpu
from jax.sharding import PartitionSpec as P

ITERS = 4
DAMPING = 0.5
START = 1.9
LANE = 128
QUAD = 4
AXES = ("groups", "dp", "cuts", "grad")
PARAMS = pltpu.CompilerParams(vmem_limit_bytes=48 * 1024 * 1024)


def half_blocks(order, half):
    count = order // LANE // 2
    own = range(half * count, (half + 1) * count)
    return [(i, j) for i in own for j in own if i < j], [(i, i + 1) for i in own[::2]]


def joining_blocks(order):
    count = order // LANE
    return [(i, j) for i in range(count // 2) for j in range(count // 2, count)]


def part_rows(order):
    above, pairs = half_blocks(order, 0)
    own = (len(above) + len(pairs)) * LANE + -(-len(pairs) // 8) * 8
    return len(joining_blocks(order)) * LANE, 2 * own


def own_start(order, half, second):
    rows = part_rows(order)[1] // 2
    return (half ^ second) * rows if isinstance(second, int) else pl.multiple_of((half ^ second) * rows, 8)


def places():
    rows = lax.broadcasted_iota(jnp.int32, (LANE, LANE), 0)
    cols = lax.broadcasted_iota(jnp.int32, (LANE, LANE), 1)
    return rows, cols


def pack(block, order, a_ref, b_ref, second=0):
    rows, cols = places()
    for slot, (i, j) in enumerate(joining_blocks(order)):
        a_ref[slot * LANE : (slot + 1) * LANE, :] = block(i, j)
    for half in range(2):
        top = own_start(order, half, second)
        above, pairs = half_blocks(order, half)
        values = [block(i, j) for i, j in above]
        values += [jnp.where(rows <= cols, block(i, i), block(j, j)) for i, j in pairs]
        last = [jnp.sum(jnp.where(rows == cols, block(j, j), 0.0), axis=0, keepdims=True) for _, j in pairs]
        values.append(jnp.concatenate(last + [jnp.zeros((-len(pairs) % 8, LANE), jnp.float32)], 0))
        for value in values:
            b_ref[pl.ds(top, value.shape[0]), :] = value
            top += value.shape[0]


def unpack(a_piece, b_piece, order, out_ref, second=0, scale=1.0, shift=0.0):
    for slot, (i, j) in enumerate(joining_blocks(order)):
        value = a_piece(slot * LANE, LANE) * scale
        put_block(out_ref, i, j, value)
        put_block(out_ref, j, i, value.T)
    unpack_own(b_piece, order, out_ref, second, scale, shift)


def put_block(out_ref, i, j, value):
    out_ref[i * LANE : (i + 1) * LANE, j * LANE : (j + 1) * LANE] = value


def unpack_own(b_piece, order, out_ref, second=0, scale=1.0, shift=0.0):
    rows, cols = places()
    damping = jnp.where(rows == cols, shift, 0.0)
    for half in range(2):
        top = own_start(order, half, second)
        above, pairs = half_blocks(order, half)
        for i, j in above:
            value = b_piece(top, LANE) * scale
            put_block(out_ref, i, j, value)
            put_block(out_ref, j, i, value.T)
            top += LANE
        last = b_piece(top + len(pairs) * LANE, -(-len(pairs) // 8) * 8)
        for k, (i, j) in enumerate(pairs):
            both = b_piece(top, LANE)
            turned = both.T
            put_block(out_ref, i, i, jnp.where(rows <= cols, both, turned) * scale + damping)
            after = jnp.where(rows > cols, both, jnp.where(rows < cols, turned, last[k : k + 1, :]))
            put_block(out_ref, j, j, after * scale + damping)
            top += LANE


def stored_block(a_ref, b_ref, order, i, j, second):
    if i > j:
        return stored_block(a_ref, b_ref, order, j, i, second).T
    if (i, j) in joining_blocks(order):
        start = joining_blocks(order).index((i, j)) * LANE
        return a_ref[start : start + LANE, :]
    half = i // (order // LANE // 2)
    above, pairs = half_blocks(order, half)
    top = own_start(order, half, second)
    if i < j:
        return b_ref[pl.ds(top + above.index((i, j)) * LANE, LANE), :]
    place = next(k for k, pair in enumerate(pairs) if i in pair)
    both = b_ref[pl.ds(top + (len(above) + place) * LANE, LANE), :]
    rows, cols = places()
    if i == pairs[place][0]:
        return jnp.where(rows <= cols, both, both.T)
    last = b_ref[pl.ds(top + (len(above) + len(pairs)) * LANE, -(-len(pairs) // 8) * 8), :]
    return jnp.where(rows > cols, both, jnp.where(rows < cols, both.T, last[place : place + 1, :]))


def halves(value):
    high = value.astype(jnp.bfloat16)
    return high, (value - high.astype(jnp.float32)).astype(jnp.bfloat16)


def times(left, right, turned=False):
    dims = (((1,), (1 if turned else 0,)), ((), ()))
    dot = functools.partial(lax.dot_general, dimension_numbers=dims, preferred_element_type=jnp.float32)
    rows = left[0].shape[0]
    both = dot(jnp.concatenate(left, 0), right[0])
    return both[:rows] + (dot(left[0], right[1]) + both[rows:])


def rows_of(pair, start, stop):
    return pair[0][start:stop, :], pair[1][start:stop, :]


def upper_times(left, right):
    middle = left[0].shape[0] // 2
    top = times(rows_of(left, 0, middle), right)
    corner = times(rows_of(left, middle, 2 * middle), (right[0][:, middle:], right[1][:, middle:]))
    return top, corner


def upper_square(value):
    dot = functools.partial(jnp.dot, preferred_element_type=jnp.float32)
    high, low = value
    middle = high.shape[0] // 2
    mixed = dot(high, low)
    top = dot(high[:middle], high) + (mixed[:middle] + mixed[:, :middle].T)
    corner = mixed[middle:, middle:]
    return top, dot(high[middle:], high[:, middle:]) + (corner + corner.T)


def whole(top, corner):
    middle = corner.shape[0]
    return jnp.concatenate([top, jnp.concatenate([top[:, middle:].T, corner], 1)], 0)


def cov_kernel(x_ref, out_ref):
    x = x_ref[...]
    order = x.shape[1]
    split = part_rows(order)[0]
    total = lax.dot_general(x, x, (((0,), (0,)), ((), ())), preferred_element_type=jnp.float32)
    pack(block_of(total), order, out_ref.at[:split], out_ref.at[split:])


def block_of(value):
    return lambda i, j: value[i * LANE : (i + 1) * LANE, j * LANE : (j + 1) * LANE]


def put_rows(out_ref, start, rows_ref):
    rows, columns = rows_ref.shape
    for column in range(columns // LANE):
        out_ref[start : start + rows, :] = rows_ref[:, column * LANE : (column + 1) * LANE]
        start += rows


def chip_kernel(kept_ref, other_ref, rows_ref, chip_ref, outer_ref):
    chip_ref[...] = kept_ref[...] + other_ref[...]

    @pl.when(is_middle())
    def _():
        used = rows_ref.shape[0] * rows_ref.shape[1] // LANE
        put_rows(outer_ref, 0, rows_ref)
        outer_ref[used:, :] = jnp.zeros((outer_ref.shape[0] - used, LANE), jnp.float32)

    @pl.when(jnp.logical_not(is_middle()))
    def _():
        outer_ref[...] = chip_ref[...]


def inverse_kernel(scale, order, *refs):
    *sums, own_rows_ref, other_rows_ref, a_ref, b_ref, direct_ref, gathered_ref, factor_ref, rows_ref = refs
    split = part_rows(order)[0]

    def piece(start, size):
        total = sums[0][start : start + size, :]
        for ref in sums[1:]:
            total = total + ref[start : start + size, :]
        return total

    unpack(piece, lambda start, size: piece(split + start, size), order, factor_ref, 0, scale, DAMPING)
    factor = factor_ref[...]
    bound = jnp.max(jnp.sum(jnp.abs(factor), axis=0, keepdims=True), axis=1, keepdims=True) + 1e-06
    start = START / bound
    rows = lax.broadcasted_iota(jnp.int32, (order, order), 0)
    cols = lax.broadcasted_iota(jnp.int32, (order, order), 1)
    eye = jnp.where(rows == cols, 1.0, 0.0)
    total = eye - start * factor
    power_halves = halves(total)
    middle = order // 2
    for step in range(1, ITERS):
        power = whole(*upper_square(power_halves))
        power_halves = halves(power)
        top, corner = upper_times(halves(total), power_halves)
        known = total + power
        top, corner = top + known[:middle], corner + known[middle:, middle:]
        if step < ITERS - 1:
            total = whole(top, corner)

    def block(i, j):
        if i < middle // LANE:
            value = block_of(top)(i, j)
        else:
            value = block_of(corner)(i - middle // LANE, j - middle // LANE)
        return start * (value + block_of(eye)(i, j))

    @pl.when(is_middle())
    def _():
        pack(block, order, a_ref, b_ref, lax.rem(lax.axis_index("cuts"), 2))
        direct_ref[:split, :] = a_ref[...]
        direct_ref[split:, :] = b_ref[...]

    @pl.when(jnp.logical_not(is_middle()))
    def _():
        core = lax.axis_index("grad")
        size = own_rows_ref.shape[0] * own_rows_ref.shape[1] // LANE
        rows_ref[2 * size :, :] = jnp.zeros((rows_ref.shape[0] - 2 * size, LANE), jnp.float32)
        for mine in range(2):

            @pl.when(core == mine)
            def _():
                put_rows(rows_ref, mine * size, own_rows_ref)
                put_rows(rows_ref, (1 - mine) * size, other_rows_ref)

            @pl.when(rows_core() == mine)
            def _():
                outer, far = sums[0][:size, :], sums[2][:size, :]
                gathered_ref[:size, :] = outer if mine else far
                gathered_ref[size:, :] = far if mine else outer

        a_ref[...] = rows_ref[:split, :]
        b_ref[...] = rows_ref[split:, :]
        direct_ref[...] = rows_ref[...]


def choose_kernel(which, start, *refs):
    *arrays, out_ref = refs
    index = which()
    rows = out_ref.shape[0]
    for place, ref in enumerate(arrays):
        first = start if place == len(arrays) - 1 else 0

        @pl.when(index == place)
        def _():
            out_ref[...] = ref[first : first + rows, :]


def fill_left(order, mine, a_ref, b_ref, left_ref):
    second = lax.rem(lax.div(lax.axis_index("dp"), 2), 2)
    for row in range(order // LANE):

        @pl.when(mine == row)
        def _():
            for column in range(order // LANE):
                block = stored_block(a_ref, b_ref, order, row, column, second)
                left_ref[:, column * LANE : (column + 1) * LANE] = block


def fill_right(order, a_ref, b_ref, right_ref):
    unpack(
        lambda start, size: a_ref[pl.ds(start, size), :],
        lambda start, size: b_ref[pl.ds(start, size), :],
        order,
        right_ref,
        lax.rem(lax.axis_index("cuts"), 2),
    )


def place_of_rows(spread):
    core = lax.axis_index("grad")
    return core, lax.rem(lax.axis_index("dp") * lax.axis_size("grad") + core, spread)


def first_kernel(order, spread, own_a, own_b, other_b, *refs):
    own_rows_ref, other_rows_ref, outer_ref, outer_other_ref, direct_ref, relayed_a, relayed_b, relayed_other, *refs = refs
    left_out, high_out, low_out, left_ref, right_ref, tile_ref = refs
    core, mine = place_of_rows(spread)
    rows_dev = own_rows_ref.shape[0]

    def place(position):
        return pl.ds(pl.multiple_of(position * rows_dev, rows_dev), rows_dev)

    tile_ref[place(mine), :] = own_rows_ref[...]
    tile_ref[place(mine ^ 1), :] = other_rows_ref[...]
    here = core == rows_core()
    cases = (
        (False, True, (outer_ref,)),
        (False, False, (outer_other_ref,)),
        (True, True, (direct_ref.at[: relayed_a.shape[0]], relayed_other)),
        (True, False, (relayed_a, relayed_b)),
    )
    for middle, arrived, parts in cases:

        @pl.when(jnp.logical_and(is_middle() == middle, here == arrived))
        def _():
            start, part = 0, 0
            for turn in range(2):
                for column in range(order // LANE):
                    if start == parts[part].shape[0]:
                        start, part = 0, part + 1
                    tile_ref[place((mine // 2 ^ 1) * 2 + turn), column * LANE : (column + 1) * LANE] = parts[part][
                        start : start + rows_dev, :
                    ]
                    start += rows_dev

    @pl.when(core != 0)
    def _():
        fill_left(order, mine, own_a, own_b, left_ref)
        left_out[...] = times(halves(left_ref[...]), halves(tile_ref[...]))
        second = lax.rem(lax.axis_index("cuts"), 2)
        unpack_own(lambda start, size: other_b[pl.ds(start, size), :], order, right_ref, second)
        for own in (slice(0, order // 2), slice(order // 2, order)):
            high_out[own, own], low_out[own, own] = halves(right_ref[own, own])

    @pl.when(core == 0)
    def _():
        fill_right(order, own_a, own_b, right_ref)
        high_out[...], low_out[...] = halves(times(halves(tile_ref[...]), halves(right_ref[...])))


def last_kernel(order, spread, other_a, other_b, first_left, high_ref, low_ref, out_ref, left_ref, result_ref, sems):
    core, mine = place_of_rows(spread)
    step = order // 2
    parts = (slice(0, step), slice(step, order))

    def finish(columns):
        copies = []
        for turn in range(2):
            result_ref[turn] = columns(turn)
            target = out_ref.at[:, pl.ds(turn * step, step)]
            copies.append(pltpu.make_async_copy(result_ref.at[turn], target, sems.at[turn]))
            copies[-1].start()
        for copy in copies:
            copy.wait()

    @pl.when(core != 0)
    def _():
        count = step // LANE
        blocks = [other_a[slot * LANE : (slot + 1) * LANE, :] for slot in range(count * count)]
        rows = [jnp.concatenate(blocks[row * count : (row + 1) * count], 1) for row in range(count)]
        joining = halves(jnp.concatenate(rows, 0))
        left = halves(first_left[...])
        left = [(left[0][:, part], left[1][:, part]) for part in parts]

        def columns(turn):
            own = high_ref[parts[turn], parts[turn]], low_ref[parts[turn], parts[turn]]
            return times(left[turn], own) + times(left[1 - turn], joining, turn == 0)

        finish(columns)

    @pl.when(core == 0)
    def _():
        fill_left(order, mine, other_a, other_b, left_ref)
        left = halves(left_ref[...])
        finish(lambda turn: times(left, (high_ref[:, parts[turn]], low_ref[:, parts[turn]])))


def call(kernel, shapes, scratch, *args, space=pltpu.VMEM):
    return pl.pallas_call(
        kernel,
        out_shape=[jax.ShapeDtypeStruct(shape[:2], *shape[2:] or (jnp.float32,)) for shape in shapes],
        out_specs=[pl.BlockSpec(memory_space=space) for shape in shapes],
        scratch_shapes=scratch,
        compiler_params=PARAMS,
    )(*args)


class Plan:
    def __init__(self, groups, dp, cuts):
        self.groups, self.dp, self.cuts = groups, dp, cuts
        self.bases = range(0, dp, QUAD)

    def index(self, z, x, core):
        return (z * self.cuts + x % self.cuts) * 2 + core

    def roots(self, base, x):
        return base + 1 + x % 2, base + 2 - x % 2

    def one_way(self, pairs):
        pairs = list(pairs)
        size = self.dp * self.cuts * 2
        return [(group * size + a, group * size + b) for group in range(self.groups) for a, b in pairs]

    def whole(self, edges, abreast=False):
        size = self.dp * self.cuts * 2
        target = dict(self.one_way(edges))

        def pair_up(other):
            for device in range(size * self.groups):
                chosen = other(device)
                if device not in target and chosen not in target and chosen < size * self.groups:
                    target[device], target[chosen] = chosen, device

        pair_up(lambda device: device ^ 1)
        if abreast and self.cuts % 2 == 0:
            pair_up(lambda device: device ^ 3)
        pair_up(lambda device: (device + size) % (2 * size) + device // (2 * size) * 2 * size)
        return sorted(target.items())

    def swaps(self, pairs):
        return self.whole([edge for a, b in pairs for edge in ((a, b), (b, a))])

    def chains(self, pairs):
        to, of = dict(pairs), {b: a for a, b in pairs}
        edges = list(pairs)
        for device in sorted(set(to) | set(of)):
            if device in of and device not in to:
                if device ^ 1 in of or device ^ 1 not in to:
                    return self.swaps(pairs)
                edges.append((device, device ^ 1))
            elif device in to and device not in of and (device ^ 1 in to or device ^ 1 not in of):
                return self.swaps(pairs)
        return self.whole(edges)

    def loops(self, pairs):
        edges = []
        for a, b in pairs:
            if (a ^ 1, b ^ 1) in pairs:
                edges += [(a, b), (b, a)]
            else:
                edges += [(a, b), (b, b ^ 1), (b ^ 1, a ^ 1), (a ^ 1, a)]
        return self.whole(edges)

    def across(self, bit):
        return self.one_way(
            (self.index(z, x, core), self.index(z ^ bit, x, core))
            for z in range(self.dp)
            for x in range(self.cuts)
            for core in range(2)
        )

    def collect(self):
        far, near, outer = [], [], []
        for x in range(self.cuts):
            for base in self.bases:
                left, right = self.roots(base, x)
                left_root, right_root = self.index(left, x, 1), self.index(right, x, 0)
                right_far, left_far = self.index(left ^ 1, x, 1), self.index(right ^ 1, x, 0)
                far += [(left_far, left_root), (left_root, right_far), (right_far, right_root), (right_root, left_far)]
                near.append((self.index(right, x, 0), left_root))
                outer.append((self.index(left ^ 1, x, 0), left_root))
                outer.append((self.index(right ^ 1, x, 1), right_root))
        return self.whole(far, True), self.swaps(near), self.loops(outer)

    def spread(self):
        hops = [[] for turn in range(1, self.cuts)]
        direct = []
        relays = [[] for turn in range(1, self.cuts)]
        for x in range(self.cuts):
            for base in self.bases:
                left, right = self.roots(base, x)
                right_root, middle = self.index(right, x, 0), self.index(left, x, 0)
                hops[0].append((right_root, middle))
                left_root = self.index(left, x, 1)
                direct.append((right_root, self.index(right ^ 1, x, 0)))
                direct.append((left_root, self.index(left ^ 1, x, 1)))
                relays[0].append((middle, self.index(left ^ 1, x, 0)))
                if x // 2 != base // QUAD:
                    continue
                for turn in range(1, self.cuts):
                    abreast = self.index(left, x + turn, 1)
                    hops[turn - 1].append((left_root, abreast))
                    relays[turn - 1].append((abreast, self.index(left ^ 1, x + turn, 1)))
        return (
            [(self.swaps(pairs), self.chains(pairs)) for pairs in hops],
            self.loops(direct),
            [self.loops(pairs) for pairs in relays],
        )

    def turn(self):
        z, x, core = (lax.axis_index(name) for name in AXES[1:])
        turn = lax.rem(x + self.cuts - lax.div(z, 2), self.cuts)
        return jnp.where(lax.rem(z, QUAD) == 1 + lax.rem(x, 2), 0, jnp.maximum(turn - 1, 0))

    def which(self):
        z, x, core = (lax.axis_index(name) for name in AXES[1:])
        zq, middle = lax.rem(z, QUAD), is_middle()
        block = lax.div(z, 2)
        turn = lax.rem(x + self.cuts - block, self.cuts)
        direct = 2 * self.cuts - 1
        left = jnp.where(middle, turn, jnp.where(turn == 0, direct, self.cuts - 1 + turn))
        right_root = 2 - lax.rem(x, 2)
        right = jnp.where(
            zq == right_root, 0, jnp.where(middle, 1, jnp.where((zq ^ 1) == right_root, direct, self.cuts))
        )
        return jnp.where(core == 1, left, right)


def is_middle():
    zq = lax.rem(lax.axis_index("dp"), QUAD)
    return jnp.logical_or(zq == 1, zq == 2)


def rows_core():
    zq = lax.rem(lax.axis_index("dp"), QUAD)
    left = 1 + lax.rem(lax.axis_index("cuts"), 2)
    return jnp.where(is_middle(), zq != left, (zq ^ 1) == left).astype(jnp.int32)


def swap_cores(array):
    return lax.ppermute(array, "grad", [(0, 1), (1, 0)])


def per_device(acts, outgrads, grads):
    groups, dp, cuts, cores = (lax.axis_size(name) for name in AXES)
    tok_rows, order = acts.shape[1:]
    dev_count = dp * cores
    spread = dev_count // cuts
    plan = Plan(groups, dp, cuts)
    split, rest = part_rows(order)
    shape = (split + rest, LANE)
    acts, outgrads, grads = acts[0], outgrads[0], grads[0]

    core = lax.axis_index("grad")
    (sent,) = call(cov_kernel, [shape], [], jnp.where(core == 0, outgrads, acts))
    (kept,) = call(cov_kernel, [shape], [], jnp.where(core == 0, acts, outgrads))
    other_rows = swap_cores(grads)
    chip, outer = call(chip_kernel, [shape] * 2, [], kept, swap_cores(sent), grads)
    bit = QUAD
    while bit < dp:
        chip = chip + lax.ppermute(chip, AXES, plan.across(bit))
        outer = jnp.where(is_middle(), outer, chip)
        bit *= 2
    far, near, outward = plan.collect()
    sums = [
        lax.ppermute(outer, AXES, outward),
        lax.ppermute(chip, AXES, near),
        lax.ppermute(outer, AXES, far),
        swap_cores(chip),
    ]
    scale = 1.0 / (tok_rows * dev_count)
    square_scratch = pltpu.VMEM((order, order), jnp.float32)
    gathered = (2 * grads.size // LANE, LANE)
    *inverse, direct, outer_rows = call(
        functools.partial(inverse_kernel, scale, order),
        [(split, LANE), (rest, LANE), shape, gathered],
        [square_scratch, pltpu.VMEM(shape, jnp.float32)],
        *sums,
        grads,
        other_rows,
    )

    hops, outward, relays = plan.spread()
    hopped = [[lax.ppermute(inverse[0], AXES, pairs) for pairs, _ in hops]]
    direct = lax.ppermute(direct, AXES, outward)
    hopped.append([lax.ppermute(inverse[1], AXES, pairs) for _, pairs in hops])
    relayed = [[lax.ppermute(array, AXES, pairs) for array, pairs in zip(arrays, relays)] for arrays in hopped]
    relayed[1], direct = lax.optimization_barrier((relayed[1], direct))
    arrived = [
        arrays[0] if cuts == 2 else call(functools.partial(choose_kernel, plan.turn, 0), [arrays[0].shape], [], *arrays)[0]
        for arrays in relayed
    ]
    own = []
    for part, start in ((0, 0), (1, split)):
        own += call(
            functools.partial(choose_kernel, plan.which, start),
            [inverse[part].shape],
            [],
            inverse[part],
            *hopped[part],
            *relayed[part],
            direct,
        )
    other_a, other_b = map(swap_cores, own)
    left_scratch = pltpu.VMEM((LANE, order), jnp.float32)
    first = call(
        functools.partial(first_kernel, order, spread),
        [(LANE, order), (order, order, jnp.bfloat16), (order, order, jnp.bfloat16)],
        [left_scratch, square_scratch, square_scratch],
        *own,
        other_b,
        grads,
        other_rows,
        outer_rows,
        swap_cores(outer_rows),
        direct,
        *arrived,
        swap_cores(arrived[1]),
    )
    (out,) = call(
        functools.partial(last_kernel, order, spread),
        [grads.shape],
        [
            left_scratch,
            pltpu.VMEM((2, LANE, order // 2), jnp.float32),
            pltpu.SemaphoreType.DMA((2,)),
        ],
        other_a,
        other_b,
        *first,
        space=pl.ANY,
    )
    return out[None]


def solution(mesh):
    in_specs = (
        P(None, ("groups", "dp", "grad"), "cuts"),
        P(None, ("groups", "dp", "grad"), "cuts"),
        P("groups", ("dp", "grad"), "cuts"),
    )
    out_specs = P("groups", ("dp", "grad"), "cuts")
    return jax.shard_map(
        per_device, mesh=mesh, in_specs=in_specs, out_specs=out_specs, check_vma=False
    )
```

```python
import functools
import jax
import jax.numpy as jnp
from jax import lax
from jax.experimental import pallas as pl
from jax.experimental.pallas import tpu as pltpu
from jax.sharding import PartitionSpec as P

ITERS = 4
DAMPING = 0.5
START = 1.9
LANE = 128
QUAD = 4
AXES = ("groups", "dp", "cuts", "grad")
PARAMS = pltpu.CompilerParams(vmem_limit_bytes=48 * 1024 * 1024)


def half_blocks(order, half):
    count = order // LANE // 2
    own = range(half * count, (half + 1) * count)
    return [(i, j) for i in own for j in own if i < j], [(i, i + 1) for i in own[::2]]


def joining_blocks(order):
    count = order // LANE
    return [(i, j) for i in range(count // 2) for j in range(count // 2, count)]


def part_rows(order):
    above, pairs = half_blocks(order, 0)
    own = (len(above) + len(pairs)) * LANE + -(-len(pairs) // 8) * 8
    return len(joining_blocks(order)) * LANE, 2 * own


def own_start(order, half, second):
    rows = part_rows(order)[1] // 2
    return (half ^ second) * rows if isinstance(second, int) else pl.multiple_of((half ^ second) * rows, 8)


def places():
    rows = lax.broadcasted_iota(jnp.int32, (LANE, LANE), 0)
    cols = lax.broadcasted_iota(jnp.int32, (LANE, LANE), 1)
    return rows, cols


def pack(block, order, a_ref, b_ref, second=0):
    rows, cols = places()
    for slot, (i, j) in enumerate(joining_blocks(order)):
        a_ref[slot * LANE : (slot + 1) * LANE, :] = block(i, j)
    for half in range(2):
        top = own_start(order, half, second)
        above, pairs = half_blocks(order, half)
        values = [block(i, j) for i, j in above]
        values += [jnp.where(rows <= cols, block(i, i), block(j, j)) for i, j in pairs]
        last = [jnp.sum(jnp.where(rows == cols, block(j, j), 0.0), axis=0, keepdims=True) for _, j in pairs]
        values.append(jnp.concatenate(last + [jnp.zeros((-len(pairs) % 8, LANE), jnp.float32)], 0))
        for value in values:
            b_ref[pl.ds(top, value.shape[0]), :] = value
            top += value.shape[0]


def unpack(a_piece, b_piece, order, out_ref, second=0, scale=1.0, shift=0.0):
    rows, cols = places()
    damping = jnp.where(rows == cols, shift, 0.0)

    def put(i, j, value):
        out_ref[i * LANE : (i + 1) * LANE, j * LANE : (j + 1) * LANE] = value

    def put_both(i, j, value):
        put(i, j, value)
        put(j, i, value.T)

    for slot, (i, j) in enumerate(joining_blocks(order)):
        put_both(i, j, a_piece(slot * LANE, LANE) * scale)
    for half in range(2):
        top = own_start(order, half, second)
        above, pairs = half_blocks(order, half)
        for i, j in above:
            put_both(i, j, b_piece(top, LANE) * scale)
            top += LANE
        last = b_piece(top + len(pairs) * LANE, -(-len(pairs) // 8) * 8)
        for k, (i, j) in enumerate(pairs):
            both = b_piece(top, LANE)
            turned = both.T
            put(i, i, jnp.where(rows <= cols, both, turned) * scale + damping)
            after = jnp.where(rows > cols, both, jnp.where(rows < cols, turned, last[k : k + 1, :]))
            put(j, j, after * scale + damping)
            top += LANE


def stored_block(a_ref, b_ref, order, i, j, second):
    if i > j:
        return stored_block(a_ref, b_ref, order, j, i, second).T
    if (i, j) in joining_blocks(order):
        start = joining_blocks(order).index((i, j)) * LANE
        return a_ref[start : start + LANE, :]
    half = i // (order // LANE // 2)
    above, pairs = half_blocks(order, half)
    top = own_start(order, half, second)
    if i < j:
        return b_ref[pl.ds(top + above.index((i, j)) * LANE, LANE), :]
    place = next(k for k, pair in enumerate(pairs) if i in pair)
    both = b_ref[pl.ds(top + (len(above) + place) * LANE, LANE), :]
    rows, cols = places()
    if i == pairs[place][0]:
        return jnp.where(rows <= cols, both, both.T)
    last = b_ref[pl.ds(top + (len(above) + len(pairs)) * LANE, -(-len(pairs) // 8) * 8), :]
    return jnp.where(rows > cols, both, jnp.where(rows < cols, both.T, last[place : place + 1, :]))


def halves(value):
    high = value.astype(jnp.bfloat16)
    return high, (value - high.astype(jnp.float32)).astype(jnp.bfloat16)


def times(left, right):
    dot = functools.partial(jnp.dot, preferred_element_type=jnp.float32)
    rows = left[0].shape[0]
    both = dot(jnp.concatenate(left, 0), right[0])
    return both[:rows] + (dot(left[0], right[1]) + both[rows:])


def rows_of(pair, start, stop):
    return pair[0][start:stop, :], pair[1][start:stop, :]


def upper_times(left, right):
    middle = left[0].shape[0] // 2
    top = times(rows_of(left, 0, middle), right)
    corner = times(rows_of(left, middle, 2 * middle), (right[0][:, middle:], right[1][:, middle:]))
    return top, corner


def upper_square(value):
    dot = functools.partial(jnp.dot, preferred_element_type=jnp.float32)
    high, low = value
    middle = high.shape[0] // 2
    mixed = dot(high, low)
    top = dot(high[:middle], high) + (mixed[:middle] + mixed[:, :middle].T)
    corner = mixed[middle:, middle:]
    return top, dot(high[middle:], high[:, middle:]) + (corner + corner.T)


def whole(top, corner):
    middle = corner.shape[0]
    return jnp.concatenate([top, jnp.concatenate([top[:, middle:].T, corner], 1)], 0)


def cov_kernel(x_ref, out_ref):
    x = x_ref[...]
    order = x.shape[1]
    split = part_rows(order)[0]
    total = lax.dot_general(x, x, (((0,), (0,)), ((), ())), preferred_element_type=jnp.float32)
    pack(block_of(total), order, out_ref.at[:split], out_ref.at[split:])


def block_of(value):
    return lambda i, j: value[i * LANE : (i + 1) * LANE, j * LANE : (j + 1) * LANE]


def put_rows(out_ref, start, rows_ref):
    rows, columns = rows_ref.shape
    for column in range(columns // LANE):
        out_ref[start : start + rows, :] = rows_ref[:, column * LANE : (column + 1) * LANE]
        start += rows


def chip_kernel(kept_ref, other_ref, rows_ref, chip_ref, outer_ref):
    chip_ref[...] = kept_ref[...] + other_ref[...]

    @pl.when(is_middle())
    def _():
        used = rows_ref.shape[0] * rows_ref.shape[1] // LANE
        put_rows(outer_ref, 0, rows_ref)
        outer_ref[used:, :] = jnp.zeros((outer_ref.shape[0] - used, LANE), jnp.float32)

    @pl.when(jnp.logical_not(is_middle()))
    def _():
        outer_ref[...] = chip_ref[...]


def inverse_kernel(scale, order, *refs):
    *sums, own_rows_ref, other_rows_ref, a_ref, b_ref, direct_ref, gathered_ref, factor_ref, rows_ref = refs
    split = part_rows(order)[0]

    def piece(start, size):
        total = sums[0][start : start + size, :]
        for ref in sums[1:]:
            total = total + ref[start : start + size, :]
        return total

    unpack(piece, lambda start, size: piece(split + start, size), order, factor_ref, 0, scale, DAMPING)
    factor = factor_ref[...]
    bound = jnp.max(jnp.sum(jnp.abs(factor), axis=0, keepdims=True), axis=1, keepdims=True) + 1e-06
    start = START / bound
    rows = lax.broadcasted_iota(jnp.int32, (order, order), 0)
    cols = lax.broadcasted_iota(jnp.int32, (order, order), 1)
    eye = jnp.where(rows == cols, 1.0, 0.0)
    total = eye - start * factor
    middle = order // 2
    square = whole(*upper_square(halves(total)))
    power = whole(*upper_square(halves(square)))
    total = total + 0.5 * (square + whole(*upper_square(halves(total + square))) - power)
    for step in range(2, ITERS):
        power_halves = halves(power)
        top, corner = upper_times(halves(total), power_halves)
        known = total + power
        top, corner = top + known[:middle], corner + known[middle:, middle:]
        if step < ITERS - 1:
            total = whole(top, corner)
            power = whole(*upper_square(power_halves))

    def block(i, j):
        if i < middle // LANE:
            value = block_of(top)(i, j)
        else:
            value = block_of(corner)(i - middle // LANE, j - middle // LANE)
        return start * (value + block_of(eye)(i, j))

    @pl.when(is_middle())
    def _():
        pack(block, order, a_ref, b_ref, lax.rem(lax.axis_index("cuts"), 2))
        direct_ref[:split, :] = a_ref[...]
        direct_ref[split:, :] = b_ref[...]

    @pl.when(jnp.logical_not(is_middle()))
    def _():
        core = lax.axis_index("grad")
        size = own_rows_ref.shape[0] * own_rows_ref.shape[1] // LANE
        rows_ref[2 * size :, :] = jnp.zeros((rows_ref.shape[0] - 2 * size, LANE), jnp.float32)
        for mine in range(2):

            @pl.when(core == mine)
            def _():
                put_rows(rows_ref, mine * size, own_rows_ref)
                put_rows(rows_ref, (1 - mine) * size, other_rows_ref)

            @pl.when(rows_core() == mine)
            def _():
                outer, far = sums[0][:size, :], sums[2][:size, :]
                gathered_ref[:size, :] = outer if mine else far
                gathered_ref[size:, :] = far if mine else outer

        a_ref[...] = rows_ref[:split, :]
        b_ref[...] = rows_ref[split:, :]
        direct_ref[...] = rows_ref[...]


def choose_kernel(which, start, *refs):
    *arrays, out_ref = refs
    index = which()
    rows = out_ref.shape[0]
    for place, ref in enumerate(arrays):
        first = start if place == len(arrays) - 1 else 0

        @pl.when(index == place)
        def _():
            out_ref[...] = ref[first : first + rows, :]


def fill_left(order, mine, a_ref, b_ref, left_ref):
    second = lax.rem(lax.div(lax.axis_index("dp"), 2), 2)
    for row in range(order // LANE):

        @pl.when(mine == row)
        def _():
            for column in range(order // LANE):
                block = stored_block(a_ref, b_ref, order, row, column, second)
                left_ref[:, column * LANE : (column + 1) * LANE] = block


def fill_right(order, a_ref, b_ref, right_ref):
    unpack(
        lambda start, size: a_ref[pl.ds(start, size), :],
        lambda start, size: b_ref[pl.ds(start, size), :],
        order,
        right_ref,
        lax.rem(lax.axis_index("cuts"), 2),
    )


def place_of_rows(spread):
    core = lax.axis_index("grad")
    return core, lax.rem(lax.axis_index("dp") * lax.axis_size("grad") + core, spread)


def first_kernel(order, spread, own_a, own_b, *refs):
    own_rows_ref, other_rows_ref, outer_ref, outer_other_ref, direct_ref, relayed_a, relayed_b, relayed_other, *refs = refs
    left_out, right_out, left_ref, right_ref, tile_ref = refs
    core, mine = place_of_rows(spread)
    rows_dev = own_rows_ref.shape[0]

    def place(position):
        return pl.ds(pl.multiple_of(position * rows_dev, rows_dev), rows_dev)

    tile_ref[place(mine), :] = own_rows_ref[...]
    tile_ref[place(mine ^ 1), :] = other_rows_ref[...]
    here = core == rows_core()
    cases = (
        (False, True, (outer_ref,)),
        (False, False, (outer_other_ref,)),
        (True, True, (direct_ref.at[: relayed_a.shape[0]], relayed_other)),
        (True, False, (relayed_a, relayed_b)),
    )
    for middle, arrived, parts in cases:

        @pl.when(jnp.logical_and(is_middle() == middle, here == arrived))
        def _():
            start, part = 0, 0
            for turn in range(2):
                for column in range(order // LANE):
                    if start == parts[part].shape[0]:
                        start, part = 0, part + 1
                    tile_ref[place((mine // 2 ^ 1) * 2 + turn), column * LANE : (column + 1) * LANE] = parts[part][
                        start : start + rows_dev, :
                    ]
                    start += rows_dev

    @pl.when(core != 0)
    def _():
        fill_left(order, mine, own_a, own_b, left_ref)
        left_out[...] = times(halves(left_ref[...]), halves(tile_ref[...]))

    @pl.when(core == 0)
    def _():
        fill_right(order, own_a, own_b, right_ref)
        right_out[...] = times(halves(tile_ref[...]), halves(right_ref[...]))


def last_kernel(order, spread, other_a, other_b, first_left, first_right, out_ref, *refs):
    left_ref, right_ref, result_ref, sems = refs
    core, mine = place_of_rows(spread)
    step = order // 2

    def finish(left, right_ref):
        copies = []
        for turn in range(2):
            columns = pl.ds(turn * step, step)
            result_ref[turn] = times(left, halves(right_ref[:, turn * step : (turn + 1) * step]))
            copies.append(pltpu.make_async_copy(result_ref.at[turn], out_ref.at[:, columns], sems.at[turn]))
            copies[-1].start()
        for copy in copies:
            copy.wait()

    @pl.when(core != 0)
    def _():
        fill_right(order, other_a, other_b, right_ref)
        finish(halves(first_left[...]), right_ref)

    @pl.when(core == 0)
    def _():
        fill_left(order, mine, other_a, other_b, left_ref)
        finish(halves(left_ref[...]), first_right)


def call(kernel, shapes, scratch, *args, space=pltpu.VMEM):
    return pl.pallas_call(
        kernel,
        out_shape=[jax.ShapeDtypeStruct(shape, jnp.float32) for shape in shapes],
        out_specs=[pl.BlockSpec(memory_space=space) for shape in shapes],
        scratch_shapes=scratch,
        compiler_params=PARAMS,
    )(*args)


class Plan:
    def __init__(self, groups, dp, cuts):
        self.groups, self.dp, self.cuts = groups, dp, cuts
        self.bases = range(0, dp, QUAD)

    def index(self, z, x, core):
        return (z * self.cuts + x % self.cuts) * 2 + core

    def roots(self, base, x):
        return base + 1 + x % 2, base + 2 - x % 2

    def one_way(self, pairs):
        pairs = list(pairs)
        size = self.dp * self.cuts * 2
        return [(group * size + a, group * size + b) for group in range(self.groups) for a, b in pairs]

    def whole(self, edges, abreast=False):
        size = self.dp * self.cuts * 2
        target = dict(self.one_way(edges))

        def pair_up(other):
            for device in range(size * self.groups):
                chosen = other(device)
                if device not in target and chosen not in target and chosen < size * self.groups:
                    target[device], target[chosen] = chosen, device

        pair_up(lambda device: device ^ 1)
        if abreast and self.cuts % 2 == 0:
            pair_up(lambda device: device ^ 3)
        pair_up(lambda device: (device + size) % (2 * size) + device // (2 * size) * 2 * size)
        return sorted(target.items())

    def swaps(self, pairs):
        return self.whole([edge for a, b in pairs for edge in ((a, b), (b, a))])

    def chains(self, pairs):
        to, of = dict(pairs), {b: a for a, b in pairs}
        edges = list(pairs)
        for device in sorted(set(to) | set(of)):
            if device in of and device not in to:
                if device ^ 1 in of or device ^ 1 not in to:
                    return self.swaps(pairs)
                edges.append((device, device ^ 1))
            elif device in to and device not in of and (device ^ 1 in to or device ^ 1 not in of):
                return self.swaps(pairs)
        return self.whole(edges)

    def loops(self, pairs):
        edges = []
        for a, b in pairs:
            if (a ^ 1, b ^ 1) in pairs:
                edges += [(a, b), (b, a)]
            else:
                edges += [(a, b), (b, b ^ 1), (b ^ 1, a ^ 1), (a ^ 1, a)]
        return self.whole(edges)

    def across(self, bit):
        return self.one_way(
            (self.index(z, x, core), self.index(z ^ bit, x, core))
            for z in range(self.dp)
            for x in range(self.cuts)
            for core in range(2)
        )

    def collect(self):
        far, near, outer = [], [], []
        for x in range(self.cuts):
            for base in self.bases:
                left, right = self.roots(base, x)
                left_root, right_root = self.index(left, x, 1), self.index(right, x, 0)
                right_far, left_far = self.index(left ^ 1, x, 1), self.index(right ^ 1, x, 0)
                far += [(left_far, left_root), (left_root, right_far), (right_far, right_root), (right_root, left_far)]
                near.append((self.index(right, x, 0), left_root))
                outer.append((self.index(left ^ 1, x, 0), left_root))
                outer.append((self.index(right ^ 1, x, 1), right_root))
        return self.whole(far, True), self.swaps(near), self.loops(outer)

    def spread(self):
        hops = [[] for turn in range(1, self.cuts)]
        direct = []
        relays = [[] for turn in range(1, self.cuts)]
        for x in range(self.cuts):
            for base in self.bases:
                left, right = self.roots(base, x)
                right_root, middle = self.index(right, x, 0), self.index(left, x, 0)
                hops[0].append((right_root, middle))
                left_root = self.index(left, x, 1)
                direct.append((right_root, self.index(right ^ 1, x, 0)))
                direct.append((left_root, self.index(left ^ 1, x, 1)))
                relays[0].append((middle, self.index(left ^ 1, x, 0)))
                if x // 2 != base // QUAD:
                    continue
                for turn in range(1, self.cuts):
                    abreast = self.index(left, x + turn, 1)
                    hops[turn - 1].append((left_root, abreast))
                    relays[turn - 1].append((abreast, self.index(left ^ 1, x + turn, 1)))
        return [self.chains(pairs) for pairs in hops], self.loops(direct), [self.loops(pairs) for pairs in relays]

    def turn(self):
        z, x, core = (lax.axis_index(name) for name in AXES[1:])
        turn = lax.rem(x + self.cuts - lax.div(z, 2), self.cuts)
        return jnp.where(lax.rem(z, QUAD) == 1 + lax.rem(x, 2), 0, jnp.maximum(turn - 1, 0))

    def which(self):
        z, x, core = (lax.axis_index(name) for name in AXES[1:])
        zq, middle = lax.rem(z, QUAD), is_middle()
        block = lax.div(z, 2)
        turn = lax.rem(x + self.cuts - block, self.cuts)
        direct = 2 * self.cuts - 1
        left = jnp.where(middle, turn, jnp.where(turn == 0, direct, self.cuts - 1 + turn))
        right_root = 2 - lax.rem(x, 2)
        right = jnp.where(
            zq == right_root, 0, jnp.where(middle, 1, jnp.where((zq ^ 1) == right_root, direct, self.cuts))
        )
        return jnp.where(core == 1, left, right)


def is_middle():
    zq = lax.rem(lax.axis_index("dp"), QUAD)
    return jnp.logical_or(zq == 1, zq == 2)


def rows_core():
    zq = lax.rem(lax.axis_index("dp"), QUAD)
    left = 1 + lax.rem(lax.axis_index("cuts"), 2)
    return jnp.where(is_middle(), zq != left, (zq ^ 1) == left).astype(jnp.int32)


def swap_cores(array):
    return lax.ppermute(array, "grad", [(0, 1), (1, 0)])


def per_device(acts, outgrads, grads):
    groups, dp, cuts, cores = (lax.axis_size(name) for name in AXES)
    tok_rows, order = acts.shape[1:]
    dev_count = dp * cores
    spread = dev_count // cuts
    plan = Plan(groups, dp, cuts)
    split, rest = part_rows(order)
    shape = (split + rest, LANE)
    acts, outgrads, grads = acts[0], outgrads[0], grads[0]

    core = lax.axis_index("grad")
    (sent,) = call(cov_kernel, [shape], [], jnp.where(core == 0, outgrads, acts))
    (kept,) = call(cov_kernel, [shape], [], jnp.where(core == 0, acts, outgrads))
    other_rows = swap_cores(grads)
    chip, outer = call(chip_kernel, [shape] * 2, [], kept, swap_cores(sent), grads)
    bit = QUAD
    while bit < dp:
        chip = chip + lax.ppermute(chip, AXES, plan.across(bit))
        outer = jnp.where(is_middle(), outer, chip)
        bit *= 2
    far, near, outward = plan.collect()
    sums = [
        lax.ppermute(outer, AXES, outward),
        lax.ppermute(chip, AXES, near),
        lax.ppermute(outer, AXES, far),
        swap_cores(chip),
    ]
    scale = 1.0 / (tok_rows * dev_count)
    square_scratch = pltpu.VMEM((order, order), jnp.float32)
    gathered = (2 * grads.size // LANE, LANE)
    *inverse, direct, outer_rows = call(
        functools.partial(inverse_kernel, scale, order),
        [(split, LANE), (rest, LANE), shape, gathered],
        [square_scratch, pltpu.VMEM(shape, jnp.float32)],
        *sums,
        grads,
        other_rows,
    )

    hops, outward, relays = plan.spread()
    hopped = [[lax.ppermute(inverse[0], AXES, pairs) for pairs in hops]]
    direct = lax.ppermute(direct, AXES, outward)
    hopped.append([lax.ppermute(inverse[1], AXES, pairs) for pairs in hops])
    relayed = [[lax.ppermute(array, AXES, pairs) for array, pairs in zip(arrays, relays)] for arrays in hopped]
    relayed[1], direct = lax.optimization_barrier((relayed[1], direct))
    arrived = [
        arrays[0] if cuts == 2 else call(functools.partial(choose_kernel, plan.turn, 0), [arrays[0].shape], [], *arrays)[0]
        for arrays in relayed
    ]
    own = []
    for part, start in ((0, 0), (1, split)):
        own += call(
            functools.partial(choose_kernel, plan.which, start),
            [inverse[part].shape],
            [],
            inverse[part],
            *hopped[part],
            *relayed[part],
            direct,
        )
    other_a, other_b = map(swap_cores, own)
    left_scratch = pltpu.VMEM((LANE, order), jnp.float32)
    first = call(
        functools.partial(first_kernel, order, spread),
        [(LANE, order), (order, order)],
        [left_scratch, square_scratch, square_scratch],
        *own,
        grads,
        other_rows,
        outer_rows,
        swap_cores(outer_rows),
        direct,
        *arrived,
        swap_cores(arrived[1]),
    )
    (out,) = call(
        functools.partial(last_kernel, order, spread),
        [grads.shape],
        [
            left_scratch,
            square_scratch,
            pltpu.VMEM((2, LANE, order // 2), jnp.float32),
            pltpu.SemaphoreType.DMA((2,)),
        ],
        other_a,
        other_b,
        *first,
        space=pl.ANY,
    )
    return out[None]


def solution(mesh):
    in_specs = (
        P(None, ("groups", "dp", "grad"), "cuts"),
        P(None, ("groups", "dp", "grad"), "cuts"),
        P("groups", ("dp", "grad"), "cuts"),
    )
    out_specs = P("groups", ("dp", "grad"), "cuts")
    return jax.shard_map(
        per_device, mesh=mesh, in_specs=in_specs, out_specs=out_specs, check_vma=False
    )
```

```python
import functools
import jax
import jax.numpy as jnp
from jax import lax
from jax.experimental import pallas as pl
from jax.experimental.pallas import tpu as pltpu
from jax.sharding import PartitionSpec as P

ITERS = 4
DAMPING = 0.5
START = 1.9
LANE = 128
QUAD = 4
AXES = ("groups", "dp", "cuts", "grad")
PARAMS = pltpu.CompilerParams(vmem_limit_bytes=48 * 1024 * 1024)


def half_blocks(order, half):
    count = order // LANE // 2
    own = range(half * count, (half + 1) * count)
    return [(i, j) for i in own for j in own if i < j], [(i, i + 1) for i in own[::2]]


def joining_blocks(order):
    count = order // LANE
    return [(i, j) for i in range(count // 2) for j in range(count // 2, count)]


def part_rows(order):
    above, pairs = half_blocks(order, 0)
    own = (len(above) + len(pairs)) * LANE + -(-len(pairs) // 8) * 8
    return len(joining_blocks(order)) * LANE, 2 * own


def own_start(order, half, second):
    rows = part_rows(order)[1] // 2
    return (half ^ second) * rows if isinstance(second, int) else pl.multiple_of((half ^ second) * rows, 8)


def places():
    rows = lax.broadcasted_iota(jnp.int32, (LANE, LANE), 0)
    cols = lax.broadcasted_iota(jnp.int32, (LANE, LANE), 1)
    return rows, cols


def pack(block, order, a_ref, b_ref, second=0):
    rows, cols = places()
    for slot, (i, j) in enumerate(joining_blocks(order)):
        a_ref[slot * LANE : (slot + 1) * LANE, :] = block(i, j)
    for half in range(2):
        top = own_start(order, half, second)
        above, pairs = half_blocks(order, half)
        values = [block(i, j) for i, j in above]
        values += [jnp.where(rows <= cols, block(i, i), block(j, j)) for i, j in pairs]
        last = [jnp.sum(jnp.where(rows == cols, block(j, j), 0.0), axis=0, keepdims=True) for _, j in pairs]
        values.append(jnp.concatenate(last + [jnp.zeros((-len(pairs) % 8, LANE), jnp.float32)], 0))
        for value in values:
            b_ref[pl.ds(top, value.shape[0]), :] = value
            top += value.shape[0]


def unpack(a_piece, b_piece, order, out_ref, second=0, scale=1.0, shift=0.0):
    for slot, (i, j) in enumerate(joining_blocks(order)):
        value = a_piece(slot * LANE, LANE) * scale
        put_block(out_ref, i, j, value)
        put_block(out_ref, j, i, value.T)
    unpack_own(b_piece, order, out_ref, second, scale, shift)


def put_block(out_ref, i, j, value):
    out_ref[i * LANE : (i + 1) * LANE, j * LANE : (j + 1) * LANE] = value


def unpack_own(b_piece, order, out_ref, second=0, scale=1.0, shift=0.0):
    rows, cols = places()
    damping = jnp.where(rows == cols, shift, 0.0)
    for half in range(2):
        top = own_start(order, half, second)
        above, pairs = half_blocks(order, half)
        for i, j in above:
            value = b_piece(top, LANE) * scale
            put_block(out_ref, i, j, value)
            put_block(out_ref, j, i, value.T)
            top += LANE
        last = b_piece(top + len(pairs) * LANE, -(-len(pairs) // 8) * 8)
        for k, (i, j) in enumerate(pairs):
            both = b_piece(top, LANE)
            turned = both.T
            put_block(out_ref, i, i, jnp.where(rows <= cols, both, turned) * scale + damping)
            after = jnp.where(rows > cols, both, jnp.where(rows < cols, turned, last[k : k + 1, :]))
            put_block(out_ref, j, j, after * scale + damping)
            top += LANE


def stored_block(a_ref, b_ref, order, i, j, second):
    if i > j:
        return stored_block(a_ref, b_ref, order, j, i, second).T
    if (i, j) in joining_blocks(order):
        start = joining_blocks(order).index((i, j)) * LANE
        return a_ref[start : start + LANE, :]
    half = i // (order // LANE // 2)
    above, pairs = half_blocks(order, half)
    top = own_start(order, half, second)
    if i < j:
        return b_ref[pl.ds(top + above.index((i, j)) * LANE, LANE), :]
    place = next(k for k, pair in enumerate(pairs) if i in pair)
    both = b_ref[pl.ds(top + (len(above) + place) * LANE, LANE), :]
    rows, cols = places()
    if i == pairs[place][0]:
        return jnp.where(rows <= cols, both, both.T)
    last = b_ref[pl.ds(top + (len(above) + len(pairs)) * LANE, -(-len(pairs) // 8) * 8), :]
    return jnp.where(rows > cols, both, jnp.where(rows < cols, both.T, last[place : place + 1, :]))


def halves(value):
    high = value.astype(jnp.bfloat16)
    return high, (value - high.astype(jnp.float32)).astype(jnp.bfloat16)


def times(left, right, turned=False):
    dims = (((1,), (1 if turned else 0,)), ((), ()))
    dot = functools.partial(lax.dot_general, dimension_numbers=dims, preferred_element_type=jnp.float32)
    rows = left[0].shape[0]
    both = dot(jnp.concatenate(left, 0), right[0])
    return both[:rows] + (dot(left[0], right[1]) + both[rows:])


def rows_of(pair, start, stop):
    return pair[0][start:stop, :], pair[1][start:stop, :]


def upper_times(left, right):
    middle = left[0].shape[0] // 2
    top = times(rows_of(left, 0, middle), right)
    corner = times(rows_of(left, middle, 2 * middle), (right[0][:, middle:], right[1][:, middle:]))
    return top, corner


def upper_square(value):
    dot = functools.partial(jnp.dot, preferred_element_type=jnp.float32)
    high, low = value
    middle = high.shape[0] // 2
    mixed = dot(high, low)
    top = dot(high[:middle], high) + (mixed[:middle] + mixed[:, :middle].T)
    corner = mixed[middle:, middle:]
    return top, dot(high[middle:], high[:, middle:]) + (corner + corner.T)


def whole(top, corner):
    middle = corner.shape[0]
    return jnp.concatenate([top, jnp.concatenate([top[:, middle:].T, corner], 1)], 0)


def cov_kernel(x_ref, out_ref):
    x = x_ref[...]
    order = x.shape[1]
    split = part_rows(order)[0]
    total = lax.dot_general(x, x, (((0,), (0,)), ((), ())), preferred_element_type=jnp.float32)
    pack(block_of(total), order, out_ref.at[:split], out_ref.at[split:])


def block_of(value):
    return lambda i, j: value[i * LANE : (i + 1) * LANE, j * LANE : (j + 1) * LANE]


def put_rows(out_ref, start, rows_ref):
    rows, columns = rows_ref.shape
    for column in range(columns // LANE):
        out_ref[start : start + rows, :] = rows_ref[:, column * LANE : (column + 1) * LANE]
        start += rows


def chip_kernel(kept_ref, other_ref, rows_ref, chip_ref, outer_ref):
    chip_ref[...] = kept_ref[...] + other_ref[...]

    @pl.when(is_middle())
    def _():
        used = rows_ref.shape[0] * rows_ref.shape[1] // LANE
        put_rows(outer_ref, 0, rows_ref)
        outer_ref[used:, :] = jnp.zeros((outer_ref.shape[0] - used, LANE), jnp.float32)

    @pl.when(jnp.logical_not(is_middle()))
    def _():
        outer_ref[...] = chip_ref[...]


def inverse_kernel(scale, order, *refs):
    *sums, own_rows_ref, other_rows_ref, a_ref, b_ref, direct_ref, gathered_ref, factor_ref, rows_ref = refs
    split = part_rows(order)[0]

    def piece(start, size):
        total = sums[0][start : start + size, :]
        for ref in sums[1:]:
            total = total + ref[start : start + size, :]
        return total

    unpack(piece, lambda start, size: piece(split + start, size), order, factor_ref, 0, scale, DAMPING)
    factor = factor_ref[...]
    bound = jnp.max(jnp.sum(jnp.abs(factor), axis=0, keepdims=True), axis=1, keepdims=True) + 1e-06
    start = START / bound
    rows = lax.broadcasted_iota(jnp.int32, (order, order), 0)
    cols = lax.broadcasted_iota(jnp.int32, (order, order), 1)
    eye = jnp.where(rows == cols, 1.0, 0.0)
    total = eye - start * factor
    middle = order // 2
    square = whole(*upper_square(halves(total)))
    power = whole(*upper_square(halves(square)))
    total = total + 0.5 * (square + whole(*upper_square(halves(total + square))) - power)
    for step in range(2, ITERS):
        power_halves = halves(power)
        top, corner = upper_times(halves(total), power_halves)
        known = total + power
        top, corner = top + known[:middle], corner + known[middle:, middle:]
        if step < ITERS - 1:
            total = whole(top, corner)
            power = whole(*upper_square(power_halves))

    def block(i, j):
        if i < middle // LANE:
            value = block_of(top)(i, j)
        else:
            value = block_of(corner)(i - middle // LANE, j - middle // LANE)
        return start * (value + block_of(eye)(i, j))

    @pl.when(is_middle())
    def _():
        pack(block, order, a_ref, b_ref, lax.rem(lax.axis_index("cuts"), 2))
        direct_ref[:split, :] = a_ref[...]
        direct_ref[split:, :] = b_ref[...]

    @pl.when(jnp.logical_not(is_middle()))
    def _():
        core = lax.axis_index("grad")
        size = own_rows_ref.shape[0] * own_rows_ref.shape[1] // LANE
        rows_ref[2 * size :, :] = jnp.zeros((rows_ref.shape[0] - 2 * size, LANE), jnp.float32)
        for mine in range(2):

            @pl.when(core == mine)
            def _():
                put_rows(rows_ref, mine * size, own_rows_ref)
                put_rows(rows_ref, (1 - mine) * size, other_rows_ref)

            @pl.when(rows_core() == mine)
            def _():
                outer, far = sums[0][:size, :], sums[2][:size, :]
                gathered_ref[:size, :] = outer if mine else far
                gathered_ref[size:, :] = far if mine else outer

        a_ref[...] = rows_ref[:split, :]
        b_ref[...] = rows_ref[split:, :]
        direct_ref[...] = rows_ref[...]


def choose_kernel(which, start, *refs):
    *arrays, out_ref = refs
    index = which()
    rows = out_ref.shape[0]
    for place, ref in enumerate(arrays):
        first = start if place == len(arrays) - 1 else 0

        @pl.when(index == place)
        def _():
            out_ref[...] = ref[first : first + rows, :]


def fill_left(order, mine, a_ref, b_ref, left_ref):
    second = lax.rem(lax.div(lax.axis_index("dp"), 2), 2)
    for row in range(order // LANE):

        @pl.when(mine == row)
        def _():
            for column in range(order // LANE):
                block = stored_block(a_ref, b_ref, order, row, column, second)
                left_ref[:, column * LANE : (column + 1) * LANE] = block


def fill_right(order, a_ref, b_ref, right_ref):
    unpack(
        lambda start, size: a_ref[pl.ds(start, size), :],
        lambda start, size: b_ref[pl.ds(start, size), :],
        order,
        right_ref,
        lax.rem(lax.axis_index("cuts"), 2),
    )


def place_of_rows(spread):
    core = lax.axis_index("grad")
    return core, lax.rem(lax.axis_index("dp") * lax.axis_size("grad") + core, spread)


def first_kernel(order, spread, own_a, own_b, other_b, *refs):
    own_rows_ref, other_rows_ref, outer_ref, outer_other_ref, direct_ref, relayed_a, relayed_b, relayed_other, *refs = refs
    left_out, high_out, low_out, left_ref, right_ref, tile_ref = refs
    core, mine = place_of_rows(spread)
    rows_dev = own_rows_ref.shape[0]

    def place(position):
        return pl.ds(pl.multiple_of(position * rows_dev, rows_dev), rows_dev)

    tile_ref[place(mine), :] = own_rows_ref[...]
    tile_ref[place(mine ^ 1), :] = other_rows_ref[...]
    here = core == rows_core()
    cases = (
        (False, True, (outer_ref,)),
        (False, False, (outer_other_ref,)),
        (True, True, (direct_ref.at[: relayed_a.shape[0]], relayed_other)),
        (True, False, (relayed_a, relayed_b)),
    )
    for middle, arrived, parts in cases:

        @pl.when(jnp.logical_and(is_middle() == middle, here == arrived))
        def _():
            start, part = 0, 0
            for turn in range(2):
                for column in range(order // LANE):
                    if start == parts[part].shape[0]:
                        start, part = 0, part + 1
                    tile_ref[place((mine // 2 ^ 1) * 2 + turn), column * LANE : (column + 1) * LANE] = parts[part][
                        start : start + rows_dev, :
                    ]
                    start += rows_dev

    @pl.when(core != 0)
    def _():
        fill_left(order, mine, own_a, own_b, left_ref)
        left_out[...] = times(halves(left_ref[...]), halves(tile_ref[...]))
        second = lax.rem(lax.axis_index("cuts"), 2)
        unpack_own(lambda start, size: other_b[pl.ds(start, size), :], order, right_ref, second)
        for own in (slice(0, order // 2), slice(order // 2, order)):
            high_out[own, own], low_out[own, own] = halves(right_ref[own, own])

    @pl.when(core == 0)
    def _():
        fill_right(order, own_a, own_b, right_ref)
        high_out[...], low_out[...] = halves(times(halves(tile_ref[...]), halves(right_ref[...])))


def last_kernel(order, spread, other_a, other_b, first_left, high_ref, low_ref, out_ref, left_ref, result_ref, sems):
    core, mine = place_of_rows(spread)
    step = order // 2
    parts = (slice(0, step), slice(step, order))

    def finish(columns):
        copies = []
        for turn in range(2):
            result_ref[turn] = columns(turn)
            target = out_ref.at[:, pl.ds(turn * step, step)]
            copies.append(pltpu.make_async_copy(result_ref.at[turn], target, sems.at[turn]))
            copies[-1].start()
        for copy in copies:
            copy.wait()

    @pl.when(core != 0)
    def _():
        count = step // LANE
        blocks = [other_a[slot * LANE : (slot + 1) * LANE, :] for slot in range(count * count)]
        rows = [jnp.concatenate(blocks[row * count : (row + 1) * count], 1) for row in range(count)]
        joining = halves(jnp.concatenate(rows, 0))
        left = halves(first_left[...])
        left = [(left[0][:, part], left[1][:, part]) for part in parts]

        def columns(turn):
            own = high_ref[parts[turn], parts[turn]], low_ref[parts[turn], parts[turn]]
            return times(left[turn], own) + times(left[1 - turn], joining, turn == 0)

        finish(columns)

    @pl.when(core == 0)
    def _():
        fill_left(order, mine, other_a, other_b, left_ref)
        left = halves(left_ref[...])
        finish(lambda turn: times(left, (high_ref[:, parts[turn]], low_ref[:, parts[turn]])))


def call(kernel, shapes, scratch, *args, space=pltpu.VMEM):
    return pl.pallas_call(
        kernel,
        out_shape=[jax.ShapeDtypeStruct(shape[:2], *shape[2:] or (jnp.float32,)) for shape in shapes],
        out_specs=[pl.BlockSpec(memory_space=space) for shape in shapes],
        scratch_shapes=scratch,
        compiler_params=PARAMS,
    )(*args)


class Plan:
    def __init__(self, groups, dp, cuts):
        self.groups, self.dp, self.cuts = groups, dp, cuts
        self.bases = range(0, dp, QUAD)

    def index(self, z, x, core):
        return (z * self.cuts + x % self.cuts) * 2 + core

    def roots(self, base, x):
        return base + 1 + x % 2, base + 2 - x % 2

    def one_way(self, pairs):
        pairs = list(pairs)
        size = self.dp * self.cuts * 2
        return [(group * size + a, group * size + b) for group in range(self.groups) for a, b in pairs]

    def whole(self, edges, abreast=False):
        size = self.dp * self.cuts * 2
        target = dict(self.one_way(edges))

        def pair_up(other):
            for device in range(size * self.groups):
                chosen = other(device)
                if device not in target and chosen not in target and chosen < size * self.groups:
                    target[device], target[chosen] = chosen, device

        pair_up(lambda device: device ^ 1)
        if abreast and self.cuts % 2 == 0:
            pair_up(lambda device: device ^ 3)
        pair_up(lambda device: (device + size) % (2 * size) + device // (2 * size) * 2 * size)
        return sorted(target.items())

    def swaps(self, pairs):
        return self.whole([edge for a, b in pairs for edge in ((a, b), (b, a))])

    def chains(self, pairs):
        to, of = dict(pairs), {b: a for a, b in pairs}
        edges = list(pairs)
        for device in sorted(set(to) | set(of)):
            if device in of and device not in to:
                if device ^ 1 in of or device ^ 1 not in to:
                    return self.swaps(pairs)
                edges.append((device, device ^ 1))
            elif device in to and device not in of and (device ^ 1 in to or device ^ 1 not in of):
                return self.swaps(pairs)
        return self.whole(edges)

    def loops(self, pairs):
        edges = []
        for a, b in pairs:
            if (a ^ 1, b ^ 1) in pairs:
                edges += [(a, b), (b, a)]
            else:
                edges += [(a, b), (b, b ^ 1), (b ^ 1, a ^ 1), (a ^ 1, a)]
        return self.whole(edges)

    def across(self, bit):
        return self.one_way(
            (self.index(z, x, core), self.index(z ^ bit, x, core))
            for z in range(self.dp)
            for x in range(self.cuts)
            for core in range(2)
        )

    def collect(self):
        far, near, outer = [], [], []
        for x in range(self.cuts):
            for base in self.bases:
                left, right = self.roots(base, x)
                left_root, right_root = self.index(left, x, 1), self.index(right, x, 0)
                right_far, left_far = self.index(left ^ 1, x, 1), self.index(right ^ 1, x, 0)
                far += [(left_far, left_root), (left_root, right_far), (right_far, right_root), (right_root, left_far)]
                near.append((self.index(right, x, 0), left_root))
                outer.append((self.index(left ^ 1, x, 0), left_root))
                outer.append((self.index(right ^ 1, x, 1), right_root))
        return self.whole(far, True), self.swaps(near), self.loops(outer)

    def spread(self):
        hops = [[] for turn in range(1, self.cuts)]
        direct = []
        relays = [[] for turn in range(1, self.cuts)]
        for x in range(self.cuts):
            for base in self.bases:
                left, right = self.roots(base, x)
                right_root, middle = self.index(right, x, 0), self.index(left, x, 0)
                hops[0].append((right_root, middle))
                left_root = self.index(left, x, 1)
                direct.append((right_root, self.index(right ^ 1, x, 0)))
                direct.append((left_root, self.index(left ^ 1, x, 1)))
                relays[0].append((middle, self.index(left ^ 1, x, 0)))
                if x // 2 != base // QUAD:
                    continue
                for turn in range(1, self.cuts):
                    abreast = self.index(left, x + turn, 1)
                    hops[turn - 1].append((left_root, abreast))
                    relays[turn - 1].append((abreast, self.index(left ^ 1, x + turn, 1)))
        return [self.chains(pairs) for pairs in hops], self.loops(direct), [self.loops(pairs) for pairs in relays]

    def turn(self):
        z, x, core = (lax.axis_index(name) for name in AXES[1:])
        turn = lax.rem(x + self.cuts - lax.div(z, 2), self.cuts)
        return jnp.where(lax.rem(z, QUAD) == 1 + lax.rem(x, 2), 0, jnp.maximum(turn - 1, 0))

    def which(self):
        z, x, core = (lax.axis_index(name) for name in AXES[1:])
        zq, middle = lax.rem(z, QUAD), is_middle()
        block = lax.div(z, 2)
        turn = lax.rem(x + self.cuts - block, self.cuts)
        direct = 2 * self.cuts - 1
        left = jnp.where(middle, turn, jnp.where(turn == 0, direct, self.cuts - 1 + turn))
        right_root = 2 - lax.rem(x, 2)
        right = jnp.where(
            zq == right_root, 0, jnp.where(middle, 1, jnp.where((zq ^ 1) == right_root, direct, self.cuts))
        )
        return jnp.where(core == 1, left, right)


def is_middle():
    zq = lax.rem(lax.axis_index("dp"), QUAD)
    return jnp.logical_or(zq == 1, zq == 2)


def rows_core():
    zq = lax.rem(lax.axis_index("dp"), QUAD)
    left = 1 + lax.rem(lax.axis_index("cuts"), 2)
    return jnp.where(is_middle(), zq != left, (zq ^ 1) == left).astype(jnp.int32)


def swap_cores(array):
    return lax.ppermute(array, "grad", [(0, 1), (1, 0)])


def per_device(acts, outgrads, grads):
    groups, dp, cuts, cores = (lax.axis_size(name) for name in AXES)
    tok_rows, order = acts.shape[1:]
    dev_count = dp * cores
    spread = dev_count // cuts
    plan = Plan(groups, dp, cuts)
    split, rest = part_rows(order)
    shape = (split + rest, LANE)
    acts, outgrads, grads = acts[0], outgrads[0], grads[0]

    core = lax.axis_index("grad")
    (sent,) = call(cov_kernel, [shape], [], jnp.where(core == 0, outgrads, acts))
    (kept,) = call(cov_kernel, [shape], [], jnp.where(core == 0, acts, outgrads))
    other_rows = swap_cores(grads)
    chip, outer = call(chip_kernel, [shape] * 2, [], kept, swap_cores(sent), grads)
    bit = QUAD
    while bit < dp:
        chip = chip + lax.ppermute(chip, AXES, plan.across(bit))
        outer = jnp.where(is_middle(), outer, chip)
        bit *= 2
    far, near, outward = plan.collect()
    sums = [
        lax.ppermute(outer, AXES, outward),
        lax.ppermute(chip, AXES, near),
        lax.ppermute(outer, AXES, far),
        swap_cores(chip),
    ]
    scale = 1.0 / (tok_rows * dev_count)
    square_scratch = pltpu.VMEM((order, order), jnp.float32)
    gathered = (2 * grads.size // LANE, LANE)
    *inverse, direct, outer_rows = call(
        functools.partial(inverse_kernel, scale, order),
        [(split, LANE), (rest, LANE), shape, gathered],
        [square_scratch, pltpu.VMEM(shape, jnp.float32)],
        *sums,
        grads,
        other_rows,
    )

    hops, outward, relays = plan.spread()
    hopped = [[lax.ppermute(inverse[0], AXES, pairs) for pairs in hops]]
    direct = lax.ppermute(direct, AXES, outward)
    hopped.append([lax.ppermute(inverse[1], AXES, pairs) for pairs in hops])
    relayed = [[lax.ppermute(array, AXES, pairs) for array, pairs in zip(arrays, relays)] for arrays in hopped]
    relayed[1], direct = lax.optimization_barrier((relayed[1], direct))
    arrived = [
        arrays[0] if cuts == 2 else call(functools.partial(choose_kernel, plan.turn, 0), [arrays[0].shape], [], *arrays)[0]
        for arrays in relayed
    ]
    own = []
    for part, start in ((0, 0), (1, split)):
        own += call(
            functools.partial(choose_kernel, plan.which, start),
            [inverse[part].shape],
            [],
            inverse[part],
            *hopped[part],
            *relayed[part],
            direct,
        )
    other_a, other_b = map(swap_cores, own)
    left_scratch = pltpu.VMEM((LANE, order), jnp.float32)
    first = call(
        functools.partial(first_kernel, order, spread),
        [(LANE, order), (order, order, jnp.bfloat16), (order, order, jnp.bfloat16)],
        [left_scratch, square_scratch, square_scratch],
        *own,
        other_b,
        grads,
        other_rows,
        outer_rows,
        swap_cores(outer_rows),
        direct,
        *arrived,
        swap_cores(arrived[1]),
    )
    (out,) = call(
        functools.partial(last_kernel, order, spread),
        [grads.shape],
        [
            left_scratch,
            pltpu.VMEM((2, LANE, order // 2), jnp.float32),
            pltpu.SemaphoreType.DMA((2,)),
        ],
        other_a,
        other_b,
        *first,
        space=pl.ANY,
    )
    return out[None]


def solution(mesh):
    in_specs = (
        P(None, ("groups", "dp", "grad"), "cuts"),
        P(None, ("groups", "dp", "grad"), "cuts"),
        P("groups", ("dp", "grad"), "cuts"),
    )
    out_specs = P("groups", ("dp", "grad"), "cuts")
    return jax.shard_map(
        per_device, mesh=mesh, in_specs=in_specs, out_specs=out_specs, check_vma=False
    )
```
